32 devices in a mesh: group: 2 (over core), expert: 16 (over z, y, x).
Axes of the slice: x: 2, y: 2, z: 4, core: 2. Of those that a mesh axis runs over, the one named last changes fastest.
Arguments:
- tokens: bfloat16 [32768, 768], P(('group', 'expert')), may hold values from -6 to 6
- gains: bfloat16 [2, 768], replicated, may hold values from 0.5 to 1.5
- qkv_weight: bfloat16 [768, 2304], replicated, may hold values from -0.21875 to 0.21875
- out_weight: bfloat16 [768, 768], replicated, may hold values from -6 to 6
- rel_bias: bfloat16 [32, 12], replicated, may hold values from -4 to 4
- router_weight: bfloat16 [768, 16], replicated, may hold values from -0.25 to 0.25
- w_in: bfloat16 [16, 768, 3072], P('expert'), may hold values from -0.21875 to 0.21875
- w_out: bfloat16 [16, 3072, 768], P('expert'), may hold values from -6 to 6
- routes: int32 [32768, 1], P(('group', 'expert')), may hold values from 0 to 15
- factors: int32 [32], P(('group', 'expert')), may hold values from 1 to 2, as said below
- cotangent: bfloat16 [32768, 768], P(('group', 'expert')), may hold values from -6 to 6
Outputs:
- output: bfloat16 [32768, 768], P(('group', 'expert'))
- grad_tokens: float32 [32768, 768], P(('group', 'expert'))
- grad_gains: float32 [2, 768], P('group', 'expert')
- grad_qkv: float32 [768, 2304], P('expert', 'group')
- grad_out_weight: float32 [768, 768], P('expert', 'group')
- grad_rel_bias: float32 [32, 12], replicated
- grad_router: float32 [768, 16], P('expert', 'group')
- grad_w_in: float32 [16, 768, 3072], P('expert', None, 'group')
- grad_w_out: float32 [16, 3072, 768], P('expert', 'group')
The draws below stay inside these ranges and needn't reach their ends.
Inputs may be any that keep to these rules, and one draw needn't show every extreme that they name: `factors`: each sequence's capacity factor; within each run of 16 sequences, half have factor 1 and half factor 2.
All inputs are finite; a program needn't handle non-finite values.
Results may differ from the reference program's by a relative error of at most 0.019.
Values may be sent and summed in bfloat16 or wider, within the bound.
A program may use at most 320 MiB of HBM per device.

```python
import jax
import jax.numpy as jnp
from jax import lax

D = 768
HEADS = 12
HDIM = 64
FF = 3072
BUCKETS = 32
LEN = 1024
EXPERTS = 16
GROUPS = 2
SEQS_GROUP = 16
TOKENS = 32768
SLOTS = 128
N_GROUP = 2
N_EXPERT = 16


def draw_factors(key, part):
    key = jax.random.fold_in(key, 7)
    pieces = []
    for number in range(GROUPS):
        shuffled = jax.random.permutation(jax.random.fold_in(key, number), SEQS_GROUP)
        pieces.append(shuffled % 2 + 1)
    return jnp.concatenate(pieces, axis=0).astype(jnp.int32)


def raised(values, own_key, source, target, parts, factor):
    def block_of(position):
        return (jnp.arange(values.shape[position]) // (values.shape[position] // parts)).reshape((-1,) + (1,) * (values.ndim - 1 - position))

    first = jax.random.permutation(own_key, parts)[block_of(target)]
    second = (block_of(target) + parts // 2) % parts
    return jnp.where((block_of(source) == first) | (block_of(source) == second), factor * values, values)


def block_scale(own_key, dims, shards, low, high):
    def one(axis_at, blocks):
        draws = jax.random.uniform(jax.random.fold_in(jax.random.fold_in(own_key, 6), axis_at), (blocks,), jnp.float32, low / len(shards), high / len(shards))
        return jnp.repeat(jnp.exp(draws), dims[axis_at] // blocks).reshape((-1,) + (1,) * (len(dims) - axis_at - 1))

    factor_of = one(*shards[0])
    for cut in shards[1:]:
        factor_of = factor_of * one(*cut)
    return factor_of


def picks_of(key, rows, amount, top, lift):
    sequence = jax.random.permutation(jax.random.fold_in(key, 1), amount)
    boost = sequence
    for power in range(3):
        boost = boost * boost // amount
    boost = boost * lift // amount
    chance = jax.random.randint(jax.random.fold_in(key, 2), (rows, amount), 0, 4096) + boost
    holders = jax.random.permutation(jax.random.fold_in(key, 3), rows)[jnp.arange(amount) % rows]
    chance = jnp.where(jnp.arange(rows)[:, None] == holders[None, :], 1 << 14, chance)
    score = chance * amount + jnp.arange(amount)
    return lax.top_k(score.astype(jnp.int32), top)[1].astype(jnp.int32)


def normal_values(key, extent, scale, most, shards=(), held_as=jnp.bfloat16):
    values = jax.random.normal(key, extent, jnp.float32) * scale
    if len(shards) > 0:
        values = block_scale(key, extent, shards, -0.22, 0.18) * values
    return jnp.clip(values, min=-most, max=most).astype(held_as)


def bell_draw_with(rng, shape, width, bound, cuts, heavy, kind=jnp.bfloat16):
    drawn = width * jax.random.normal(rng, shape, jnp.float32)
    if cuts:
        drawn = drawn * block_scale(rng, shape, cuts, -0.22, 0.18)
    return jnp.clip(raised(drawn, jax.random.fold_in(rng, 3), *heavy), -bound, bound).astype(kind)


def setup_inputs(seed: int = 0) -> dict:
    arg_keys = jax.random.split(jax.random.key(seed), 12)
    return {
        "tokens": normal_values(arg_keys[0], (TOKENS, D), 1.0, 6.0, ((0, 32),)),
        "gains": jnp.clip(1.0 + 0.1 * jax.random.normal(arg_keys[1], (2, D), jnp.float32), 0.5, 1.5).astype(jnp.bfloat16),
        "qkv_weight": normal_values(arg_keys[2], (D, 3 * D), D ** -0.5, 0.21875),
        "out_weight": normal_values(arg_keys[3], (D, D), ((LEN / (8 * D)) ** 0.5), 6.0),
        "rel_bias": normal_values(arg_keys[4], (BUCKETS, HEADS), 1.0, 4.0),
        "router_weight": normal_values(arg_keys[5], (D, EXPERTS), (0.5 / D ** 0.5), 0.25),
        "w_in": normal_values(arg_keys[6], (EXPERTS, D, FF), D ** -0.5, 0.21875, ((0, 16),)),
        "w_out": normal_values(arg_keys[7], (EXPERTS, FF, D), (2 * EXPERTS / FF ** 0.5), 6.0, ((0, 16),)),
        "routes": picks_of(arg_keys[8], TOKENS, EXPERTS, 1, 512),
        "factors": draw_factors(jax.random.fold_in(arg_keys[11], 71), 0),
        "cotangent": bell_draw_with(arg_keys[10], (TOKENS, D), 1.0, 6.0, ((0, 32),), (0, 1, 32, 2.75)),
    }


EPSILON = 1e-06
BOUNDARIES = (12, 16, 23, 32, 46, 64, 91)
PRECISE = lax.Precision.HIGHEST

@jax.custom_vjp
def low(v):
    return lax.optimization_barrier(v.astype(jnp.bfloat16)).astype(jnp.float32)

@jax.custom_vjp
def low_back(v):
    return v

def low_keep(v):
    return (low(v), None)

def low_pass(kept, grad):
    return (grad,)

def back_keep(v):
    return (v, None)

def back_low(kept, grad):
    return (low(grad),)
low.defvjp(low_keep, low_pass)
low_back.defvjp(back_keep, back_low)

def bucket_index(relative):
    distance = jnp.abs(relative)
    farther = jnp.full(relative.shape, 8, jnp.int32)
    for boundary in BOUNDARIES:
        farther = farther + (distance >= boundary).astype(jnp.int32)
    nearest = jnp.where(distance < 8, distance, farther)
    return nearest + 16 * (relative > 0).astype(jnp.int32)

def norm_rows(values, gain_row):
    return values * lax.rsqrt(lax.optimization_barrier(jnp.mean(values * values, axis=-1, keepdims=True)) + EPSILON) * gain_row

def attend(queries, keys_all, values_all, bias):
    scores = jnp.einsum('qhd,khd->hqk', queries, keys_all, precision=PRECISE) * HDIM ** (-0.5) + bias
    scores = low_back(scores)
    row_max = lax.optimization_barrier(jnp.max(scores, axis=-1, keepdims=True))
    shifted_exp = jnp.exp(scores - row_max)
    weights = low(shifted_exp / lax.optimization_barrier(jnp.sum(shifted_exp, axis=-1, keepdims=True)))
    return low(low_back(jnp.einsum('hqk,khd->qhd', weights, values_all, precision=PRECISE)))

def reference(tokens, gains, qkv_weight, out_weight, rel_bias, router_weight, w_in, w_out, routes, factors, cotangent):
    devices = N_GROUP * N_EXPERT
    seq_index = jnp.arange(devices, dtype=jnp.int32)[:, None]
    routed = routes[:, 0].reshape(devices, LEN)
    chosen_int = (routed[:, :, None] == jnp.arange(EXPERTS, dtype=jnp.int32)[None, None, :]).astype(jnp.int32)
    before = jnp.cumsum(chosen_int, axis=1, dtype=jnp.int32) - chosen_int
    place = lax.optimization_barrier(jnp.sum(before * chosen_int, axis=-1, dtype=jnp.int32))
    capacity = factors.astype(jnp.int32) * (LEN // EXPERTS)
    kept_mask = place < capacity[:, None]
    target = jnp.where(kept_mask, routed * SLOTS + place, EXPERTS * SLOTS).astype(jnp.int32)
    row_index = jnp.arange(LEN, dtype=jnp.int32)

    def fill_slots(targets):
        return jnp.full((EXPERTS * SLOTS,), LEN, jnp.int32).at[targets].set(row_index, mode='drop')
    local_token = jax.vmap(fill_slots)(target)
    slot_token = jnp.where(local_token < LEN, seq_index * LEN + local_token, TOKENS).reshape(-1).astype(jnp.int32)
    lookup = (seq_index * (EXPERTS * SLOTS) + jnp.minimum(target, EXPERTS * SLOTS - 1)).reshape(-1).astype(jnp.int32)
    kept_float = kept_mask.reshape(-1).astype(jnp.float32)
    chosen_float = chosen_int.reshape(TOKENS, EXPERTS).astype(jnp.float32)
    buckets = bucket_index(row_index[None, :] - row_index[:, None])

    def forward(inputs, gain_rows, qkv_w, out_w, table, router_w, first_w, second_w):
        normed_in = low(norm_rows(inputs, gain_rows[0]))
        projected = low(low_back(jnp.dot(normed_in, qkv_w, precision=PRECISE)))
        shaped = projected.reshape(devices, LEN, 3, HEADS, HDIM)
        bias = jnp.transpose(table[buckets], (2, 0, 1))

        def one_sequence(member):
            return attend(member[0], member[1], member[2], bias)
        attended = lax.map(jax.checkpoint(one_sequence), (shaped[:, :, 0], shaped[:, :, 1], shaped[:, :, 2]))
        attended = attended.reshape(TOKENS, D)
        residual_one = inputs + low_back(jnp.dot(attended, out_w, precision=PRECISE))
        hidden = low(norm_rows(residual_one, gain_rows[1]))
        logits = low_back(jnp.dot(hidden, router_w, precision=PRECISE))
        router_exp = jnp.exp(logits - lax.optimization_barrier(jnp.max(logits, axis=-1, keepdims=True)))
        router = router_exp / lax.optimization_barrier(jnp.sum(router_exp, axis=-1, keepdims=True))
        gate_value = lax.optimization_barrier(jnp.sum(router * chosen_float, axis=-1))
        toward = low_back(hidden)
        padded = jnp.concatenate([toward, jnp.zeros((1, D), jnp.float32)], axis=0)
        dispatched = padded[slot_token].reshape(devices, EXPERTS, SLOTS, D)
        dispatched = jnp.moveaxis(dispatched, 1, 0)

        def one_expert(member):
            row_block, first_block, second_block = member
            preact = low_back(jnp.einsum('bcd,df->bcf', row_block, first_block, precision=PRECISE))
            activated = low(jax.nn.gelu(preact))
            return low(low_back(jnp.einsum('bcf,fd->bcd', activated, second_block, precision=PRECISE)))
        produced = lax.map(jax.checkpoint(one_expert), (dispatched, first_w, second_w))
        produced = jnp.moveaxis(produced, 0, 1).reshape(-1, D)
        brought = produced[lookup] * kept_float[:, None]
        return residual_one + gate_value[:, None] * brought
    primals = (tokens.astype(jnp.float32), gains.astype(jnp.float32), qkv_weight.astype(jnp.float32), out_weight.astype(jnp.float32), rel_bias.astype(jnp.float32), router_weight.astype(jnp.float32), w_in.astype(jnp.float32), w_out.astype(jnp.float32))
    result, pullback = jax.vjp(forward, *primals)
    grads = pullback(cotangent.astype(jnp.float32))
    return (result.astype(jnp.bfloat16), grads[0], grads[1], grads[2], grads[3], grads[4], grads[5], grads[6], grads[7])
```

```python
import functools

import jax
import jax.numpy as jnp
from jax import lax
from jax.experimental import pallas as pl
from jax.experimental.pallas import tpu as pltpu
from jax.sharding import PartitionSpec as P

EPSILON = 1e-06
BOUNDARIES = (12, 16, 23, 32, 46, 64, 91)
F32 = jnp.float32
BF16 = jnp.bfloat16
LANES = 128
HEAD = 64
NT = (((1,), (1,)), ((), ()))
TN = (((0,), (0,)), ((), ()))
MIB = 2**20


def bucket_index(relative):
    distance = jnp.abs(relative)
    farther = jnp.full(relative.shape, 8, jnp.int32)
    for boundary in BOUNDARIES:
        farther = farther + (distance >= boundary).astype(jnp.int32)
    nearest = jnp.where(distance < 8, distance, farther)
    return nearest + 16 * (relative > 0).astype(jnp.int32)


def norm_rows(values, gain_row):
    return (
        values * lax.rsqrt(jnp.mean(values * values, axis=-1, keepdims=True) + EPSILON) * gain_row
    )


def attend_kernel(q_ref, k_ref, v_ref, line_ref, out_ref, kept_ref, slab_ref, *, rows):
    length = q_ref.shape[0]
    lane = lax.broadcasted_iota(jnp.int32, (1, LANES), 1)
    keys, values = k_ref[...], v_ref[...]
    for head in range(2):
        line = jnp.broadcast_to(line_ref[head], (rows, 2 * length))
        slab_ref[head] = pltpu.roll(line, 0, 1, stride=1, stride_axis=0)
    for step in range(length // rows):
        block = pl.ds(step * rows, rows)
        queries = q_ref[block, :].astype(F32) * HEAD**-0.5
        joined = []
        for head in range(2):
            mine = (lane < HEAD) if head == 0 else (lane >= HEAD)
            own = jnp.where(mine, queries, 0.0).astype(BF16)
            scores = lax.dot_general(own, keys, NT, preferred_element_type=F32)
            scores = scores + slab_ref[head, :, pl.ds(length - rows * step, length)]
            top = jnp.max(scores, axis=1, keepdims=True)
            raised = jnp.exp(scores - top)
            total = jnp.sum(raised, axis=1, keepdims=True)
            weights = (raised * (1.0 / total)).astype(BF16)
            kept_ref[head, block, :] = weights
            joined.append(jnp.dot(weights, values, preferred_element_type=F32))
        out_ref[block, :] = jnp.where(lane < HEAD, joined[0], joined[1]).astype(BF16)


def attend(projected, lines, rows):
    length, features = projected.shape[0], projected.shape[1] // 3
    heads = lines.shape[0]
    pairs = heads // 2
    return pl.pallas_call(
        functools.partial(attend_kernel, rows=rows),
        grid=(pairs,),
        in_specs=[
            pl.BlockSpec((length, LANES), lambda i: (0, i)),
            pl.BlockSpec((length, LANES), lambda i: (0, pairs + i)),
            pl.BlockSpec((length, LANES), lambda i: (0, 2 * pairs + i)),
            pl.BlockSpec((2, 1, 2 * length), lambda i: (i, 0, 0)),
        ],
        out_specs=[
            pl.BlockSpec((length, LANES), lambda i: (0, i)),
            pl.BlockSpec((2, length, length), lambda i: (i, 0, 0)),
        ],
        out_shape=[
            jax.ShapeDtypeStruct((length, features), BF16),
            jax.ShapeDtypeStruct((heads, length, length), BF16),
        ],
        scratch_shapes=[pltpu.VMEM((2, rows, 2 * length), F32)],
        compiler_params=pltpu.CompilerParams(vmem_limit_bytes=50 * MIB),
        cost_estimate=pl.CostEstimate(
            flops=16 * heads * length * length * HEAD,
            bytes_accessed=2 * heads * length * length + 8 * length * features,
            transcendentals=heads * length * length,
        ),
    )(projected, projected, projected, lines)


def attend_back_kernel(
    q_ref, k_ref, v_ref, out_ref, dout_ref, kept_ref, tile_ref,
    grad_ref, band_ref, far_ref, dscores_ref, *, rows,
):
    length = q_ref.shape[0]
    tiles = length // LANES
    inner = rows // LANES
    lane = lax.broadcasted_iota(jnp.int32, (1, LANES), 1)
    queries, values, dout = q_ref[...], v_ref[...], dout_ref[...]
    widened = jnp.concatenate([k_ref[...], tile_ref[...]], axis=1)
    dout_wide = dout.astype(F32)
    product = dout_wide * out_ref[...].astype(F32)
    dout_turned, queries_turned = dout.T, queries.T
    dqueries = [[], []]
    dkeys, dvalues = [], []
    for head in range(2):
        mine = (lane < HEAD) if head == 0 else (lane >= HEAD)
        inner_sum = jnp.sum(jnp.where(mine, product, 0.0), axis=1, keepdims=True)
        own = jnp.where(mine, dout_wide, 0.0).astype(BF16)
        band_ref[head] = jnp.zeros_like(band_ref[head])
        for step in range(length // rows):
            first = step * rows
            block = pl.ds(first, rows)
            dprob = lax.dot_general(
                own[first : first + rows], values, NT, preferred_element_type=F32
            )
            dscores = kept_ref[head, block, :].astype(F32) * (
                dprob - inner_sum[first : first + rows]
            )
            rounded = dscores.astype(BF16)
            dscores_ref[block, :] = rounded
            for part in range(inner):
                tile = step * inner + part
                low, high = max(tile - 1, 0), min(tile + 2, tiles)
                at = low - (tile - 1)
                band_ref[head, :, at * LANES : (at + high - low) * LANES] += dscores[
                    part * LANES : (part + 1) * LANES, low * LANES : high * LANES
                ]
            both = jnp.dot(rounded, widened, preferred_element_type=F32)
            dqueries[head].append(both[:, :LANES])
            for part in range(inner):
                far_ref[head, step * inner + part] = jnp.sum(
                    both[part * LANES : (part + 1) * LANES, LANES:], axis=0
                )
        half = slice(HEAD * head, HEAD * head + HEAD)
        dkeys.append(jnp.dot(queries_turned[half], dscores_ref[...], preferred_element_type=F32))
        dvalues.append(jnp.dot(dout_turned[half], kept_ref[head], preferred_element_type=F32))
    scale = HEAD**-0.5
    for step in range(length // rows):
        grad_ref[0, pl.ds(step * rows, rows), :] = (
            jnp.where(lane < HEAD, dqueries[0][step], dqueries[1][step]) * scale
        ).astype(BF16)
    grad_ref[1] = (jnp.concatenate(dkeys, axis=0) * scale).T.astype(BF16)
    grad_ref[2] = jnp.concatenate(dvalues, axis=0).T.astype(BF16)


def attend_back(projected, attended, datt, kept, rows):
    length, features = projected.shape[0], projected.shape[1] // 3
    heads = kept.shape[0]
    pairs = heads // 2
    tiles = length // LANES
    tile_of = (
        jnp.arange(length)[:, None] // LANES == jnp.arange(LANES)[None, :]
    ).astype(BF16)
    return pl.pallas_call(
        functools.partial(attend_back_kernel, rows=rows),
        grid=(pairs,),
        in_specs=[
            pl.BlockSpec((length, LANES), lambda i: (0, i)),
            pl.BlockSpec((length, LANES), lambda i: (0, pairs + i)),
            pl.BlockSpec((length, LANES), lambda i: (0, 2 * pairs + i)),
            pl.BlockSpec((length, LANES), lambda i: (0, i)),
            pl.BlockSpec((length, LANES), lambda i: (0, i)),
            pl.BlockSpec((2, length, length), lambda i: (i, 0, 0)),
            pl.BlockSpec((length, LANES), lambda i: (0, 0)),
        ],
        out_specs=[
            pl.BlockSpec((3, length, LANES), lambda i: (0, 0, i)),
            pl.BlockSpec((2, LANES, 3 * LANES), lambda i: (i, 0, 0)),
            pl.BlockSpec((2, tiles, LANES), lambda i: (i, 0, 0)),
        ],
        out_shape=[
            jax.ShapeDtypeStruct((3, length, features), BF16),
            jax.ShapeDtypeStruct((heads, LANES, 3 * LANES), F32),
            jax.ShapeDtypeStruct((heads, tiles, LANES), F32),
        ],
        scratch_shapes=[pltpu.VMEM((length, length), BF16)],
        compiler_params=pltpu.CompilerParams(vmem_limit_bytes=56 * MIB),
        cost_estimate=pl.CostEstimate(
            flops=32 * heads * length * length * HEAD,
            bytes_accessed=2 * heads * length * length + 18 * length * features,
            transcendentals=0,
        ),
    )(projected, projected, projected, attended, datt, kept, tile_of)


def bias_lines(rel_bias, length):
    relative = jnp.arange(2 * length, dtype=jnp.int32) - length
    onehot = (
        bucket_index(relative)[None, :]
        == jnp.arange(rel_bias.shape[0], dtype=jnp.int32)[:, None]
    ).astype(F32)
    return jnp.einsum(
        "ch,cr->hr", rel_bias.astype(F32), onehot, precision=lax.Precision.HIGHEST
    )[:, None, :]


def table_gradient(band, far, bucket_count):
    heads, tiles = far.shape[0], far.shape[1]
    relative = jnp.arange(3 * LANES)[None, :] - LANES - jnp.arange(LANES)[:, None]
    onehot = (bucket_index(relative)[:, :, None] == jnp.arange(bucket_count)).astype(F32)
    near = jnp.dot(
        band.reshape(heads, -1),
        onehot.reshape(-1, bucket_count),
        precision=lax.Precision.HIGHEST,
    )
    here = jnp.arange(tiles)[:, None]
    there = jnp.arange(LANES)[None, :]
    before = jnp.sum(jnp.where(there <= here - 2, far, 0.0), axis=(1, 2))
    after = jnp.sum(jnp.where(there >= here + 2, far, 0.0), axis=(1, 2))
    buckets = jnp.arange(bucket_count)
    last = bucket_index(jnp.array([-length_far(), length_far()], jnp.int32))
    return (
        near
        + before[:, None] * (buckets == last[0])
        + after[:, None] * (buckets == last[1])
    ).T


def length_far():
    return LANES


def expert_kernel(
    x_ref, c_ref, w_in_ref, w_out_ref, router_ref, mine_ref,
    made_ref, dmoved_ref, act_ref, dpre_ref, dexp_ref, drouter_ref, *, width, expert_count,
):
    x, c = x_ref[...], c_ref[...]
    router_weight = router_ref[...]
    lane = lax.broadcasted_iota(jnp.int32, (1, router_weight.shape[1]), 1)
    logits = jnp.dot(x, router_weight, preferred_element_type=F32)
    logits = jnp.where(lane < expert_count, logits, -jnp.inf)
    raised = jnp.exp(logits - jnp.max(logits, axis=-1, keepdims=True))
    router = raised / jnp.sum(raised, axis=-1, keepdims=True)
    chosen = mine_ref[...]
    gate = jnp.sum(router * chosen, axis=-1, keepdims=True)
    upstream = c.astype(F32)
    dexp = (gate * upstream).astype(BF16)
    dexp_ref[...] = dexp
    hidden_width = w_in_ref.shape[1]
    made = jnp.zeros(x.shape, F32)
    dmoved = jnp.zeros(x.shape, F32)
    root = (2.0 / jnp.pi) ** 0.5
    for first in range(0, hidden_width, width):
        part = slice(first, first + width)
        pre = jnp.dot(x, w_in_ref[:, part], preferred_element_type=F32)
        square = pre * pre
        turned = jnp.tanh(pre * (root + (root * 0.044715) * square))
        half = 0.5 + 0.5 * turned
        act = (pre * half).astype(BF16)
        slope = half + pre * (half * (1.0 - turned)) * (root + (3 * root * 0.044715) * square)
        act_ref[:, part] = act
        made = made + jnp.dot(act, w_out_ref[part, :], preferred_element_type=F32)
        dact = lax.dot_general(dexp, w_out_ref[part, :], NT, preferred_element_type=F32)
        dpre = (dact * slope).astype(BF16)
        dpre_ref[:, part] = dpre
        dmoved = dmoved + lax.dot_general(
            dpre, w_in_ref[:, part], NT, preferred_element_type=F32
        )
    made = made.astype(BF16)
    made_ref[...] = made
    dgate = jnp.sum(upstream * made.astype(F32), axis=-1, keepdims=True)
    dlogits = (dgate * gate * (chosen - router)).astype(BF16)
    dmoved_ref[...] = (
        dmoved + lax.dot_general(dlogits, router_weight, NT, preferred_element_type=F32)
    ).astype(BF16)

    @pl.when(pl.program_id(0) == 0)
    def _():
        drouter_ref[...] = jnp.zeros_like(drouter_ref)

    drouter_ref[...] += lax.dot_general(x, dlogits, TN, preferred_element_type=F32)


def run_expert(x, c, w_in, w_out, router_padded, mine, expert_count):
    total, features = x.shape
    hidden_width = w_in.shape[1]
    rows = min(256, total)
    padded = router_padded.shape[1]
    row_block = pl.BlockSpec((rows, features), lambda i: (i, 0))
    wide_block = pl.BlockSpec((rows, hidden_width), lambda i: (i, 0))

    def whole(shape):
        return pl.BlockSpec(shape, lambda i: (0, 0))

    return pl.pallas_call(
        functools.partial(
            expert_kernel, width=min(1024, hidden_width), expert_count=expert_count
        ),
        grid=(total // rows,),
        in_specs=[
            row_block,
            row_block,
            whole(w_in.shape),
            whole(w_out.shape),
            whole(router_padded.shape),
            whole(mine.shape),
        ],
        out_specs=[
            row_block,
            row_block,
            wide_block,
            wide_block,
            row_block,
            whole((features, padded)),
        ],
        out_shape=[
            jax.ShapeDtypeStruct((total, features), BF16),
            jax.ShapeDtypeStruct((total, features), BF16),
            jax.ShapeDtypeStruct((total, hidden_width), BF16),
            jax.ShapeDtypeStruct((total, hidden_width), BF16),
            jax.ShapeDtypeStruct((total, features), BF16),
            jax.ShapeDtypeStruct((features, padded), F32),
        ],
        compiler_params=pltpu.CompilerParams(vmem_limit_bytes=56 * MIB),
        cost_estimate=pl.CostEstimate(
            flops=8 * total * features * hidden_width,
            bytes_accessed=4 * features * hidden_width + 4 * total * (hidden_width + features),
            transcendentals=total * hidden_width,
        ),
    )(x, c, w_in, w_out, router_padded, mine)


def core_sum(values, dim):
    half = values.shape[dim] // 2
    core = lax.axis_index("group")
    own = lax.dynamic_slice_in_dim(values, core * half, half, dim)
    other = lax.dynamic_slice_in_dim(values, (1 - core) * half, half, dim).astype(BF16)
    return own + lax.ppermute(other, "group", [(0, 1), (1, 0)]).astype(F32)


def exchange(values):
    return lax.all_to_all(values, "expert", split_axis=0, concat_axis=0, tiled=True)


def per_device(
    tokens, gains, qkv_weight, out_weight, rel_bias, router_weight, w_in, w_out, routes, factors,
    cotangent,
):
    length, features = tokens.shape
    bucket_count = rel_bias.shape[0]
    expert_count = router_weight.shape[1]
    slot_count = 2 * length // expert_count
    chunk = slot_count // 2
    rows = min(256, length)
    gain_rows = gains.astype(F32)
    w_in, w_out = w_in[0], w_out[0]
    me = lax.axis_index("expert")
    core = lax.axis_index("group")

    routed = routes[:, 0]
    row_index = jnp.arange(length, dtype=jnp.int32)
    chosen = routed[:, None] == jnp.arange(expert_count, dtype=jnp.int32)[None, :]
    earlier = (row_index[:, None] > row_index[None, :]).astype(BF16)
    before = jnp.dot(earlier, chosen.astype(BF16), preferred_element_type=F32)
    place = jnp.sum(before * chosen.astype(F32), axis=-1).astype(jnp.int32)
    capacity = factors[0] * (length // expert_count)
    placed = jnp.where(place < capacity, place, slot_count)
    slots = jnp.arange(expert_count * chunk, dtype=jnp.int32)
    picks = []
    for number in range(2):
        inside = (placed >= number * chunk) & (placed < (number + 1) * chunk)
        target = jnp.where(inside, routed * chunk + placed - number * chunk, -1)
        picks.append((slots[:, None] == target[None, :]).astype(BF16))

    def pack(values, number):
        return jnp.dot(picks[number], values, preferred_element_type=F32).astype(BF16)

    def unpack(parts):
        return sum(
            lax.dot_general(picks[n], parts[n], TN, preferred_element_type=F32) for n in range(2)
        )

    def send(values):
        return exchange(values.reshape(expert_count, chunk, features)).reshape(-1, features)

    upstream_there = [send(pack(cotangent, n)) for n in range(2)]

    inputs = tokens.astype(F32)
    normed_in = norm_rows(inputs, gain_rows[0]).astype(BF16)
    projected = jnp.dot(normed_in, qkv_weight, preferred_element_type=F32).astype(BF16)
    attended, kept = attend(projected, bias_lines(rel_bias, length), rows)
    residual_one = inputs + jnp.dot(attended, out_weight, preferred_element_type=F32)
    hidden = norm_rows(residual_one, gain_rows[1]).astype(BF16)

    logits = jnp.dot(hidden, router_weight, preferred_element_type=F32)
    raised = jnp.exp(logits - jnp.max(logits, axis=-1, keepdims=True))
    router = raised / jnp.sum(raised, axis=-1, keepdims=True)
    gate_value = jnp.sum(router * chosen.astype(F32), axis=-1)

    hidden_there = [send(pack(hidden, n)) for n in range(2)]
    padded = -expert_count % LANES
    router_padded = jnp.pad(router_weight, ((0, 0), (0, padded)))
    mine = (jnp.arange(expert_count + padded)[None, :] == me).astype(F32)
    results = [
        run_expert(
            hidden_there[n], upstream_there[n], w_in, w_out, router_padded, mine, expert_count
        )
        for n in range(2)
    ]
    made, dmoved, act, dpre, dexp, drouter = zip(*results, strict=True)
    dmoved_back = [send(dmoved[n]) for n in range(2)]
    made, _ = lax.optimization_barrier((made, dmoved_back))
    made_back = [send(made[n]) for n in range(2)]

    def joined(left, right):
        return sum(
            lax.dot_general(left[n], right[n], TN, preferred_element_type=F32) for n in range(2)
        )

    grad_first = core_sum(joined(hidden_there, dpre), 1)[None]
    grad_second = core_sum(joined(act, dexp), 0)[None]
    grad_router = (drouter[0] + drouter[1])[:, :expert_count]

    dhidden = unpack(dmoved_back)
    upstream = cotangent.astype(F32)
    _, back_two = jax.vjp(norm_rows, residual_one, gain_rows[1])
    dres_norm, dgain_two = back_two(dhidden)
    dres = upstream + dres_norm
    dbranch = dres.astype(BF16)
    datt = lax.dot_general(dbranch, out_weight, NT, preferred_element_type=F32).astype(BF16)
    grad_out = lax.dot_general(attended, dbranch, TN, preferred_element_type=F32)
    dqkv, band, far = attend_back(projected, attended, datt, kept, rows)
    grad_proj = jnp.einsum("td,cte->dce", normed_in, dqkv, preferred_element_type=F32)
    grad_proj = grad_proj.reshape(features, 3 * features)
    dnormed = jnp.einsum(
        "cte,dce->td",
        dqkv,
        qkv_weight.reshape(features, 3, features),
        preferred_element_type=F32,
    )
    _, back_one = jax.vjp(norm_rows, inputs, gain_rows[0])
    dinput_norm, dgain_one = back_one(dnormed)
    grad_tokens = dres + dinput_norm

    brought = unpack(made_back)
    output = (residual_one + gate_value[:, None] * brought).astype(BF16)

    def scattered(values):
        return lax.psum_scatter(
            core_sum(values, 1).astype(BF16), "expert", scatter_dimension=0, tiled=True
        ).astype(F32)

    small = [
        jnp.stack([dgain_one, dgain_two], axis=0),
        grad_router,
        table_gradient(band, far, bucket_count),
    ]
    flat = lax.psum(jnp.concatenate([s.reshape(-1) for s in small]), ("group", "expert"))
    summed = []
    at = 0
    for s in small:
        summed.append(flat[at : at + s.size].reshape(s.shape))
        at += s.size
    experts = lax.axis_size("expert")
    cores = lax.axis_size("group")
    grad_gains = lax.dynamic_slice(
        summed[0], (core, me * (features // experts)), (2 // cores, features // experts)
    )
    grad_router = lax.dynamic_slice(
        summed[1],
        (me * (features // experts), core * (expert_count // cores)),
        (features // experts, expert_count // cores),
    )
    return (
        output,
        grad_tokens,
        grad_gains,
        scattered(grad_proj),
        scattered(grad_out),
        summed[2],
        grad_router,
        grad_first,
        grad_second,
    )


def solution(mesh):
    return jax.shard_map(
        per_device,
        mesh=mesh,
        in_specs=(
            P(("group", "expert"), None),
            P(),
            P(),
            P(),
            P(),
            P(),
            P("expert", None, None),
            P("expert", None, None),
            P(("group", "expert"), None),
            P(("group", "expert")),
            P(("group", "expert"), None),
        ),
        out_specs=(
            P(("group", "expert"), None),
            P(("group", "expert"), None),
            P("group", "expert"),
            P("expert", "group"),
            P("expert", "group"),
            P(),
            P("expert", "group"),
            P("expert", None, "group"),
            P("expert", "group", None),
        ),
        check_vma=False,
    )
```

```python
import functools

import jax
import jax.numpy as jnp
from jax import lax
from jax.experimental import pallas as pl
from jax.experimental.pallas import tpu as pltpu
from jax.sharding import PartitionSpec as P

EPSILON = 1e-06
BOUNDARIES = (12, 16, 23, 32, 46, 64, 91)
F32 = jnp.float32
BF16 = jnp.bfloat16
LANES = 128
HEAD = 64
NT = (((1,), (1,)), ((), ()))
TN = (((0,), (0,)), ((), ()))
MIB = 2**20


def bucket_index(relative):
    distance = jnp.abs(relative)
    farther = jnp.full(relative.shape, 8, jnp.int32)
    for boundary in BOUNDARIES:
        farther = farther + (distance >= boundary).astype(jnp.int32)
    nearest = jnp.where(distance < 8, distance, farther)
    return nearest + 16 * (relative > 0).astype(jnp.int32)


def norm_rows(values, gain_row):
    return (
        values * lax.rsqrt(jnp.mean(values * values, axis=-1, keepdims=True) + EPSILON) * gain_row
    )


def attend_kernel(q_ref, k_ref, v_ref, line_ref, out_ref, kept_ref, slab_ref, *, rows):
    length = q_ref.shape[0]
    lane = lax.broadcasted_iota(jnp.int32, (1, LANES), 1)
    keys, values = k_ref[...], v_ref[...]
    for head in range(2):
        line = jnp.broadcast_to(line_ref[head], (rows, 2 * length))
        slab_ref[head] = pltpu.roll(line, 0, 1, stride=1, stride_axis=0)
    for step in range(length // rows):
        block = pl.ds(step * rows, rows)
        queries = q_ref[block, :].astype(F32) * HEAD**-0.5
        joined = []
        for head in range(2):
            mine = (lane < HEAD) if head == 0 else (lane >= HEAD)
            own = jnp.where(mine, queries, 0.0).astype(BF16)
            scores = lax.dot_general(own, keys, NT, preferred_element_type=F32)
            scores = scores + slab_ref[head, :, pl.ds(length - rows * step, length)]
            top = jnp.max(scores, axis=1, keepdims=True)
            raised = jnp.exp(scores - top)
            total = jnp.sum(raised, axis=1, keepdims=True)
            weights = (raised * (1.0 / total)).astype(BF16)
            kept_ref[head, block, :] = weights
            joined.append(jnp.dot(weights, values, preferred_element_type=F32))
        out_ref[block, :] = jnp.where(lane < HEAD, joined[0], joined[1]).astype(BF16)


def attend(projected, lines, rows):
    length, features = projected.shape[0], projected.shape[1] // 3
    heads = lines.shape[0]
    pairs = heads // 2
    return pl.pallas_call(
        functools.partial(attend_kernel, rows=rows),
        grid=(pairs,),
        in_specs=[
            pl.BlockSpec((length, LANES), lambda i: (0, i)),
            pl.BlockSpec((length, LANES), lambda i: (0, pairs + i)),
            pl.BlockSpec((length, LANES), lambda i: (0, 2 * pairs + i)),
            pl.BlockSpec((2, 1, 2 * length), lambda i: (i, 0, 0)),
        ],
        out_specs=[
            pl.BlockSpec((length, LANES), lambda i: (0, i)),
            pl.BlockSpec((2, length, length), lambda i: (i, 0, 0)),
        ],
        out_shape=[
            jax.ShapeDtypeStruct((length, features), BF16),
            jax.ShapeDtypeStruct((heads, length, length), BF16),
        ],
        scratch_shapes=[pltpu.VMEM((2, rows, 2 * length), F32)],
        compiler_params=pltpu.CompilerParams(vmem_limit_bytes=50 * MIB),
        cost_estimate=pl.CostEstimate(
            flops=16 * heads * length * length * HEAD,
            bytes_accessed=2 * heads * length * length + 8 * length * features,
            transcendentals=heads * length * length,
        ),
    )(projected, projected, projected, lines)


def attend_back_kernel(
    q_ref, k_ref, v_ref, out_ref, dout_ref, kept_ref, tile_ref,
    grad_ref, band_ref, far_ref, dscores_ref, *, rows,
):
    length = q_ref.shape[0]
    tiles = length // LANES
    inner = rows // LANES
    lane = lax.broadcasted_iota(jnp.int32, (1, LANES), 1)
    queries, values, dout = q_ref[...], v_ref[...], dout_ref[...]
    widened = jnp.concatenate([k_ref[...], tile_ref[...]], axis=1)
    dout_wide = dout.astype(F32)
    product = dout_wide * out_ref[...].astype(F32)
    dout_turned, queries_turned = dout.T, queries.T
    dqueries = [[], []]
    dkeys, dvalues = [], []
    for head in range(2):
        mine = (lane < HEAD) if head == 0 else (lane >= HEAD)
        inner_sum = jnp.sum(jnp.where(mine, product, 0.0), axis=1, keepdims=True)
        own = jnp.where(mine, dout_wide, 0.0).astype(BF16)
        band_ref[head] = jnp.zeros_like(band_ref[head])
        for step in range(length // rows):
            first = step * rows
            block = pl.ds(first, rows)
            dprob = lax.dot_general(
                own[first : first + rows], values, NT, preferred_element_type=F32
            )
            dscores = kept_ref[head, block, :].astype(F32) * (
                dprob - inner_sum[first : first + rows]
            )
            rounded = dscores.astype(BF16)
            dscores_ref[block, :] = rounded
            for part in range(inner):
                tile = step * inner + part
                low, high = max(tile - 1, 0), min(tile + 2, tiles)
                at = low - (tile - 1)
                band_ref[head, :, at * LANES : (at + high - low) * LANES] += dscores[
                    part * LANES : (part + 1) * LANES, low * LANES : high * LANES
                ]
            both = jnp.dot(rounded, widened, preferred_element_type=F32)
            dqueries[head].append(both[:, :LANES])
            for part in range(inner):
                far_ref[head, step * inner + part] = jnp.sum(
                    both[part * LANES : (part + 1) * LANES, LANES:], axis=0
                )
        half = slice(HEAD * head, HEAD * head + HEAD)
        dkeys.append(jnp.dot(queries_turned[half], dscores_ref[...], preferred_element_type=F32))
        dvalues.append(jnp.dot(dout_turned[half], kept_ref[head], preferred_element_type=F32))
    scale = HEAD**-0.5
    for step in range(length // rows):
        grad_ref[0, pl.ds(step * rows, rows), :] = (
            jnp.where(lane < HEAD, dqueries[0][step], dqueries[1][step]) * scale
        ).astype(BF16)
    grad_ref[1] = (jnp.concatenate(dkeys, axis=0) * scale).T.astype(BF16)
    grad_ref[2] = jnp.concatenate(dvalues, axis=0).T.astype(BF16)


def attend_back(projected, attended, datt, kept, rows):
    length, features = projected.shape[0], projected.shape[1] // 3
    heads = kept.shape[0]
    pairs = heads // 2
    tiles = length // LANES
    tile_of = (
        jnp.arange(length)[:, None] // LANES == jnp.arange(LANES)[None, :]
    ).astype(BF16)
    return pl.pallas_call(
        functools.partial(attend_back_kernel, rows=rows),
        grid=(pairs,),
        in_specs=[
            pl.BlockSpec((length, LANES), lambda i: (0, i)),
            pl.BlockSpec((length, LANES), lambda i: (0, pairs + i)),
            pl.BlockSpec((length, LANES), lambda i: (0, 2 * pairs + i)),
            pl.BlockSpec((length, LANES), lambda i: (0, i)),
            pl.BlockSpec((length, LANES), lambda i: (0, i)),
            pl.BlockSpec((2, length, length), lambda i: (i, 0, 0)),
            pl.BlockSpec((length, LANES), lambda i: (0, 0)),
        ],
        out_specs=[
            pl.BlockSpec((3, length, LANES), lambda i: (0, 0, i)),
            pl.BlockSpec((2, LANES, 3 * LANES), lambda i: (i, 0, 0)),
            pl.BlockSpec((2, tiles, LANES), lambda i: (i, 0, 0)),
        ],
        out_shape=[
            jax.ShapeDtypeStruct((3, length, features), BF16),
            jax.ShapeDtypeStruct((heads, LANES, 3 * LANES), F32),
            jax.ShapeDtypeStruct((heads, tiles, LANES), F32),
        ],
        scratch_shapes=[pltpu.VMEM((length, length), BF16)],
        compiler_params=pltpu.CompilerParams(vmem_limit_bytes=56 * MIB),
        cost_estimate=pl.CostEstimate(
            flops=32 * heads * length * length * HEAD,
            bytes_accessed=2 * heads * length * length + 18 * length * features,
            transcendentals=0,
        ),
    )(projected, projected, projected, attended, datt, kept, tile_of)


def bias_lines(rel_bias, length):
    relative = jnp.arange(2 * length, dtype=jnp.int32) - length
    onehot = (
        bucket_index(relative)[None, :]
        == jnp.arange(rel_bias.shape[0], dtype=jnp.int32)[:, None]
    ).astype(F32)
    return jnp.einsum(
        "ch,cr->hr", rel_bias.astype(F32), onehot, precision=lax.Precision.HIGHEST
    )[:, None, :]


def table_gradient(band, far, bucket_count):
    heads, tiles = far.shape[0], far.shape[1]
    relative = jnp.arange(3 * LANES)[None, :] - LANES - jnp.arange(LANES)[:, None]
    onehot = (bucket_index(relative)[:, :, None] == jnp.arange(bucket_count)).astype(F32)
    near = jnp.dot(
        band.reshape(heads, -1),
        onehot.reshape(-1, bucket_count),
        precision=lax.Precision.HIGHEST,
    )
    here = jnp.arange(tiles)[:, None]
    there = jnp.arange(LANES)[None, :]
    before = jnp.sum(jnp.where(there <= here - 2, far, 0.0), axis=(1, 2))
    after = jnp.sum(jnp.where(there >= here + 2, far, 0.0), axis=(1, 2))
    buckets = jnp.arange(bucket_count)
    last = bucket_index(jnp.array([-length_far(), length_far()], jnp.int32))
    return (
        near
        + before[:, None] * (buckets == last[0])
        + after[:, None] * (buckets == last[1])
    ).T


def length_far():
    return LANES


def expert_kernel(
    hidden_ref, cot_ref, w_in_ref, w_out_ref, router_ref,
    made_ref, back_ref, first_ref, second_ref, drouter_ref,
    w_in, w_out, x, c, x_turned, dexp_turned, moved, act, dpre, stage_first, stage_second, load_sem, cot_sem, out_sem, sent, came, moved_sent, moved_came, core_sent,
    core_came, stage_sem, core_ready, *, ranks, expert_count, rows, width, columns,
):
    features = x.shape[1]
    slots = x.shape[0] // ranks
    hidden_width = w_in.shape[1]
    half = hidden_width // 2
    per_step = rows // slots
    core, me = lax.axis_index("group"), lax.axis_index("expert")
    plane = 4 if ranks % 4 == 0 else 1
    layers = ranks // plane

    def partner(k, sign):
        layer = (me // plane + layers + sign * (k // plane)) % layers
        return layer * plane + (me % plane + plane + sign * (k % plane)) % plane

    def span(k):
        return pl.ds(pl.multiple_of(k * slots, slots), slots)

    barrier = pltpu.get_barrier_semaphore()

    def greet(k, carry):
        pl.semaphore_signal(
            barrier, inc=1, device_id=(core, partner(k, 1)), device_id_type=pl.DeviceIdType.MESH
        )
        return carry

    lax.fori_loop(1, ranks, greet, 0)
    pl.semaphore_signal(
        barrier, inc=1, device_id=(1 - core, me), device_id_type=pl.DeviceIdType.MESH
    )

    loads = [
        pltpu.make_async_copy(w_in_ref, w_in, load_sem.at[0]),
        pltpu.make_async_copy(w_out_ref, w_out, load_sem.at[1]),
        pltpu.make_async_copy(hidden_ref.at[me], x.at[pl.ds(0, slots)], load_sem.at[2]),
    ]
    for load in loads:
        load.start()

    def cot_copy(k):
        return pltpu.make_async_copy(cot_ref.at[partner(k, -1)], c.at[span(k)], cot_sem.at[k])

    def load_cot(k, carry):
        cot_copy(k).start()
        return carry

    lax.fori_loop(0, ranks, load_cot, 0)
    pl.semaphore_wait(barrier, ranks)

    def hidden_copy(k):
        return pltpu.make_async_remote_copy(
            src_ref=hidden_ref.at[partner(k, 1)],
            dst_ref=x.at[span(k)],
            send_sem=sent.at[k],
            recv_sem=came.at[k],
            device_id=(core, partner(k, 1)),
            device_id_type=pl.DeviceIdType.MESH,
        )

    def moved_copy(k):
        return pltpu.make_async_remote_copy(
            src_ref=moved.at[span(k)],
            dst_ref=back_ref.at[me],
            send_sem=moved_sent.at[k],
            recv_sem=moved_came.at[k],
            device_id=(core, partner(k, -1)),
            device_id_type=pl.DeviceIdType.MESH,
        )

    def own_moved_copy():
        return pltpu.make_async_copy(moved.at[pl.ds(0, slots)], back_ref.at[me], load_sem.at[3])

    def made_copy(k):
        return pltpu.make_async_copy(c.at[span(k)], made_ref.at[partner(k, -1)], out_sem.at[k])

    def start_hidden(k, carry):
        hidden_copy(k).start()
        return carry

    lax.fori_loop(1, ranks, start_hidden, 0)
    for load in loads:
        load.wait()
    drouter_ref[...] = jnp.zeros_like(drouter_ref)
    root = (2.0 / jnp.pi) ** 0.5

    def run(first_rank):
        block = pl.ds(pl.multiple_of(first_rank * slots, rows), rows)
        xs = x[block, :]
        upstream = c[block, :].astype(F32)
        router_weight = router_ref[...]
        lane = lax.broadcasted_iota(jnp.int32, (1, router_weight.shape[1]), 1)
        logits = jnp.dot(xs, router_weight, preferred_element_type=F32)
        logits = jnp.where(lane < expert_count, logits, -jnp.inf)
        raised = jnp.exp(logits - jnp.max(logits, axis=-1, keepdims=True))
        router = raised / jnp.sum(raised, axis=-1, keepdims=True)
        chosen = (lane == me).astype(F32)
        gate = jnp.sum(router * chosen, axis=-1, keepdims=True)
        dexp = (gate * upstream).astype(BF16)
        made = jnp.zeros((rows, features), F32)
        dmoved = jnp.zeros((rows, features), F32)
        for at in range(0, hidden_width, width):
            part = slice(at, at + width)
            pre = jnp.dot(xs, w_in[:, part], preferred_element_type=F32)
            square = pre * pre
            turned = jnp.tanh(pre * (root + (root * 0.044715) * square))
            upper = 0.5 + 0.5 * turned
            active = (pre * upper).astype(BF16)
            slope = upper + pre * (upper * (1.0 - turned)) * (
                root + (3 * root * 0.044715) * square
            )
            act[block, part] = active
            made = made + jnp.dot(active, w_out[part, :], preferred_element_type=F32)
            dact = lax.dot_general(dexp, w_out[part, :], NT, preferred_element_type=F32)
            dpart = (dact * slope).astype(BF16)
            dpre[block, part] = dpart
            dmoved = dmoved + lax.dot_general(
                dpart, w_in[:, part], NT, preferred_element_type=F32
            )
        made = made.astype(BF16)
        c[block, :] = made
        dgate = jnp.sum(upstream * made.astype(F32), axis=-1, keepdims=True)
        dlogits = (dgate * gate * (chosen - router)).astype(BF16)
        dmoved = dmoved + lax.dot_general(dlogits, router_weight, NT, preferred_element_type=F32)
        moved[block, :] = dmoved.astype(BF16)
        xt = xs.T
        x_turned[:, block] = xt
        dexp_turned[:, block] = dexp.T
        drouter_ref[...] += jnp.dot(xt, dlogits, preferred_element_type=F32)

    def step(number, carry):
        first_rank = number * per_step
        for inner in range(per_step):
            k = first_rank + inner
            cot_copy(k).wait()

            @pl.when(k > 0)
            def _(k=k):
                hidden_copy(k).wait_recv()

        run(first_rank)
        for inner in range(per_step):
            k = first_rank + inner
            made_copy(k).start()

            @pl.when(k > 0)
            def _(k=k):
                moved_copy(k).start()

        @pl.when(number == 0)
        def _():
            own_moved_copy().start()

        return carry

    lax.fori_loop(0, ranks // per_step, step, 0)

    other = 1 - core
    across = features // columns

    def landed_first(n):
        return pl.ds(n // across * features, features), pl.ds(n % across * columns, columns)

    def first_copy(n):
        part = pl.ds(n * columns, columns)
        return pltpu.make_async_remote_copy(
            src_ref=w_in.at[:, part],
            dst_ref=c.at[landed_first(n)],
            send_sem=core_sent.at[0, n],
            recv_sem=core_came.at[0, n],
            device_id=(other, me),
            device_id_type=pl.DeviceIdType.MESH,
        )

    def second_copy(n):
        part = pl.ds(n * columns, columns)
        return pltpu.make_async_remote_copy(
            src_ref=w_out.at[part],
            dst_ref=x.at[part],
            send_sem=core_sent.at[1, n],
            recv_sem=core_came.at[1, n],
            device_id=(other, me),
            device_id_type=pl.DeviceIdType.MESH,
        )

    def product(turned, wide, part):
        return jnp.dot(turned[...], wide[:, part], preferred_element_type=F32)

    def made_out(k, carry):
        made_copy(k).wait()
        return carry

    lax.fori_loop(0, ranks, made_out, 0)
    pl.semaphore_signal(
        core_ready, inc=1, device_id=(other, me), device_id_type=pl.DeviceIdType.MESH
    )
    tiles = half // columns
    for n in range(tiles):
        part = pl.ds(pl.multiple_of(other * half + n * columns, columns), columns)
        w_in[:, n * columns : (n + 1) * columns] = product(x_turned, dpre, part).astype(BF16)
        if n == 0:
            pl.semaphore_wait(core_ready, 1)
        first_copy(n).start()
        w_out[n * columns : (n + 1) * columns, :] = product(dexp_turned, act, part).T.astype(BF16)
        second_copy(n).start()
    stores = []
    for n in range(tiles):
        part = pl.ds(pl.multiple_of(core * half + n * columns, columns), columns)
        here = slice(n * columns, (n + 1) * columns)
        own = product(x_turned, dpre, part)
        first_copy(n).wait_recv()
        if n:
            stores[2 * n - 2].wait()
        stage_first[...] = own + c[landed_first(n)].astype(F32)
        stores.append(
            pltpu.make_async_copy(
                stage_first, first_ref.at[:, pl.ds(n * columns, columns)],
                stage_sem.at[0, n],
            )
        )
        stores[-1].start()
        own = product(dexp_turned, act, part).T
        second_copy(n).wait_recv()
        if n:
            stores[2 * n - 1].wait()
        stage_second[...] = own + x[here, :].astype(F32)
        stores.append(
            pltpu.make_async_copy(
                stage_second, second_ref.at[pl.ds(n * columns, columns)],
                stage_sem.at[1, n],
            )
        )
        stores[-1].start()
    for store in stores[-2:]:
        store.wait()
    for n in range(tiles):
        first_copy(n).wait_send()
        second_copy(n).wait_send()

    def finish(k, carry):
        @pl.when(k > 0)
        def _():
            hidden_copy(k).wait_send()
            moved_copy(k).wait_send()
            moved_copy(k).wait_recv()

        return carry

    lax.fori_loop(0, ranks, finish, 0)
    own_moved_copy().wait()


def run_expert(hidden, cot, w_in, w_out, router_padded, expert_count):
    ranks, slots, features = hidden.shape
    hidden_width = w_in.shape[1]
    rows = max(min(256, ranks * slots), slots)
    total = ranks * slots
    padded = router_padded.shape[1]
    half = hidden_width // 2
    columns = min(256, half)
    tiles = half // columns
    any_ref = pl.BlockSpec(memory_space=pl.ANY)
    vmem = pl.BlockSpec(memory_space=pltpu.VMEM)
    dma = pltpu.SemaphoreType.DMA
    return pl.pallas_call(
        functools.partial(
            expert_kernel,
            ranks=ranks,
            expert_count=expert_count,
            rows=rows,
            width=min(512, hidden_width),
            columns=columns,
        ),
        in_specs=[any_ref, any_ref, any_ref, any_ref, vmem],
        out_specs=[any_ref, any_ref, any_ref, any_ref, vmem],
        out_shape=[
            jax.ShapeDtypeStruct((ranks, slots, features), BF16),
            jax.ShapeDtypeStruct((ranks, slots, features), BF16),
            jax.ShapeDtypeStruct((features, half), F32),
            jax.ShapeDtypeStruct((half, features), F32),
            jax.ShapeDtypeStruct((features, padded), F32),
        ],
        scratch_shapes=[
            pltpu.VMEM((features, hidden_width), BF16),
            pltpu.VMEM((hidden_width, features), BF16),
            pltpu.VMEM((total, features), BF16),
            pltpu.VMEM((total, features), BF16),
            pltpu.VMEM((features, total), BF16),
            pltpu.VMEM((features, total), BF16),
            pltpu.VMEM((total, features), BF16),
            pltpu.VMEM((total, hidden_width), BF16),
            pltpu.VMEM((total, hidden_width), BF16),
            pltpu.VMEM((features, columns), F32),
            pltpu.VMEM((columns, features), F32),
            dma((4,)),
            dma((ranks,)),
            dma((ranks,)),
            dma((ranks,)),
            dma((ranks,)),
            dma((ranks,)),
            dma((ranks,)),
            dma((2, tiles)),
            dma((2, tiles)),
            dma((2, tiles)),
            pltpu.SemaphoreType.REGULAR,
        ],
        compiler_params=pltpu.CompilerParams(
            collective_id=1, has_side_effects=True, vmem_limit_bytes=63 * MIB
        ),
        cost_estimate=pl.CostEstimate(
            flops=12 * total * features * hidden_width,
            bytes_accessed=8 * features * hidden_width + 8 * total * features,
            transcendentals=total * hidden_width,
        ),
    )(hidden, cot, w_in, w_out, router_padded)


def core_sum(values, dim):
    half = values.shape[dim] // 2
    core = lax.axis_index("group")
    own = lax.dynamic_slice_in_dim(values, core * half, half, dim)
    other = lax.dynamic_slice_in_dim(values, (1 - core) * half, half, dim).astype(BF16)
    return own + lax.ppermute(other, "group", [(0, 1), (1, 0)]).astype(F32)


def exchange(values):
    return lax.all_to_all(values, "expert", split_axis=0, concat_axis=0, tiled=True)


def per_device(
    tokens, gains, qkv_weight, out_weight, rel_bias, router_weight, w_in, w_out, routes, factors,
    cotangent,
):
    length, features = tokens.shape
    bucket_count = rel_bias.shape[0]
    expert_count = router_weight.shape[1]
    slot_count = 2 * length // expert_count
    rows = min(256, length)
    gain_rows = gains.astype(F32)
    w_in, w_out = w_in[0], w_out[0]
    me = lax.axis_index("expert")
    core = lax.axis_index("group")

    routed = routes[:, 0]
    row_index = jnp.arange(length, dtype=jnp.int32)
    chosen = routed[:, None] == jnp.arange(expert_count, dtype=jnp.int32)[None, :]
    earlier = (row_index[:, None] > row_index[None, :]).astype(BF16)
    before = jnp.dot(earlier, chosen.astype(BF16), preferred_element_type=F32)
    place = jnp.sum(before * chosen.astype(F32), axis=-1).astype(jnp.int32)
    capacity = factors[0] * (length // expert_count)
    target = jnp.where(place < capacity, routed * slot_count + place, -1)
    slots = jnp.arange(expert_count * slot_count, dtype=jnp.int32)
    picks = (slots[:, None] == target[None, :]).astype(BF16)

    def pack(values):
        packed = jnp.dot(picks, values, preferred_element_type=F32).astype(BF16)
        return packed.reshape(expert_count, slot_count, features)

    def unpack(values):
        return lax.dot_general(
            picks, values.reshape(-1, features), TN, preferred_element_type=F32
        )

    upstream_there = exchange(pack(cotangent))

    inputs = tokens.astype(F32)
    normed_in = norm_rows(inputs, gain_rows[0]).astype(BF16)
    projected = jnp.dot(normed_in, qkv_weight, preferred_element_type=F32).astype(BF16)
    attended, kept = attend(projected, bias_lines(rel_bias, length), rows)
    residual_one = inputs + jnp.dot(attended, out_weight, preferred_element_type=F32)
    hidden = norm_rows(residual_one, gain_rows[1]).astype(BF16)

    logits = jnp.dot(hidden, router_weight, preferred_element_type=F32)
    raised = jnp.exp(logits - jnp.max(logits, axis=-1, keepdims=True))
    router = raised / jnp.sum(raised, axis=-1, keepdims=True)
    gate_value = jnp.sum(router * chosen.astype(F32), axis=-1)

    padded = -expert_count % LANES
    router_padded = jnp.pad(router_weight, ((0, 0), (0, padded)))
    hidden, upstream_there = lax.optimization_barrier((hidden, upstream_there))
    made, dmoved_back, grad_first, grad_second, drouter = run_expert(
        pack(hidden), upstream_there, w_in, w_out, router_padded, expert_count
    )
    made_back = exchange(made)
    grad_router = drouter[:, :expert_count]

    dhidden = unpack(dmoved_back)
    upstream = cotangent.astype(F32)
    _, back_two = jax.vjp(norm_rows, residual_one, gain_rows[1])
    dres_norm, dgain_two = back_two(dhidden)
    dres = upstream + dres_norm
    dbranch = dres.astype(BF16)
    datt = lax.dot_general(dbranch, out_weight, NT, preferred_element_type=F32).astype(BF16)
    grad_out = lax.dot_general(attended, dbranch, TN, preferred_element_type=F32)
    dqkv, band, far = attend_back(projected, attended, datt, kept, rows)
    grad_proj = jnp.einsum("td,cte->dce", normed_in, dqkv, preferred_element_type=F32)
    grad_proj = grad_proj.reshape(features, 3 * features)
    dnormed = jnp.einsum(
        "cte,dce->td",
        dqkv,
        qkv_weight.reshape(features, 3, features),
        preferred_element_type=F32,
    )
    _, back_one = jax.vjp(norm_rows, inputs, gain_rows[0])
    dinput_norm, dgain_one = back_one(dnormed)
    grad_tokens = dres + dinput_norm

    brought = unpack(made_back)
    output = (residual_one + gate_value[:, None] * brought).astype(BF16)

    def scattered(values):
        return lax.psum_scatter(
            core_sum(values, 1).astype(BF16), "expert", scatter_dimension=0, tiled=True
        ).astype(F32)

    small = [
        jnp.stack([dgain_one, dgain_two], axis=0),
        grad_router,
        table_gradient(band, far, bucket_count),
    ]
    flat = lax.psum(jnp.concatenate([s.reshape(-1) for s in small]), ("group", "expert"))
    summed = []
    at = 0
    for s in small:
        summed.append(flat[at : at + s.size].reshape(s.shape))
        at += s.size
    experts = lax.axis_size("expert")
    cores = lax.axis_size("group")
    grad_gains = lax.dynamic_slice(
        summed[0], (core, me * (features // experts)), (2 // cores, features // experts)
    )
    grad_router = lax.dynamic_slice(
        summed[1],
        (me * (features // experts), core * (expert_count // cores)),
        (features // experts, expert_count // cores),
    )
    return (
        output,
        grad_tokens,
        grad_gains,
        scattered(grad_proj),
        scattered(grad_out),
        summed[2],
        grad_router,
        grad_first[None],
        grad_second[None],
    )


def solution(mesh):
    return jax.shard_map(
        per_device,
        mesh=mesh,
        in_specs=(
            P(("group", "expert"), None),
            P(),
            P(),
            P(),
            P(),
            P(),
            P("expert", None, None),
            P("expert", None, None),
            P(("group", "expert"), None),
            P(("group", "expert")),
            P(("group", "expert"), None),
        ),
        out_specs=(
            P(("group", "expert"), None),
            P(("group", "expert"), None),
            P("group", "expert"),
            P("expert", "group"),
            P("expert", "group"),
            P(),
            P("expert", "group"),
            P("expert", None, "group"),
            P("expert", "group", None),
        ),
        check_vma=False,
    )
```

```python
import functools

import jax
import jax.numpy as jnp
from jax import lax
from jax.experimental import pallas as pl
from jax.experimental.pallas import tpu as pltpu
from jax.sharding import PartitionSpec as P

EPSILON = 1e-06
BOUNDARIES = (12, 16, 23, 32, 46, 64, 91)
F32 = jnp.float32
BF16 = jnp.bfloat16
LANES = 128
HEAD = 64
NT = (((1,), (1,)), ((), ()))
TN = (((0,), (0,)), ((), ()))
MIB = 2**20


def bucket_index(relative):
    distance = jnp.abs(relative)
    farther = jnp.full(relative.shape, 8, jnp.int32)
    for boundary in BOUNDARIES:
        farther = farther + (distance >= boundary).astype(jnp.int32)
    nearest = jnp.where(distance < 8, distance, farther)
    return nearest + 16 * (relative > 0).astype(jnp.int32)


def norm_rows(values, gain_row):
    return (
        values * lax.rsqrt(jnp.mean(values * values, axis=-1, keepdims=True) + EPSILON) * gain_row
    )


def attend_kernel(q_ref, k_ref, v_ref, line_ref, out_ref, kept_ref, slab_ref, *, rows):
    length = q_ref.shape[0]
    lane = lax.broadcasted_iota(jnp.int32, (1, LANES), 1)
    keys, values = k_ref[...], v_ref[...]
    for head in range(2):
        line = jnp.broadcast_to(line_ref[head], (rows, 2 * length))
        slab_ref[head] = pltpu.roll(line, 0, 1, stride=1, stride_axis=0)
    for step in range(length // rows):
        block = pl.ds(step * rows, rows)
        queries = q_ref[block, :].astype(F32) * HEAD**-0.5
        joined = []
        for head in range(2):
            mine = (lane < HEAD) if head == 0 else (lane >= HEAD)
            own = jnp.where(mine, queries, 0.0).astype(BF16)
            scores = lax.dot_general(own, keys, NT, preferred_element_type=F32)
            scores = scores + slab_ref[head, :, pl.ds(length - rows * step, length)]
            top = jnp.max(scores, axis=1, keepdims=True)
            raised = jnp.exp(scores - top)
            total = jnp.sum(raised, axis=1, keepdims=True)
            weights = (raised * (1.0 / total)).astype(BF16)
            kept_ref[head, block, :] = weights
            joined.append(jnp.dot(weights, values, preferred_element_type=F32))
        out_ref[block, :] = jnp.where(lane < HEAD, joined[0], joined[1]).astype(BF16)


def attend(projected, lines, rows):
    length, features = projected.shape[0], projected.shape[1] // 3
    heads = lines.shape[0]
    pairs = heads // 2
    return pl.pallas_call(
        functools.partial(attend_kernel, rows=rows),
        grid=(pairs,),
        in_specs=[
            pl.BlockSpec((length, LANES), lambda i: (0, i)),
            pl.BlockSpec((length, LANES), lambda i: (0, pairs + i)),
            pl.BlockSpec((length, LANES), lambda i: (0, 2 * pairs + i)),
            pl.BlockSpec((2, 1, 2 * length), lambda i: (i, 0, 0)),
        ],
        out_specs=[
            pl.BlockSpec((length, LANES), lambda i: (0, i)),
            pl.BlockSpec((2, length, length), lambda i: (i, 0, 0)),
        ],
        out_shape=[
            jax.ShapeDtypeStruct((length, features), BF16),
            jax.ShapeDtypeStruct((heads, length, length), BF16),
        ],
        scratch_shapes=[pltpu.VMEM((2, rows, 2 * length), F32)],
        compiler_params=pltpu.CompilerParams(vmem_limit_bytes=50 * MIB),
        cost_estimate=pl.CostEstimate(
            flops=16 * heads * length * length * HEAD,
            bytes_accessed=2 * heads * length * length + 8 * length * features,
            transcendentals=heads * length * length,
        ),
    )(projected, projected, projected, lines)


def attend_back_kernel(
    q_ref, k_ref, v_ref, out_ref, dout_ref, kept_ref, tile_ref,
    grad_ref, band_ref, far_ref, dscores_ref, *, rows,
):
    length = q_ref.shape[0]
    tiles = length // LANES
    inner = rows // LANES
    lane = lax.broadcasted_iota(jnp.int32, (1, LANES), 1)
    queries, values, dout = q_ref[...], v_ref[...], dout_ref[...]
    widened = jnp.concatenate([k_ref[...], tile_ref[...]], axis=1)
    dout_wide = dout.astype(F32)
    product = dout_wide * out_ref[...].astype(F32)
    dout_turned, queries_turned = dout.T, queries.T
    dqueries = [[], []]
    dkeys, dvalues = [], []
    for head in range(2):
        mine = (lane < HEAD) if head == 0 else (lane >= HEAD)
        inner_sum = jnp.sum(jnp.where(mine, product, 0.0), axis=1, keepdims=True)
        own = jnp.where(mine, dout_wide, 0.0).astype(BF16)
        band_ref[head] = jnp.zeros_like(band_ref[head])
        for step in range(length // rows):
            first = step * rows
            block = pl.ds(first, rows)
            dprob = lax.dot_general(
                own[first : first + rows], values, NT, preferred_element_type=F32
            )
            dscores = kept_ref[head, block, :].astype(F32) * (
                dprob - inner_sum[first : first + rows]
            )
            rounded = dscores.astype(BF16)
            dscores_ref[block, :] = rounded
            for part in range(inner):
                tile = step * inner + part
                low, high = max(tile - 1, 0), min(tile + 2, tiles)
                at = low - (tile - 1)
                band_ref[head, :, at * LANES : (at + high - low) * LANES] += dscores[
                    part * LANES : (part + 1) * LANES, low * LANES : high * LANES
                ]
            both = jnp.dot(rounded, widened, preferred_element_type=F32)
            dqueries[head].append(both[:, :LANES])
            for part in range(inner):
                far_ref[head, step * inner + part] = jnp.sum(
                    both[part * LANES : (part + 1) * LANES, LANES:], axis=0
                )
        half = slice(HEAD * head, HEAD * head + HEAD)
        dkeys.append(jnp.dot(queries_turned[half], dscores_ref[...], preferred_element_type=F32))
        dvalues.append(jnp.dot(dout_turned[half], kept_ref[head], preferred_element_type=F32))
    scale = HEAD**-0.5
    for step in range(length // rows):
        grad_ref[0, pl.ds(step * rows, rows), :] = (
            jnp.where(lane < HEAD, dqueries[0][step], dqueries[1][step]) * scale
        ).astype(BF16)
    grad_ref[1] = (jnp.concatenate(dkeys, axis=0) * scale).T.astype(BF16)
    grad_ref[2] = jnp.concatenate(dvalues, axis=0).T.astype(BF16)


def attend_back(projected, attended, datt, kept, rows):
    length, features = projected.shape[0], projected.shape[1] // 3
    heads = kept.shape[0]
    pairs = heads // 2
    tiles = length // LANES
    tile_of = (
        jnp.arange(length)[:, None] // LANES == jnp.arange(LANES)[None, :]
    ).astype(BF16)
    return pl.pallas_call(
        functools.partial(attend_back_kernel, rows=rows),
        grid=(pairs,),
        in_specs=[
            pl.BlockSpec((length, LANES), lambda i: (0, i)),
            pl.BlockSpec((length, LANES), lambda i: (0, pairs + i)),
            pl.BlockSpec((length, LANES), lambda i: (0, 2 * pairs + i)),
            pl.BlockSpec((length, LANES), lambda i: (0, i)),
            pl.BlockSpec((length, LANES), lambda i: (0, i)),
            pl.BlockSpec((2, length, length), lambda i: (i, 0, 0)),
            pl.BlockSpec((length, LANES), lambda i: (0, 0)),
        ],
        out_specs=[
            pl.BlockSpec((3, length, LANES), lambda i: (0, 0, i)),
            pl.BlockSpec((2, LANES, 3 * LANES), lambda i: (i, 0, 0)),
            pl.BlockSpec((2, tiles, LANES), lambda i: (i, 0, 0)),
        ],
        out_shape=[
            jax.ShapeDtypeStruct((3, length, features), BF16),
            jax.ShapeDtypeStruct((heads, LANES, 3 * LANES), F32),
            jax.ShapeDtypeStruct((heads, tiles, LANES), F32),
        ],
        scratch_shapes=[pltpu.VMEM((length, length), BF16)],
        compiler_params=pltpu.CompilerParams(vmem_limit_bytes=56 * MIB),
        cost_estimate=pl.CostEstimate(
            flops=32 * heads * length * length * HEAD,
            bytes_accessed=2 * heads * length * length + 18 * length * features,
            transcendentals=0,
        ),
    )(projected, projected, projected, attended, datt, kept, tile_of)


def bias_lines(rel_bias, length):
    relative = jnp.arange(2 * length, dtype=jnp.int32) - length
    onehot = (
        bucket_index(relative)[None, :]
        == jnp.arange(rel_bias.shape[0], dtype=jnp.int32)[:, None]
    ).astype(F32)
    return jnp.einsum(
        "ch,cr->hr", rel_bias.astype(F32), onehot, precision=lax.Precision.HIGHEST
    )[:, None, :]


def table_gradient(band, far, bucket_count):
    heads, tiles = far.shape[0], far.shape[1]
    relative = jnp.arange(3 * LANES)[None, :] - LANES - jnp.arange(LANES)[:, None]
    onehot = (bucket_index(relative)[:, :, None] == jnp.arange(bucket_count)).astype(F32)
    near = jnp.dot(
        band.reshape(heads, -1),
        onehot.reshape(-1, bucket_count),
        precision=lax.Precision.HIGHEST,
    )
    here = jnp.arange(tiles)[:, None]
    there = jnp.arange(LANES)[None, :]
    before = jnp.sum(jnp.where(there <= here - 2, far, 0.0), axis=(1, 2))
    after = jnp.sum(jnp.where(there >= here + 2, far, 0.0), axis=(1, 2))
    buckets = jnp.arange(bucket_count)
    last = bucket_index(jnp.array([-length_far(), length_far()], jnp.int32))
    return (
        near
        + before[:, None] * (buckets == last[0])
        + after[:, None] * (buckets == last[1])
    ).T


def length_far():
    return LANES


def expert_kernel(
    hidden_ref, cot_ref, w_in_ref, w_out_ref, router_ref,
    made_ref, back_ref, first_ref, second_ref, drouter_ref,
    w_in, w_out, x, c, x_turned, dexp_turned, moved, act, dpre, stage_first, stage_second, load_sem, cot_sem, out_sem, sent, came, moved_sent, moved_came, core_sent,
    core_came, stage_sem, core_ready, *, ranks, expert_count, rows, width, columns,
):
    features = x.shape[1]
    slots = x.shape[0] // ranks
    hidden_width = w_in.shape[1]
    half = hidden_width // 2
    per_step = rows // slots
    core, me = lax.axis_index("group"), lax.axis_index("expert")
    plane = 4 if ranks % 4 == 0 else 1
    layers = ranks // plane

    def partner(k, sign):
        layer = (me // plane + layers + sign * (k // plane)) % layers
        return layer * plane + (me % plane + plane + sign * (k % plane)) % plane

    def span(k):
        return pl.ds(pl.multiple_of(k * slots, slots), slots)

    barrier = pltpu.get_barrier_semaphore()

    def greet(k, carry):
        pl.semaphore_signal(
            barrier, inc=1, device_id=(core, partner(k, 1)), device_id_type=pl.DeviceIdType.MESH
        )
        return carry

    lax.fori_loop(1, ranks, greet, 0)
    pl.semaphore_signal(
        barrier, inc=1, device_id=(1 - core, me), device_id_type=pl.DeviceIdType.MESH
    )

    loads = [
        pltpu.make_async_copy(w_in_ref, w_in, load_sem.at[0]),
        pltpu.make_async_copy(w_out_ref, w_out, load_sem.at[1]),
        pltpu.make_async_copy(hidden_ref.at[me], x.at[pl.ds(0, slots)], load_sem.at[2]),
    ]
    for load in loads:
        load.start()

    def cot_copy(k):
        return pltpu.make_async_copy(cot_ref.at[partner(k, -1)], c.at[span(k)], cot_sem.at[k])

    def load_cot(k, carry):
        cot_copy(k).start()
        return carry

    lax.fori_loop(0, ranks, load_cot, 0)
    pl.semaphore_wait(barrier, ranks)

    def hidden_copy(k):
        return pltpu.make_async_remote_copy(
            src_ref=hidden_ref.at[partner(k, 1)],
            dst_ref=x.at[span(k)],
            send_sem=sent.at[k],
            recv_sem=came.at[k],
            device_id=(core, partner(k, 1)),
            device_id_type=pl.DeviceIdType.MESH,
        )

    def moved_copy(k):
        return pltpu.make_async_remote_copy(
            src_ref=moved.at[span(k)],
            dst_ref=back_ref.at[me],
            send_sem=moved_sent.at[k],
            recv_sem=moved_came.at[k],
            device_id=(core, partner(k, -1)),
            device_id_type=pl.DeviceIdType.MESH,
        )

    def own_moved_copy():
        return pltpu.make_async_copy(moved.at[pl.ds(0, slots)], back_ref.at[me], load_sem.at[3])

    def made_copy(k):
        return pltpu.make_async_copy(c.at[span(k)], made_ref.at[partner(k, -1)], out_sem.at[k])

    def start_hidden(k, carry):
        hidden_copy(k).start()
        return carry

    lax.fori_loop(1, ranks, start_hidden, 0)
    for load in loads:
        load.wait()
    drouter_ref[...] = jnp.zeros_like(drouter_ref)
    root = (2.0 / jnp.pi) ** 0.5

    def run(first_rank):
        block = pl.ds(pl.multiple_of(first_rank * slots, rows), rows)
        xs = x[block, :]
        upstream = c[block, :].astype(F32)
        router_weight = router_ref[...]
        lane = lax.broadcasted_iota(jnp.int32, (1, router_weight.shape[1]), 1)
        logits = jnp.dot(xs, router_weight, preferred_element_type=F32)
        logits = jnp.where(lane < expert_count, logits, -jnp.inf)
        raised = jnp.exp(logits - jnp.max(logits, axis=-1, keepdims=True))
        router = raised / jnp.sum(raised, axis=-1, keepdims=True)
        chosen = (lane == me).astype(F32)
        gate = jnp.sum(router * chosen, axis=-1, keepdims=True)
        dexp = (gate * upstream).astype(BF16)
        made = jnp.zeros((rows, features), F32)
        dmoved = jnp.zeros((rows, features), F32)
        for at in range(0, hidden_width, width):
            part = slice(at, at + width)
            pre = jnp.dot(xs, w_in[:, part], preferred_element_type=F32)
            square = pre * pre
            turned = jnp.tanh(pre * (root + (root * 0.044715) * square))
            upper = 0.5 + 0.5 * turned
            active = (pre * upper).astype(BF16)
            slope = upper + pre * (upper * (1.0 - turned)) * (
                root + (3 * root * 0.044715) * square
            )
            act[block, part] = active
            made = made + jnp.dot(active, w_out[part, :], preferred_element_type=F32)
            dact = lax.dot_general(dexp, w_out[part, :], NT, preferred_element_type=F32)
            dpart = (dact * slope).astype(BF16)
            dpre[block, part] = dpart
            dmoved = dmoved + lax.dot_general(
                dpart, w_in[:, part], NT, preferred_element_type=F32
            )
        made = made.astype(BF16)
        c[block, :] = made
        dgate = jnp.sum(upstream * made.astype(F32), axis=-1, keepdims=True)
        dlogits = (dgate * gate * (chosen - router)).astype(BF16)
        dmoved = dmoved + lax.dot_general(dlogits, router_weight, NT, preferred_element_type=F32)
        moved[block, :] = dmoved.astype(BF16)
        xt = xs.T
        x_turned[:, block] = xt
        dexp_turned[:, block] = dexp.T
        drouter_ref[...] += jnp.dot(xt, dlogits, preferred_element_type=F32)

    def step(number, carry):
        first_rank = number * per_step
        for inner in range(per_step):
            k = first_rank + inner
            cot_copy(k).wait()

            @pl.when(k > 0)
            def _(k=k):
                hidden_copy(k).wait_recv()

        run(first_rank)
        for inner in range(per_step):
            k = first_rank + inner
            made_copy(k).start()

            @pl.when(k > 0)
            def _(k=k):
                moved_copy(k).start()

        @pl.when(number == 0)
        def _():
            own_moved_copy().start()

        return carry

    lax.fori_loop(0, ranks // per_step, step, 0)

    other = 1 - core
    across = features // columns

    def landed_first(n):
        return pl.ds(n // across * features, features), pl.ds(n % across * columns, columns)

    def first_copy(n):
        part = pl.ds(n * columns, columns)
        return pltpu.make_async_remote_copy(
            src_ref=w_in.at[:, part],
            dst_ref=c.at[landed_first(n)],
            send_sem=core_sent.at[0, n],
            recv_sem=core_came.at[0, n],
            device_id=(other, me),
            device_id_type=pl.DeviceIdType.MESH,
        )

    def second_copy(n):
        part = pl.ds(n * columns, columns)
        return pltpu.make_async_remote_copy(
            src_ref=w_out.at[part],
            dst_ref=x.at[part],
            send_sem=core_sent.at[1, n],
            recv_sem=core_came.at[1, n],
            device_id=(other, me),
            device_id_type=pl.DeviceIdType.MESH,
        )

    def product(turned, wide, part):
        return jnp.dot(turned[...], wide[:, part], preferred_element_type=F32)

    def made_out(k, carry):
        made_copy(k).wait()
        return carry

    lax.fori_loop(0, ranks, made_out, 0)
    pl.semaphore_signal(
        core_ready, inc=1, device_id=(other, me), device_id_type=pl.DeviceIdType.MESH
    )
    tiles = half // columns
    for n in range(tiles):
        part = pl.ds(pl.multiple_of(other * half + n * columns, columns), columns)
        w_in[:, n * columns : (n + 1) * columns] = product(x_turned, dpre, part).astype(BF16)
        if n == 0:
            pl.semaphore_wait(core_ready, 1)
        first_copy(n).start()
        w_out[n * columns : (n + 1) * columns, :] = product(dexp_turned, act, part).T.astype(BF16)
        second_copy(n).start()
    stores = []
    for n in range(tiles):
        part = pl.ds(pl.multiple_of(core * half + n * columns, columns), columns)
        here = slice(n * columns, (n + 1) * columns)
        own = product(x_turned, dpre, part)
        first_copy(n).wait_recv()
        if n:
            stores[2 * n - 2].wait()
        stage_first[...] = own + c[landed_first(n)].astype(F32)
        stores.append(
            pltpu.make_async_copy(
                stage_first, first_ref.at[:, pl.ds(n * columns, columns)],
                stage_sem.at[0, n],
            )
        )
        stores[-1].start()
        own = product(dexp_turned, act, part).T
        second_copy(n).wait_recv()
        if n:
            stores[2 * n - 1].wait()
        stage_second[...] = own + x[here, :].astype(F32)
        stores.append(
            pltpu.make_async_copy(
                stage_second, second_ref.at[pl.ds(n * columns, columns)],
                stage_sem.at[1, n],
            )
        )
        stores[-1].start()
    for store in stores[-2:]:
        store.wait()
    for n in range(tiles):
        first_copy(n).wait_send()
        second_copy(n).wait_send()

    def finish(k, carry):
        @pl.when(k > 0)
        def _():
            hidden_copy(k).wait_send()
            moved_copy(k).wait_send()
            moved_copy(k).wait_recv()

        return carry

    lax.fori_loop(0, ranks, finish, 0)
    own_moved_copy().wait()


def run_expert(hidden, cot, w_in, w_out, router_padded, expert_count):
    ranks, slots, features = hidden.shape
    hidden_width = w_in.shape[1]
    rows = max(min(256, ranks * slots), slots)
    total = ranks * slots
    padded = router_padded.shape[1]
    half = hidden_width // 2
    columns = min(256, half)
    tiles = half // columns
    any_ref = pl.BlockSpec(memory_space=pl.ANY)
    vmem = pl.BlockSpec(memory_space=pltpu.VMEM)
    dma = pltpu.SemaphoreType.DMA
    return pl.pallas_call(
        functools.partial(
            expert_kernel,
            ranks=ranks,
            expert_count=expert_count,
            rows=rows,
            width=min(512, hidden_width),
            columns=columns,
        ),
        in_specs=[any_ref, any_ref, any_ref, any_ref, vmem],
        out_specs=[any_ref, any_ref, any_ref, any_ref, vmem],
        out_shape=[
            jax.ShapeDtypeStruct((ranks, slots, features), BF16),
            jax.ShapeDtypeStruct((ranks, slots, features), BF16),
            jax.ShapeDtypeStruct((features, half), F32),
            jax.ShapeDtypeStruct((half, features), F32),
            jax.ShapeDtypeStruct((features, padded), F32),
        ],
        scratch_shapes=[
            pltpu.VMEM((features, hidden_width), BF16),
            pltpu.VMEM((hidden_width, features), BF16),
            pltpu.VMEM((total, features), BF16),
            pltpu.VMEM((total, features), BF16),
            pltpu.VMEM((features, total), BF16),
            pltpu.VMEM((features, total), BF16),
            pltpu.VMEM((total, features), BF16),
            pltpu.VMEM((total, hidden_width), BF16),
            pltpu.VMEM((total, hidden_width), BF16),
            pltpu.VMEM((features, columns), F32),
            pltpu.VMEM((columns, features), F32),
            dma((4,)),
            dma((ranks,)),
            dma((ranks,)),
            dma((ranks,)),
            dma((ranks,)),
            dma((ranks,)),
            dma((ranks,)),
            dma((2, tiles)),
            dma((2, tiles)),
            dma((2, tiles)),
            pltpu.SemaphoreType.REGULAR,
        ],
        compiler_params=pltpu.CompilerParams(
            collective_id=1, has_side_effects=True, vmem_limit_bytes=63 * MIB
        ),
        cost_estimate=pl.CostEstimate(
            flops=12 * total * features * hidden_width,
            bytes_accessed=8 * features * hidden_width + 8 * total * features,
            transcendentals=total * hidden_width,
        ),
    )(hidden, cot, w_in, w_out, router_padded)


def tail_kernel(
    q_ref, k_ref, v_ref, out_ref, dout_ref, kept_ref, wq_ref, wk_ref, wv_ref, tile_ref,
    normed_ref, tokens_ref, dres_ref, gain_ref, dgain_ref, bucket_ref, first_ref,
    tokens_grad_ref, dense_ref, early_ref, small_ref,
    dscores, dnormed, lines, own, core_out, core_in, plane_out, plane_in, layer_out, layer_in,
    early_core, early_own, early_plane_out, early_plane_in, early_layer_out, early_layer_in,
    small_out, small_in, load_sem, core_sent, core_came, plane_sent, plane_came, layer_sent,
    layer_came, small_sent, small_came, *, rows, ranks, plane,
):
    length, features = tokens_ref.shape
    tiles = length // LANES
    inner = rows // LANES
    layers = ranks // plane
    slab = features // ranks
    heads = 2 * (pl.num_programs(0) - 1)
    groups = (pl.num_programs(0) - 1) // 2
    step = pl.program_id(0)
    core, me = lax.axis_index("group"), lax.axis_index("expert")
    other = 1 - core
    layer, spot = me // plane, me % plane
    mesh = pl.DeviceIdType.MESH

    def in_plane(k, sign):
        return (spot + plane + sign * k) % plane

    def in_line(k, sign):
        return (layer + layers + sign * k) % layers

    def rank_of(a_layer, a_spot):
        return a_layer * plane + a_spot

    def core_copy(unit):
        early = unit == 0
        return pltpu.make_async_remote_copy(
            src_ref=first_ref.at[other] if early else core_out.at[unit - 1],
            dst_ref=early_core if early else core_in.at[unit - 1],
            send_sem=core_sent.at[unit],
            recv_sem=core_came.at[unit],
            device_id=(other, me),
            device_id_type=mesh,
        )

    def plane_copy(unit, k):
        early = unit == 0
        source = early_plane_out if early else plane_out.at[unit - 1]
        return pltpu.make_async_remote_copy(
            src_ref=source.at[:, in_plane(k, 1)],
            dst_ref=early_plane_in.at[k - 1] if early else plane_in.at[unit - 1, k - 1],
            send_sem=plane_sent.at[unit, k],
            recv_sem=plane_came.at[unit, k],
            device_id=(core, rank_of(layer, in_plane(k, 1))),
            device_id_type=mesh,
        )

    def layer_copy(unit, k):
        early = unit == 0
        source = early_layer_out if early else layer_out.at[unit - 1]
        return pltpu.make_async_remote_copy(
            src_ref=source.at[in_line(k, 1)],
            dst_ref=early_layer_in.at[k - 1] if early else layer_in.at[unit - 1, k - 1],
            send_sem=layer_sent.at[unit, k],
            recv_sem=layer_came.at[unit, k],
            device_id=(core, rank_of(in_line(k, 1), spot)),
            device_id_type=mesh,
        )

    def peer(number):
        return (core + number // ranks) % 2, (me + number) % ranks

    def small_copy(number):
        return pltpu.make_async_remote_copy(
            src_ref=small_out,
            dst_ref=small_in.at[number],
            send_sem=small_sent.at[number],
            recv_sem=small_came.at[number],
            device_id=peer(number),
            device_id_type=mesh,
        )

    def own_load():
        return pltpu.make_async_copy(first_ref.at[core], early_own, load_sem.at[0])

    def sum_cores(unit):
        core_copy(unit).wait_recv()
        if unit == 0:
            own_load().wait()
            summed = early_own[...].astype(F32) + early_core[...].astype(F32)
            early_plane_out[...] = summed.astype(BF16).reshape(early_plane_out.shape)
        else:
            summed = own[unit % 2] + core_in[unit - 1].astype(F32)
            plane_out[unit - 1] = summed.astype(BF16).reshape(plane_out.shape[1:])
        for k in range(1, plane):
            plane_copy(unit, k).start()

    def sum_planes(unit):
        summed = (early_plane_out[:, spot] if unit == 0 else plane_out[unit - 1, :, spot]).astype(F32)
        for k in range(1, plane):
            plane_copy(unit, k).wait_recv()
            came = early_plane_in[k - 1] if unit == 0 else plane_in[unit - 1, k - 1]
            summed = summed + came.astype(F32)
        if unit == 0:
            early_layer_out[...] = summed.astype(BF16)
        else:
            layer_out[unit - 1] = summed.astype(BF16)
        for k in range(1, layers):
            layer_copy(unit, k).start()

    def sum_layers(unit):
        summed = (early_layer_out[layer] if unit == 0 else layer_out[unit - 1, layer]).astype(F32)
        for k in range(1, layers):
            layer_copy(unit, k).wait_recv()
            came = early_layer_in[k - 1] if unit == 0 else layer_in[unit - 1, k - 1]
            summed = summed + came.astype(F32)
        if unit == 0:
            early_ref[...] = summed
        else:
            group = unit - 1
            base = core * (groups * LANES)
            keys_at = other * (2 * groups * LANES) + group * LANES
            for part, at in enumerate(
                (base + group * LANES, base + (groups + group) * LANES, keys_at)
            ):
                dense_ref[:, pl.ds(pl.multiple_of(at, LANES), LANES)] = summed[
                    :, part * LANES : (part + 1) * LANES
                ]

    @pl.when(step == 0)
    def _():
        own_load().start()
        barrier = pltpu.get_barrier_semaphore()

        def greet(number, carry):
            pl.semaphore_signal(barrier, inc=1, device_id=peer(number), device_id_type=mesh)
            return carry

        lax.fori_loop(1, 2 * ranks, greet, 0)
        dnormed[...] = jnp.zeros_like(dnormed)
        pl.semaphore_wait(barrier, 2 * ranks - 1)
        core_copy(0).start()

    @pl.when(step < 2 * groups)
    def _():
        lane = lax.broadcasted_iota(jnp.int32, (1, LANES), 1)
        queries, values, dout = q_ref[...], v_ref[...], dout_ref[...]
        widened = jnp.concatenate([k_ref[...], tile_ref[...]], axis=1)
        dout_wide = dout.astype(F32)
        product = dout_wide * out_ref[...].astype(F32)
        dout_turned, queries_turned = dout.T, queries.T
        mirror = (
            lax.broadcasted_iota(jnp.int32, (LANES, LANES), 0)
            + lax.broadcasted_iota(jnp.int32, (LANES, LANES), 1)
            == LANES - 1
        ).astype(F32)
        dqueries = [[], []]
        dkeys, dvalues = [], []
        for head in range(2):
            mine = (lane < HEAD) if head == 0 else (lane >= HEAD)
            inner_sum = jnp.sum(jnp.where(mine, product, 0.0), axis=1, keepdims=True)
            masked = jnp.where(mine, dout_wide, 0.0).astype(BF16)
            bands = [jnp.zeros((LANES, LANES), F32) for _ in range(3)]
            before = jnp.zeros((1, LANES), F32)
            after = jnp.zeros((1, LANES), F32)
            for part_of in range(length // rows):
                first = part_of * rows
                block = pl.ds(first, rows)
                dprob = lax.dot_general(
                    masked[first : first + rows], values, NT, preferred_element_type=F32
                )
                scores = kept_ref[head, block, :].astype(F32) * (
                    dprob - inner_sum[first : first + rows]
                )
                rounded = scores.astype(BF16)
                dscores[block, :] = rounded
                both = jnp.dot(rounded, widened, preferred_element_type=F32)
                dqueries[head].append(both[:, :LANES])
                for part in range(inner):
                    tile = part_of * inner + part
                    here = slice(part * LANES, (part + 1) * LANES)
                    for at in range(3):
                        there = tile - 1 + at
                        if 0 <= there < tiles:
                            bands[at] = bands[at] + scores[here, there * LANES : (there + 1) * LANES]
                    sums = jnp.sum(both[here, LANES:], axis=0, keepdims=True)
                    before = before + jnp.where(lane <= tile - 2, sums, 0.0)
                    after = after + jnp.where((lane >= tile + 2) & (lane < tiles), sums, 0.0)
            band = jnp.concatenate([*bands, jnp.zeros((LANES, LANES), F32)], axis=1)
            band = jnp.dot(
                mirror, band, preferred_element_type=F32, precision=lax.Precision.HIGHEST
            )
            band = pltpu.roll(band, 3 * LANES + 1, 1, stride=1, stride_axis=0)
            near = jnp.sum(band, axis=0, keepdims=True)
            pair = step % 2 * groups + step // 2
            lines[pl.ds(2 * pair + head, 1), :] = jnp.concatenate([near, before, after], axis=1)
            half = slice(HEAD * head, HEAD * head + HEAD)
            dkeys.append(
                jnp.dot(queries_turned[half], dscores[...], preferred_element_type=F32)
            )
            dvalues.append(jnp.dot(dout_turned[half], kept_ref[head], preferred_element_type=F32))
        scale = HEAD**-0.5
        dq = jnp.concatenate(
            [
                (jnp.where(lane < HEAD, left, right) * scale).astype(BF16)
                for left, right in zip(*dqueries, strict=True)
            ],
            axis=0,
        )
        dk = (jnp.concatenate(dkeys, axis=0) * scale).T.astype(BF16)
        dv = jnp.concatenate(dvalues, axis=0).T.astype(BF16)
        joined = jnp.concatenate([dq, dk, dv], axis=1)
        weights = jnp.concatenate([wq_ref[...], wk_ref[...], wv_ref[...]], axis=1)
        dnormed[...] += lax.dot_general(joined, weights, NT, preferred_element_type=F32)
        dense = jnp.dot(normed_ref[...], joined, preferred_element_type=F32)
        dwq, dwk, dwv = dense[:, :LANES], dense[:, LANES : 2 * LANES], dense[:, 2 * LANES :]
        own_first, away_first = jnp.where(core == 0, dwq, dwv), jnp.where(core == 0, dwv, dwq)
        for now in range(2 * groups):

            @pl.when(step == now)
            def _(now=now):
                unit, part = now // 2 + 1, now % 2
                at = slice(part * LANES, (part + 1) * LANES)
                own[unit % 2, :, at] = own_first
                core_out[unit - 1, :, at] = away_first.astype(BF16)

                @pl.when(core == part)
                def _():
                    own[unit % 2, :, 2 * LANES :] = dwk

                @pl.when(core != part)
                def _():
                    core_out[unit - 1, :, 2 * LANES :] = dwk.astype(BF16)

                if part == 1:
                    core_copy(unit).start()

    last = 2 * groups
    plan = {}
    for unit in range(groups + 1):
        made = 0 if unit == 0 else 2 * unit - 1
        plan.setdefault(min(made + 1, last), []).append((sum_cores, unit))
        plan.setdefault(min(made + 3, last), []).append((sum_planes, unit))
        plan.setdefault(min(made + 5, last), []).append((sum_layers, unit))
    order = [sum_layers, sum_planes, sum_cores]
    for now in range(1, last):

        @pl.when(step == now)
        def _(now=now):
            for action, unit in sorted(plan.get(now, []), key=lambda p: order.index(p[0])):
                action(unit)

    @pl.when(step == last)
    def _():
        todo = plan.get(last, [])
        for action, unit in todo:
            if action is sum_cores:
                action(unit)
        for action, unit in todo:
            if action is sum_planes and unit < groups:
                action(unit)
        gain = gain_ref[...]
        inputs = tokens_ref[...].astype(F32)
        spread = lax.rsqrt(jnp.mean(inputs * inputs, axis=1, keepdims=True) + EPSILON)
        back = dnormed[...]
        scaled = inputs * spread
        dgain = jnp.sum(back * scaled, axis=0, keepdims=True)
        moved = back * gain
        tokens_grad_ref[...] = dres_ref[...] + spread * (
            moved - scaled * jnp.mean(moved * scaled, axis=1, keepdims=True)
        )
        table = jnp.dot(
            lines[...], bucket_ref[...], preferred_element_type=F32, precision=lax.Precision.HIGHEST
        )
        small_out[0 : lines.shape[0], :] = table
        base = lines.shape[0]
        wide = features // LANES
        for part in range(wide):
            small_out[base + part : base + part + 1, :] = dgain[
                :, part * LANES : (part + 1) * LANES
            ]
        small_out[base + wide : base + 2 * wide, :] = dgain_ref[...]
        if small_out.shape[0] > base + 2 * wide:
            small_out[base + 2 * wide :, :] = jnp.zeros(
                (small_out.shape[0] - base - 2 * wide, LANES), F32
            )

        def start_small(number, carry):
            small_copy(number).start()
            return carry

        lax.fori_loop(1, 2 * ranks, start_small, 0)
        for action, unit in todo:
            if action is sum_planes and unit == groups:
                action(unit)
        for action, unit in todo:
            if action is sum_layers:
                action(unit)
        small_ref[...] = small_out[...]

        def add_small(number, carry):
            small_copy(number).wait_recv()
            small_ref[...] += small_in[number]
            return carry

        lax.fori_loop(1, 2 * ranks, add_small, 0)

        def drop_small(number, carry):
            small_copy(number).wait_send()
            return carry

        lax.fori_loop(1, 2 * ranks, drop_small, 0)
        for unit in range(groups + 1):
            core_copy(unit).wait_send()
            for k in range(1, plane):
                plane_copy(unit, k).wait_send()
            for k in range(1, layers):
                layer_copy(unit, k).wait_send()


def run_tail(
    projected, attended, datt, kept, qkv_weight, normed_turned, tokens, dres, gain, dgain, first, ranks,
    bucket_count, rows,
):
    length, features = tokens.shape
    heads = kept.shape[0]
    pairs = heads // 2
    groups = pairs // 2
    plane = 4
    layers = ranks // plane
    slab = features // ranks
    early = first.shape[2]
    late = 3 * LANES
    tile_of = (
        jnp.arange(length)[:, None] // LANES == jnp.arange(LANES)[None, :]
    ).astype(BF16)
    at = jnp.arange(4 * LANES, dtype=jnp.int32)
    relative = jnp.where(at < 3 * LANES, at - LANES, at - 5 * LANES)
    ends = bucket_index(jnp.array([-length, length], jnp.int32))
    bucket = jnp.concatenate([bucket_index(relative), jnp.repeat(ends, LANES)])
    bucket_of = (bucket[:, None] == jnp.arange(LANES)[None, :]).astype(F32)
    line_rows = heads + -heads % 4
    small_rows = line_rows + 2 * (features // LANES)
    small_rows += -small_rows % 8

    def pair_of(i):
        i = jnp.minimum(i, pairs - 1)
        return i % 2 * groups + i // 2

    def column(shape, offset):
        return pl.BlockSpec(shape, lambda i: (0, offset + pair_of(i)))

    def whole(shape):
        return pl.BlockSpec(shape, lambda i: (0, 0), pipeline_mode=pl.Buffered(1))

    dma = pltpu.SemaphoreType.DMA
    units = groups + 1
    return pl.pallas_call(
        functools.partial(tail_kernel, rows=rows, ranks=ranks, plane=plane),
        grid=(pairs + 1,),
        in_specs=[
            column((length, LANES), 0),
            column((length, LANES), pairs),
            column((length, LANES), 2 * pairs),
            column((length, LANES), 0),
            column((length, LANES), 0),
            pl.BlockSpec((2, length, length), lambda i: (pair_of(i), 0, 0)),
            column((features, LANES), 0),
            column((features, LANES), pairs),
            column((features, LANES), 2 * pairs),
            whole((length, LANES)),
            whole((features, length)),
            whole((length, features)),
            whole((length, features)),
            whole((1, features)),
            whole(dgain.shape),
            whole(bucket_of.shape),
            pl.BlockSpec(memory_space=pl.ANY),
        ],
        out_specs=[
            whole((length, features)),
            whole((slab, groups * late)),
            whole((slab, early)),
            whole((small_rows, LANES)),
        ],
        out_shape=[
            jax.ShapeDtypeStruct((length, features), F32),
            jax.ShapeDtypeStruct((slab, groups * late), F32),
            jax.ShapeDtypeStruct((slab, early), F32),
            jax.ShapeDtypeStruct((small_rows, LANES), F32),
        ],
        scratch_shapes=[
            pltpu.VMEM((length, length), BF16),
            pltpu.VMEM((length, features), F32),
            pltpu.VMEM((line_rows, 6 * LANES), F32),
            pltpu.VMEM((2, features, late), F32),
            pltpu.VMEM((groups, features, late), BF16),
            pltpu.VMEM((groups, features, late), BF16),
            pltpu.VMEM((groups, layers, plane, slab, late), BF16),
            pltpu.VMEM((groups, plane - 1, layers, slab, late), BF16),
            pltpu.VMEM((groups, layers, slab, late), BF16),
            pltpu.VMEM((groups, layers - 1, slab, late), BF16),
            pltpu.VMEM((features, early), BF16),
            pltpu.VMEM((features, early), BF16),
            pltpu.VMEM((layers, plane, slab, early), BF16),
            pltpu.VMEM((plane - 1, layers, slab, early), BF16),
            pltpu.VMEM((layers, slab, early), BF16),
            pltpu.VMEM((layers - 1, slab, early), BF16),
            pltpu.VMEM((small_rows, LANES), F32),
            pltpu.VMEM((2 * ranks, small_rows, LANES), F32),
            dma((1,)),
            dma((units,)),
            dma((units,)),
            dma((units, plane)),
            dma((units, plane)),
            dma((units, layers)),
            dma((units, layers)),
            dma((2 * ranks,)),
            dma((2 * ranks,)),
        ],
        compiler_params=pltpu.CompilerParams(
            collective_id=2, has_side_effects=True, vmem_limit_bytes=62 * MIB
        ),
        cost_estimate=pl.CostEstimate(
            flops=36 * heads * length * length * HEAD,
            bytes_accessed=2 * heads * length * length + 30 * length * features,
            transcendentals=0,
        ),
    )(
        projected, projected, projected, attended, datt, kept, qkv_weight, qkv_weight, qkv_weight,
        tile_of, normed_turned, tokens, dres, gain, dgain, bucket_of, first,
    )


def core_sum(values, dim):
    half = values.shape[dim] // 2
    core = lax.axis_index("group")
    own = lax.dynamic_slice_in_dim(values, core * half, half, dim)
    other = lax.dynamic_slice_in_dim(values, (1 - core) * half, half, dim).astype(BF16)
    return own + lax.ppermute(other, "group", [(0, 1), (1, 0)]).astype(F32)


def exchange(values):
    return lax.all_to_all(values, "expert", split_axis=0, concat_axis=0, tiled=True)


def per_device(
    tokens, gains, qkv_weight, out_weight, rel_bias, router_weight, w_in, w_out, routes, factors,
    cotangent,
):
    length, features = tokens.shape
    bucket_count = rel_bias.shape[0]
    expert_count = router_weight.shape[1]
    slot_count = 2 * length // expert_count
    rows = min(256, length)
    gain_rows = gains.astype(F32)
    w_in, w_out = w_in[0], w_out[0]
    me = lax.axis_index("expert")
    core = lax.axis_index("group")

    routed = routes[:, 0]
    row_index = jnp.arange(length, dtype=jnp.int32)
    chosen = routed[:, None] == jnp.arange(expert_count, dtype=jnp.int32)[None, :]
    earlier = (row_index[:, None] > row_index[None, :]).astype(BF16)
    before = jnp.dot(earlier, chosen.astype(BF16), preferred_element_type=F32)
    place = jnp.sum(before * chosen.astype(F32), axis=-1).astype(jnp.int32)
    capacity = factors[0] * (length // expert_count)
    target = jnp.where(place < capacity, routed * slot_count + place, -1)
    slots = jnp.arange(expert_count * slot_count, dtype=jnp.int32)
    picks = (slots[:, None] == target[None, :]).astype(BF16)

    def pack(values):
        packed = jnp.dot(picks, values, preferred_element_type=F32).astype(BF16)
        return packed.reshape(expert_count, slot_count, features)

    def unpack(values):
        return lax.dot_general(
            picks, values.reshape(-1, features), TN, preferred_element_type=F32
        )

    upstream_there = exchange(pack(cotangent))

    inputs = tokens.astype(F32)
    normed_in = norm_rows(inputs, gain_rows[0]).astype(BF16)
    projected = jnp.dot(normed_in, qkv_weight, preferred_element_type=F32).astype(BF16)
    attended, kept = attend(projected, bias_lines(rel_bias, length), rows)
    residual_one = inputs + jnp.dot(attended, out_weight, preferred_element_type=F32)
    hidden = norm_rows(residual_one, gain_rows[1]).astype(BF16)

    logits = jnp.dot(hidden, router_weight, preferred_element_type=F32)
    raised = jnp.exp(logits - jnp.max(logits, axis=-1, keepdims=True))
    router = raised / jnp.sum(raised, axis=-1, keepdims=True)
    gate_value = jnp.sum(router * chosen.astype(F32), axis=-1)

    padded = -expert_count % LANES
    router_padded = jnp.pad(router_weight, ((0, 0), (0, padded)))
    hidden, upstream_there = lax.optimization_barrier((hidden, upstream_there))
    made, dmoved_back, grad_first, grad_second, drouter = run_expert(
        pack(hidden), upstream_there, w_in, w_out, router_padded, expert_count
    )
    made_back = exchange(made)
    grad_router = drouter[:, :expert_count]

    def finish():
        return (residual_one + gate_value[:, None] * unpack(made_back)).astype(BF16)

    dhidden = unpack(dmoved_back)
    upstream = cotangent.astype(F32)
    _, back_two = jax.vjp(norm_rows, residual_one, gain_rows[1])
    dres_norm, dgain_two = back_two(dhidden)
    dres = upstream + dres_norm
    dbranch = dres.astype(BF16)
    datt = lax.dot_general(dbranch, out_weight, NT, preferred_element_type=F32).astype(BF16)
    experts = lax.axis_size("expert")
    cores = lax.axis_size("group")
    slab = features // experts
    gain_at = (core, me * slab)
    if experts == 16 and cores == 2 and expert_count <= 2 * LANES and features % (16 * experts) == 0:
        dense_out = jnp.einsum(
            "td,tce->cde",
            attended,
            dbranch.reshape(length, cores, features // cores),
            preferred_element_type=F32,
        )
        router_half = jnp.moveaxis(grad_router.reshape(features, cores, -1), 1, 0)
        router_half = jnp.pad(router_half, ((0, 0), (0, 0), (0, LANES - router_half.shape[2])))
        first = jnp.concatenate([dense_out, router_half], axis=2).astype(BF16)
        grad_tokens, grad_qkv, early, small = run_tail(
            projected, attended, datt, kept, qkv_weight, normed_in.T, tokens, dres, gain_rows[:1],
            dgain_two.reshape(-1, LANES), first, experts, bucket_count, rows,
        )
        heads = rel_bias.shape[1]
        gain_sums = small[heads + -heads % 4 :][: 2 * features // LANES].reshape(2, features)
        return (
            finish(),
            grad_tokens,
            lax.dynamic_slice(gain_sums, gain_at, (2 // cores, slab)),
            grad_qkv,
            early[:, : features // cores],
            small[:heads, :bucket_count].T,
            early[:, features // cores : features // cores + expert_count // cores],
            grad_first[None],
            grad_second[None],
        )

    grad_out = lax.dot_general(attended, dbranch, TN, preferred_element_type=F32)
    dqkv, band, far = attend_back(projected, attended, datt, kept, rows)
    grad_proj = jnp.einsum("td,cte->dce", normed_in, dqkv, preferred_element_type=F32)
    grad_proj = grad_proj.reshape(features, 3 * features)
    dnormed = jnp.einsum(
        "cte,dce->td",
        dqkv,
        qkv_weight.reshape(features, 3, features),
        preferred_element_type=F32,
    )
    _, back_one = jax.vjp(norm_rows, inputs, gain_rows[0])
    dinput_norm, dgain_one = back_one(dnormed)
    grad_tokens = dres + dinput_norm

    def scattered(values):
        return lax.psum_scatter(
            core_sum(values, 1).astype(BF16), "expert", scatter_dimension=0, tiled=True
        ).astype(F32)

    small = [
        jnp.stack([dgain_one, dgain_two], axis=0),
        grad_router,
        table_gradient(band, far, bucket_count),
    ]
    flat = lax.psum(jnp.concatenate([s.reshape(-1) for s in small]), ("group", "expert"))
    summed = []
    at = 0
    for s in small:
        summed.append(flat[at : at + s.size].reshape(s.shape))
        at += s.size
    grad_gains = lax.dynamic_slice(summed[0], gain_at, (2 // cores, slab))
    grad_router = lax.dynamic_slice(
        summed[1],
        (me * slab, core * (expert_count // cores)),
        (slab, expert_count // cores),
    )
    return (
        finish(),
        grad_tokens,
        grad_gains,
        scattered(grad_proj),
        scattered(grad_out),
        summed[2],
        grad_router,
        grad_first[None],
        grad_second[None],
    )


def solution(mesh):
    return jax.shard_map(
        per_device,
        mesh=mesh,
        in_specs=(
            P(("group", "expert"), None),
            P(),
            P(),
            P(),
            P(),
            P(),
            P("expert", None, None),
            P("expert", None, None),
            P(("group", "expert"), None),
            P(("group", "expert")),
            P(("group", "expert"), None),
        ),
        out_specs=(
            P(("group", "expert"), None),
            P(("group", "expert"), None),
            P("group", "expert"),
            P("expert", "group"),
            P("expert", "group"),
            P(),
            P("expert", "group"),
            P("expert", None, "group"),
            P("expert", "group", None),
        ),
        check_vma=False,
    )
```

```python
import functools

import jax
import jax.numpy as jnp
from jax import lax
from jax.experimental import pallas as pl
from jax.experimental.pallas import tpu as pltpu
from jax.sharding import PartitionSpec as P

EPSILON = 1e-06
BOUNDARIES = (12, 16, 23, 32, 46, 64, 91)
F32 = jnp.float32
BF16 = jnp.bfloat16
LANES = 128
HEAD = 64
NT = (((1,), (1,)), ((), ()))
TN = (((0,), (0,)), ((), ()))
MIB = 2**20


def bucket_index(relative):
    distance = jnp.abs(relative)
    farther = jnp.full(relative.shape, 8, jnp.int32)
    for boundary in BOUNDARIES:
        farther = farther + (distance >= boundary).astype(jnp.int32)
    nearest = jnp.where(distance < 8, distance, farther)
    return nearest + 16 * (relative > 0).astype(jnp.int32)


def norm_rows(values, gain_row):
    return (
        values * lax.rsqrt(jnp.mean(values * values, axis=-1, keepdims=True) + EPSILON) * gain_row
    )


def attend_kernel(q_ref, k_ref, v_ref, line_ref, out_ref, kept_ref, slab_ref, *, rows):
    length = q_ref.shape[0]
    lane = lax.broadcasted_iota(jnp.int32, (1, LANES), 1)
    keys, values = k_ref[...], v_ref[...]
    for head in range(2):
        line = jnp.broadcast_to(line_ref[head], (rows, 2 * length))
        slab_ref[head] = pltpu.roll(line, 0, 1, stride=1, stride_axis=0)
    for step in range(length // rows):
        block = pl.ds(step * rows, rows)
        queries = q_ref[block, :].astype(F32) * HEAD**-0.5
        joined = []
        for head in range(2):
            mine = (lane < HEAD) if head == 0 else (lane >= HEAD)
            own = jnp.where(mine, queries, 0.0).astype(BF16)
            scores = lax.dot_general(own, keys, NT, preferred_element_type=F32)
            scores = scores + slab_ref[head, :, pl.ds(length - rows * step, length)]
            top = jnp.max(scores, axis=1, keepdims=True)
            raised = jnp.exp(scores - top)
            total = jnp.sum(raised, axis=1, keepdims=True)
            weights = (raised * (1.0 / total)).astype(BF16)
            kept_ref[head, block, :] = weights
            joined.append(jnp.dot(weights, values, preferred_element_type=F32))
        out_ref[block, :] = jnp.where(lane < HEAD, joined[0], joined[1]).astype(BF16)


def attend(projected, lines, rows):
    length, features = projected.shape[0], projected.shape[1] // 3
    heads = lines.shape[0]
    pairs = heads // 2
    return pl.pallas_call(
        functools.partial(attend_kernel, rows=rows),
        grid=(pairs,),
        in_specs=[
            pl.BlockSpec((length, LANES), lambda i: (0, i)),
            pl.BlockSpec((length, LANES), lambda i: (0, pairs + i)),
            pl.BlockSpec((length, LANES), lambda i: (0, 2 * pairs + i)),
            pl.BlockSpec((2, 1, 2 * length), lambda i: (i, 0, 0)),
        ],
        out_specs=[
            pl.BlockSpec((length, LANES), lambda i: (0, i)),
            pl.BlockSpec((2, length, length), lambda i: (i, 0, 0)),
        ],
        out_shape=[
            jax.ShapeDtypeStruct((length, features), BF16),
            jax.ShapeDtypeStruct((heads, length, length), BF16),
        ],
        scratch_shapes=[pltpu.VMEM((2, rows, 2 * length), F32)],
        compiler_params=pltpu.CompilerParams(vmem_limit_bytes=50 * MIB),
        cost_estimate=pl.CostEstimate(
            flops=16 * heads * length * length * HEAD,
            bytes_accessed=2 * heads * length * length + 8 * length * features,
            transcendentals=heads * length * length,
        ),
    )(projected, projected, projected, lines)


def attend_back_kernel(
    q_ref, k_ref, v_ref, out_ref, dout_ref, kept_ref, tile_ref,
    grad_ref, band_ref, far_ref, dscores_ref, *, rows,
):
    length = q_ref.shape[0]
    tiles = length // LANES
    inner = rows // LANES
    lane = lax.broadcasted_iota(jnp.int32, (1, LANES), 1)
    queries, values, dout = q_ref[...], v_ref[...], dout_ref[...]
    widened = jnp.concatenate([k_ref[...], tile_ref[...]], axis=1)
    dout_wide = dout.astype(F32)
    product = dout_wide * out_ref[...].astype(F32)
    dout_turned, queries_turned = dout.T, queries.T
    dqueries = [[], []]
    dkeys, dvalues = [], []
    for head in range(2):
        mine = (lane < HEAD) if head == 0 else (lane >= HEAD)
        inner_sum = jnp.sum(jnp.where(mine, product, 0.0), axis=1, keepdims=True)
        own = jnp.where(mine, dout_wide, 0.0).astype(BF16)
        band_ref[head] = jnp.zeros_like(band_ref[head])
        for step in range(length // rows):
            first = step * rows
            block = pl.ds(first, rows)
            dprob = lax.dot_general(
                own[first : first + rows], values, NT, preferred_element_type=F32
            )
            dscores = kept_ref[head, block, :].astype(F32) * (
                dprob - inner_sum[first : first + rows]
            )
            rounded = dscores.astype(BF16)
            dscores_ref[block, :] = rounded
            for part in range(inner):
                tile = step * inner + part
                low, high = max(tile - 1, 0), min(tile + 2, tiles)
                at = low - (tile - 1)
                band_ref[head, :, at * LANES : (at + high - low) * LANES] += dscores[
                    part * LANES : (part + 1) * LANES, low * LANES : high * LANES
                ]
            both = jnp.dot(rounded, widened, preferred_element_type=F32)
            dqueries[head].append(both[:, :LANES])
            for part in range(inner):
                far_ref[head, step * inner + part] = jnp.sum(
                    both[part * LANES : (part + 1) * LANES, LANES:], axis=0
                )
        half = slice(HEAD * head, HEAD * head + HEAD)
        dkeys.append(jnp.dot(queries_turned[half], dscores_ref[...], preferred_element_type=F32))
        dvalues.append(jnp.dot(dout_turned[half], kept_ref[head], preferred_element_type=F32))
    scale = HEAD**-0.5
    for step in range(length // rows):
        grad_ref[0, pl.ds(step * rows, rows), :] = (
            jnp.where(lane < HEAD, dqueries[0][step], dqueries[1][step]) * scale
        ).astype(BF16)
    grad_ref[1] = (jnp.concatenate(dkeys, axis=0) * scale).T.astype(BF16)
    grad_ref[2] = jnp.concatenate(dvalues, axis=0).T.astype(BF16)


def attend_back(projected, attended, datt, kept, rows):
    length, features = projected.shape[0], projected.shape[1] // 3
    heads = kept.shape[0]
    pairs = heads // 2
    tiles = length // LANES
    tile_of = (
        jnp.arange(length)[:, None] // LANES == jnp.arange(LANES)[None, :]
    ).astype(BF16)
    return pl.pallas_call(
        functools.partial(attend_back_kernel, rows=rows),
        grid=(pairs,),
        in_specs=[
            pl.BlockSpec((length, LANES), lambda i: (0, i)),
            pl.BlockSpec((length, LANES), lambda i: (0, pairs + i)),
            pl.BlockSpec((length, LANES), lambda i: (0, 2 * pairs + i)),
            pl.BlockSpec((length, LANES), lambda i: (0, i)),
            pl.BlockSpec((length, LANES), lambda i: (0, i)),
            pl.BlockSpec((2, length, length), lambda i: (i, 0, 0)),
            pl.BlockSpec((length, LANES), lambda i: (0, 0)),
        ],
        out_specs=[
            pl.BlockSpec((3, length, LANES), lambda i: (0, 0, i)),
            pl.BlockSpec((2, LANES, 3 * LANES), lambda i: (i, 0, 0)),
            pl.BlockSpec((2, tiles, LANES), lambda i: (i, 0, 0)),
        ],
        out_shape=[
            jax.ShapeDtypeStruct((3, length, features), BF16),
            jax.ShapeDtypeStruct((heads, LANES, 3 * LANES), F32),
            jax.ShapeDtypeStruct((heads, tiles, LANES), F32),
        ],
        scratch_shapes=[pltpu.VMEM((length, length), BF16)],
        compiler_params=pltpu.CompilerParams(vmem_limit_bytes=56 * MIB),
        cost_estimate=pl.CostEstimate(
            flops=32 * heads * length * length * HEAD,
            bytes_accessed=2 * heads * length * length + 18 * length * features,
            transcendentals=0,
        ),
    )(projected, projected, projected, attended, datt, kept, tile_of)


def bias_lines(rel_bias, length):
    relative = jnp.arange(2 * length, dtype=jnp.int32) - length
    onehot = (
        bucket_index(relative)[None, :]
        == jnp.arange(rel_bias.shape[0], dtype=jnp.int32)[:, None]
    ).astype(F32)
    return jnp.einsum(
        "ch,cr->hr", rel_bias.astype(F32), onehot, precision=lax.Precision.HIGHEST
    )[:, None, :]


def table_gradient(band, far, bucket_count):
    heads, tiles = far.shape[0], far.shape[1]
    relative = jnp.arange(3 * LANES)[None, :] - LANES - jnp.arange(LANES)[:, None]
    onehot = (bucket_index(relative)[:, :, None] == jnp.arange(bucket_count)).astype(F32)
    near = jnp.dot(
        band.reshape(heads, -1),
        onehot.reshape(-1, bucket_count),
        precision=lax.Precision.HIGHEST,
    )
    here = jnp.arange(tiles)[:, None]
    there = jnp.arange(LANES)[None, :]
    before = jnp.sum(jnp.where(there <= here - 2, far, 0.0), axis=(1, 2))
    after = jnp.sum(jnp.where(there >= here + 2, far, 0.0), axis=(1, 2))
    buckets = jnp.arange(bucket_count)
    last = bucket_index(jnp.array([-length_far(), length_far()], jnp.int32))
    return (
        near
        + before[:, None] * (buckets == last[0])
        + after[:, None] * (buckets == last[1])
    ).T


def length_far():
    return LANES


def expert_kernel(
    hidden_ref, cot_ref, w_in_ref, w_out_ref, router_ref,
    made_ref, back_ref, first_ref, second_ref, drouter_ref,
    w_in, w_out, x, c, x_turned, dexp_turned, moved, act, dpre, stage_first, stage_second, load_sem, cot_sem, out_sem, sent, came, moved_sent, moved_came, core_sent,
    core_came, stage_sem, core_ready, *, ranks, expert_count, rows, width, columns,
):
    features = x.shape[1]
    slots = x.shape[0] // ranks
    hidden_width = w_in.shape[1]
    half = hidden_width // 2
    per_step = rows // slots
    core, me = lax.axis_index("group"), lax.axis_index("expert")
    plane = 4 if ranks % 4 == 0 else 1
    layers = ranks // plane

    def partner(k, sign):
        layer = (me // plane + layers + sign * (k // plane)) % layers
        return layer * plane + (me % plane + plane + sign * (k % plane)) % plane

    def span(k):
        return pl.ds(pl.multiple_of(k * slots, slots), slots)

    barrier = pltpu.get_barrier_semaphore()

    def greet(k, carry):
        pl.semaphore_signal(
            barrier, inc=1, device_id=(core, partner(k, 1)), device_id_type=pl.DeviceIdType.MESH
        )
        return carry

    lax.fori_loop(1, ranks, greet, 0)
    pl.semaphore_signal(
        barrier, inc=1, device_id=(1 - core, me), device_id_type=pl.DeviceIdType.MESH
    )

    loads = [
        pltpu.make_async_copy(w_in_ref, w_in, load_sem.at[0]),
        pltpu.make_async_copy(w_out_ref, w_out, load_sem.at[1]),
        pltpu.make_async_copy(hidden_ref.at[me], x.at[pl.ds(0, slots)], load_sem.at[2]),
    ]
    for load in loads:
        load.start()

    def cot_copy(k):
        return pltpu.make_async_copy(cot_ref.at[partner(k, -1)], c.at[span(k)], cot_sem.at[k])

    def load_cot(k, carry):
        cot_copy(k).start()
        return carry

    lax.fori_loop(0, ranks, load_cot, 0)
    pl.semaphore_wait(barrier, ranks)

    def hidden_copy(k):
        return pltpu.make_async_remote_copy(
            src_ref=hidden_ref.at[partner(k, 1)],
            dst_ref=x.at[span(k)],
            send_sem=sent.at[k],
            recv_sem=came.at[k],
            device_id=(core, partner(k, 1)),
            device_id_type=pl.DeviceIdType.MESH,
        )

    def moved_copy(k):
        return pltpu.make_async_remote_copy(
            src_ref=moved.at[span(k)],
            dst_ref=back_ref.at[me],
            send_sem=moved_sent.at[k],
            recv_sem=moved_came.at[k],
            device_id=(core, partner(k, -1)),
            device_id_type=pl.DeviceIdType.MESH,
        )

    def own_moved_copy():
        return pltpu.make_async_copy(moved.at[pl.ds(0, slots)], back_ref.at[me], load_sem.at[3])

    def made_copy(k):
        return pltpu.make_async_copy(c.at[span(k)], made_ref.at[partner(k, -1)], out_sem.at[k])

    def start_hidden(k, carry):
        hidden_copy(k).start()
        return carry

    lax.fori_loop(1, ranks, start_hidden, 0)
    for load in loads:
        load.wait()
    drouter_ref[...] = jnp.zeros_like(drouter_ref)
    root = (2.0 / jnp.pi) ** 0.5

    def run(first_rank):
        block = pl.ds(pl.multiple_of(first_rank * slots, rows), rows)
        xs = x[block, :]
        upstream = c[block, :].astype(F32)
        router_weight = router_ref[...]
        lane = lax.broadcasted_iota(jnp.int32, (1, router_weight.shape[1]), 1)
        logits = jnp.dot(xs, router_weight, preferred_element_type=F32)
        logits = jnp.where(lane < expert_count, logits, -jnp.inf)
        raised = jnp.exp(logits - jnp.max(logits, axis=-1, keepdims=True))
        router = raised / jnp.sum(raised, axis=-1, keepdims=True)
        chosen = (lane == me).astype(F32)
        gate = jnp.sum(router * chosen, axis=-1, keepdims=True)
        dexp = (gate * upstream).astype(BF16)
        made = jnp.zeros((rows, features), F32)
        dmoved = jnp.zeros((rows, features), F32)
        for at in range(0, hidden_width, width):
            part = slice(at, at + width)
            pre = jnp.dot(xs, w_in[:, part], preferred_element_type=F32)
            square = pre * pre
            turned = jnp.tanh(pre * (root + (root * 0.044715) * square))
            upper = 0.5 + 0.5 * turned
            active = (pre * upper).astype(BF16)
            slope = upper + pre * (upper * (1.0 - turned)) * (
                root + (3 * root * 0.044715) * square
            )
            act[block, part] = active
            made = made + jnp.dot(active, w_out[part, :], preferred_element_type=F32)
            dact = lax.dot_general(dexp, w_out[part, :], NT, preferred_element_type=F32)
            dpart = (dact * slope).astype(BF16)
            dpre[block, part] = dpart
            dmoved = dmoved + lax.dot_general(
                dpart, w_in[:, part], NT, preferred_element_type=F32
            )
        made = made.astype(BF16)
        c[block, :] = made
        dgate = jnp.sum(upstream * made.astype(F32), axis=-1, keepdims=True)
        dlogits = (dgate * gate * (chosen - router)).astype(BF16)
        dmoved = dmoved + lax.dot_general(dlogits, router_weight, NT, preferred_element_type=F32)
        moved[block, :] = dmoved.astype(BF16)
        xt = xs.T
        x_turned[:, block] = xt
        dexp_turned[:, block] = dexp.T
        drouter_ref[...] += jnp.dot(xt, dlogits, preferred_element_type=F32)

    def step(number, carry):
        first_rank = number * per_step
        for inner in range(per_step):
            k = first_rank + inner
            cot_copy(k).wait()

            @pl.when(k > 0)
            def _(k=k):
                hidden_copy(k).wait_recv()

        run(first_rank)
        for inner in range(per_step):
            k = first_rank + inner
            made_copy(k).start()

            @pl.when((k > 0) & (k < plane))
            def _(k=k):
                moved_copy(k).start()

        @pl.when(number == 0)
        def _():
            own_moved_copy().start()

        return carry

    lax.fori_loop(0, ranks // per_step, step, 0)

    def start_moved(k, carry):
        moved_copy(k).start()
        return carry

    lax.fori_loop(plane, ranks, start_moved, 0)

    other = 1 - core
    across = features // columns

    def landed_first(n):
        return pl.ds(n // across * features, features), pl.ds(n % across * columns, columns)

    def first_copy(n):
        part = pl.ds(n * columns, columns)
        return pltpu.make_async_remote_copy(
            src_ref=w_in.at[:, part],
            dst_ref=c.at[landed_first(n)],
            send_sem=core_sent.at[0, n],
            recv_sem=core_came.at[0, n],
            device_id=(other, me),
            device_id_type=pl.DeviceIdType.MESH,
        )

    def second_copy(n):
        part = pl.ds(n * columns, columns)
        return pltpu.make_async_remote_copy(
            src_ref=w_out.at[part],
            dst_ref=x.at[part],
            send_sem=core_sent.at[1, n],
            recv_sem=core_came.at[1, n],
            device_id=(other, me),
            device_id_type=pl.DeviceIdType.MESH,
        )

    def product(turned, wide, part):
        return jnp.dot(turned[...], wide[:, part], preferred_element_type=F32)

    def made_out(k, carry):
        made_copy(k).wait()
        return carry

    lax.fori_loop(0, ranks, made_out, 0)
    pl.semaphore_signal(
        core_ready, inc=1, device_id=(other, me), device_id_type=pl.DeviceIdType.MESH
    )
    tiles = half // columns
    for n in range(tiles):
        part = pl.ds(pl.multiple_of(other * half + n * columns, columns), columns)
        w_in[:, n * columns : (n + 1) * columns] = product(x_turned, dpre, part).astype(BF16)
        if n == 0:
            pl.semaphore_wait(core_ready, 1)
        first_copy(n).start()
        w_out[n * columns : (n + 1) * columns, :] = product(dexp_turned, act, part).T.astype(BF16)
        second_copy(n).start()
    stores = []
    for n in range(tiles):
        part = pl.ds(pl.multiple_of(core * half + n * columns, columns), columns)
        here = slice(n * columns, (n + 1) * columns)
        own = product(x_turned, dpre, part)
        first_copy(n).wait_recv()
        if n:
            stores[2 * n - 2].wait()
        stage_first[...] = own + c[landed_first(n)].astype(F32)
        stores.append(
            pltpu.make_async_copy(
                stage_first, first_ref.at[:, pl.ds(n * columns, columns)],
                stage_sem.at[0, n],
            )
        )
        stores[-1].start()
        own = product(dexp_turned, act, part).T
        second_copy(n).wait_recv()
        if n:
            stores[2 * n - 1].wait()
        stage_second[...] = own + x[here, :].astype(F32)
        stores.append(
            pltpu.make_async_copy(
                stage_second, second_ref.at[pl.ds(n * columns, columns)],
                stage_sem.at[1, n],
            )
        )
        stores[-1].start()
    for store in stores[-2:]:
        store.wait()
    for n in range(tiles):
        first_copy(n).wait_send()
        second_copy(n).wait_send()

    def finish(k, carry):
        @pl.when(k > 0)
        def _():
            hidden_copy(k).wait_send()
            moved_copy(k).wait_send()
            moved_copy(k).wait_recv()

        return carry

    lax.fori_loop(0, ranks, finish, 0)
    own_moved_copy().wait()


def run_expert(hidden, cot, w_in, w_out, router_padded, expert_count):
    ranks, slots, features = hidden.shape
    hidden_width = w_in.shape[1]
    rows = max(min(256, ranks * slots), slots)
    total = ranks * slots
    padded = router_padded.shape[1]
    half = hidden_width // 2
    columns = min(256, half)
    tiles = half // columns
    any_ref = pl.BlockSpec(memory_space=pl.ANY)
    vmem = pl.BlockSpec(memory_space=pltpu.VMEM)
    dma = pltpu.SemaphoreType.DMA
    return pl.pallas_call(
        functools.partial(
            expert_kernel,
            ranks=ranks,
            expert_count=expert_count,
            rows=rows,
            width=min(512, hidden_width),
            columns=columns,
        ),
        in_specs=[any_ref, any_ref, any_ref, any_ref, vmem],
        out_specs=[any_ref, any_ref, any_ref, any_ref, vmem],
        out_shape=[
            jax.ShapeDtypeStruct((ranks, slots, features), BF16),
            jax.ShapeDtypeStruct((ranks, slots, features), BF16),
            jax.ShapeDtypeStruct((features, half), F32),
            jax.ShapeDtypeStruct((half, features), F32),
            jax.ShapeDtypeStruct((features, padded), F32),
        ],
        scratch_shapes=[
            pltpu.VMEM((features, hidden_width), BF16),
            pltpu.VMEM((hidden_width, features), BF16),
            pltpu.VMEM((total, features), BF16),
            pltpu.VMEM((total, features), BF16),
            pltpu.VMEM((features, total), BF16),
            pltpu.VMEM((features, total), BF16),
            pltpu.VMEM((total, features), BF16),
            pltpu.VMEM((total, hidden_width), BF16),
            pltpu.VMEM((total, hidden_width), BF16),
            pltpu.VMEM((features, columns), F32),
            pltpu.VMEM((columns, features), F32),
            dma((4,)),
            dma((ranks,)),
            dma((ranks,)),
            dma((ranks,)),
            dma((ranks,)),
            dma((ranks,)),
            dma((ranks,)),
            dma((2, tiles)),
            dma((2, tiles)),
            dma((2, tiles)),
            pltpu.SemaphoreType.REGULAR,
        ],
        compiler_params=pltpu.CompilerParams(
            collective_id=1, has_side_effects=True, vmem_limit_bytes=63 * MIB
        ),
        cost_estimate=pl.CostEstimate(
            flops=12 * total * features * hidden_width,
            bytes_accessed=8 * features * hidden_width + 8 * total * features,
            transcendentals=total * hidden_width,
        ),
    )(hidden, cot, w_in, w_out, router_padded)


def tail_kernel(
    q_ref, k_ref, v_ref, kept_ref, wq_ref, wk_ref, wv_ref, tile_ref, gain_ref, bucket_ref,
    drouter_ref, target_ref, gate_ref, normed_hbm, tokens_hbm, cot_hbm, residual_hbm, attended_hbm,
    out_weight_hbm, moved_hbm, made_hbm,
    tokens_grad_ref, dense_ref, early_ref, router_ref, small_ref, output_hbm, came_hbm,
    normed, narrow, attended, out_weight, slots, datt,
    dscores, dnormed, lines, own, core_out, core_in, plane_out, plane_in, layer_out, layer_in,
    early_out, early_core, early_own, early_plane_out, early_plane_in, early_layer_out,
    early_layer_in, small_out, small_in, load_sem, made_sent, made_came, core_sent, core_came,
    plane_sent, plane_came, layer_sent, layer_came, small_sent, small_came, *, rows, ranks, plane,
):
    length, features = narrow.shape
    tiles = length // LANES
    inner = rows // LANES
    layers = ranks // plane
    groups = (pl.num_programs(0) - 2) // 2
    per_slot = slots.shape[0] // ranks
    step = pl.program_id(0)
    core, me = lax.axis_index("group"), lax.axis_index("expert")
    other = 1 - core
    layer, spot = me // plane, me % plane
    mesh = pl.DeviceIdType.MESH

    def in_plane(k, sign):
        return (spot + plane + sign * k) % plane

    def in_line(k, sign):
        return (layer + layers + sign * k) % layers

    def rank_of(a_layer, a_spot):
        return a_layer * plane + a_spot

    def core_copy(unit):
        early = unit == 0
        return pltpu.make_async_remote_copy(
            src_ref=early_out if early else core_out.at[unit - 1],
            dst_ref=early_core if early else core_in.at[unit - 1],
            send_sem=core_sent.at[unit],
            recv_sem=core_came.at[unit],
            device_id=(other, me),
            device_id_type=mesh,
        )

    def plane_copy(unit, k):
        early = unit == 0
        source = early_plane_out if early else plane_out.at[unit - 1]
        return pltpu.make_async_remote_copy(
            src_ref=source.at[:, in_plane(k, 1)],
            dst_ref=early_plane_in.at[k - 1] if early else plane_in.at[unit - 1, k - 1],
            send_sem=plane_sent.at[unit, k],
            recv_sem=plane_came.at[unit, k],
            device_id=(core, rank_of(layer, in_plane(k, 1))),
            device_id_type=mesh,
        )

    def layer_copy(unit, k):
        early = unit == 0
        source = early_layer_out if early else layer_out.at[unit - 1]
        return pltpu.make_async_remote_copy(
            src_ref=source.at[in_line(k, 1)],
            dst_ref=early_layer_in.at[k - 1] if early else layer_in.at[unit - 1, k - 1],
            send_sem=layer_sent.at[unit, k],
            recv_sem=layer_came.at[unit, k],
            device_id=(core, rank_of(in_line(k, 1), spot)),
            device_id_type=mesh,
        )

    def small_copy(number):
        if number == 0:
            there = (other, me)
        elif number < plane:
            there = (core, rank_of(layer, in_plane(number, 1)))
        else:
            there = (core, rank_of(in_line(number - plane + 1, 1), spot))
        return pltpu.make_async_remote_copy(
            src_ref=small_out.at[min(number, 1) + number // plane],
            dst_ref=small_in.at[number],
            send_sem=small_sent.at[number],
            recv_sem=small_came.at[number],
            device_id=there,
            device_id_type=mesh,
        )

    def small_start(stage, first, end):
        for number in range(first, end):
            small_copy(number).start()

    def small_add(stage, first, end):
        total = small_out[stage]
        for number in range(first, end):
            small_copy(number).wait_recv()
            total = total + small_in[number]
        return total

    def partner(number):
        return rank_of(in_line(number // plane, 1), in_plane(number % plane, 1))

    def made_copy(number):
        return pltpu.make_async_remote_copy(
            src_ref=made_hbm.at[partner(number)],
            dst_ref=came_hbm.at[me],
            send_sem=made_sent.at[number],
            recv_sem=made_came.at[number],
            device_id=(core, partner(number)),
            device_id_type=mesh,
        )

    def load(source, target, number):
        return pltpu.make_async_copy(source, target, load_sem.at[number])

    def moved_load(number):
        part = pl.ds(pl.multiple_of(number * per_slot, per_slot), per_slot)
        return pltpu.make_async_copy(moved_hbm.at[number], slots.at[part], load_sem.at[8])

    def came_load(number):
        part = pl.ds(pl.multiple_of(number * per_slot, per_slot), per_slot)
        return pltpu.make_async_copy(came_hbm.at[number], slots.at[part], load_sem.at[9])

    def own_made():
        return load(made_hbm.at[me], came_hbm.at[me], 7)

    def each(first, last, action):
        def run(number, carry):
            action(number)
            return carry

        lax.fori_loop(first, last, run, 0)

    def taken(block):
        total = jnp.zeros((rows, features), F32)
        width = 4 * LANES
        for first in range(0, slots.shape[0], width):
            at = first + lax.broadcasted_iota(jnp.int32, (1, width), 1)
            picks = (target_ref[block, :] == at).astype(F32).astype(BF16)
            total = total + jnp.dot(
                picks, slots[first : first + width, :], preferred_element_type=F32
            )
        return total

    def sum_cores(unit):
        core_copy(unit).wait_recv()
        if unit == 0:
            summed = early_own[...].astype(F32) + early_core[...].astype(F32)
            early_plane_out[...] = summed.astype(BF16).reshape(early_plane_out.shape)
        else:
            summed = own[unit % 2] + core_in[unit - 1].astype(F32)
            plane_out[unit - 1] = summed.astype(BF16).reshape(plane_out.shape[1:])
        for k in range(1, plane):
            plane_copy(unit, k).start()

    def sum_planes(unit):
        summed = (early_plane_out[:, spot] if unit == 0 else plane_out[unit - 1, :, spot]).astype(F32)
        for k in range(1, plane):
            plane_copy(unit, k).wait_recv()
            came = early_plane_in[k - 1] if unit == 0 else plane_in[unit - 1, k - 1]
            summed = summed + came.astype(F32)
        if unit == 0:
            early_layer_out[...] = summed.astype(BF16)
        else:
            layer_out[unit - 1] = summed.astype(BF16)
        for k in range(1, layers):
            layer_copy(unit, k).start()

    def sum_layers(unit):
        summed = (early_layer_out[layer] if unit == 0 else layer_out[unit - 1, layer]).astype(F32)
        for k in range(1, layers):
            layer_copy(unit, k).wait_recv()
            came = early_layer_in[k - 1] if unit == 0 else layer_in[unit - 1, k - 1]
            summed = summed + came.astype(F32)
        if unit == 0:
            early_ref[...] = summed[:, : early_ref.shape[1]]
            router_ref[...] = summed[:, early_ref.shape[1] :]
        else:
            group = unit - 1
            base = core * (groups * LANES)
            keys_at = other * (2 * groups * LANES) + group * LANES
            for part, at in enumerate(
                (base + group * LANES, base + (groups + group) * LANES, keys_at)
            ):
                dense_ref[:, pl.ds(pl.multiple_of(at, LANES), LANES)] = summed[
                    :, part * LANES : (part + 1) * LANES
                ]

    @pl.when(step == 0)
    def _():
        each(0, ranks, lambda number: moved_load(number).start())
        load(residual_hbm, dnormed, 0).start()
        load(cot_hbm, narrow, 1).start()
        load(out_weight_hbm, out_weight, 2).start()
        load(attended_hbm, attended, 3).start()
        load(normed_hbm, normed, 4).start()
        own_made().start()
        barrier = pltpu.get_barrier_semaphore()
        each(
            1,
            ranks,
            lambda number: pl.semaphore_signal(
                barrier, inc=1, device_id=(core, partner(number)), device_id_type=mesh
            ),
        )
        pl.semaphore_signal(barrier, inc=1, device_id=(other, me), device_id_type=mesh)
        pl.semaphore_wait(barrier, ranks)

    middle = min(3 * plane, ranks)
    for now, (first, end) in enumerate(((plane, middle), (middle, ranks), (1, plane))):

        @pl.when(step == now)
        def _(first=first, end=end):
            each(first, end, lambda number: made_copy(number).start())

    @pl.when(step == 0)
    def _():
        each(0, ranks, lambda number: moved_load(number).wait())
        load(residual_hbm, dnormed, 0).wait()
        load(cot_hbm, narrow, 1).wait()
        load(out_weight_hbm, out_weight, 2).wait()

        def branch(number, dgain):
            block = pl.ds(pl.multiple_of(number * rows, rows), rows)
            back = taken(block)
            residual = dnormed[block, :]
            spread = lax.rsqrt(jnp.mean(residual * residual, axis=1, keepdims=True) + EPSILON)
            scaled = residual * spread
            moved = back * gain_ref[1:2, :]
            dres = narrow[block, :].astype(F32) + spread * (
                moved - scaled * jnp.mean(moved * scaled, axis=1, keepdims=True)
            )
            tokens_grad_ref[block, :] = dres
            dbranch = dres.astype(BF16)
            dscores[block, :features] = dbranch
            datt[block, :] = lax.dot_general(
                dbranch, out_weight[...], NT, preferred_element_type=F32
            ).astype(BF16)
            return dgain + jnp.sum(back * scaled, axis=0, keepdims=True)

        dgain = lax.fori_loop(0, length // rows, branch, jnp.zeros((1, features), F32))
        for part in range(features // LANES):
            at = lines.shape[0] + features // LANES + part
            small_out[0, at : at + 1, :] = dgain[:, part * LANES : (part + 1) * LANES]
        load(attended_hbm, attended, 3).wait()
        load(normed_hbm, normed, 4).wait()
        load(tokens_hbm, narrow, 5).start()
        dense = lax.dot_general(
            attended[...], dscores[:, :features], TN, preferred_element_type=F32
        )
        half = features // 2
        early_own[:, :half] = jnp.where(core == 0, dense[:, :half], dense[:, half:]).astype(BF16)
        early_out[:, :half] = jnp.where(core == 0, dense[:, half:], dense[:, :half]).astype(BF16)
        drouter = drouter_ref[...].astype(BF16)
        early_own[:, half:] = drouter
        early_out[:, half:] = drouter
        core_copy(0).start()
        dnormed[...] = jnp.zeros_like(dnormed)

    @pl.when((step > 0) & (step <= 2 * groups))
    def _():
        lane = lax.broadcasted_iota(jnp.int32, (1, LANES), 1)
        pair = (step - 1) % 2 * groups + (step - 1) // 2
        columns = pl.ds(pl.multiple_of(pair * LANES, LANES), LANES)
        queries, values, dout = q_ref[...], v_ref[...], datt[:, columns]
        widened = jnp.concatenate([k_ref[...], tile_ref[...]], axis=1)
        dout_wide = dout.astype(F32)
        product = dout_wide * attended[:, columns].astype(F32)
        dout_turned, queries_turned = dout.T, queries.T
        mirror = (
            lax.broadcasted_iota(jnp.int32, (LANES, LANES), 0)
            + lax.broadcasted_iota(jnp.int32, (LANES, LANES), 1)
            == LANES - 1
        ).astype(F32)
        dqueries = [[], []]
        dkeys, dvalues = [], []
        for head in range(2):
            mine = (lane < HEAD) if head == 0 else (lane >= HEAD)
            inner_sum = jnp.sum(jnp.where(mine, product, 0.0), axis=1, keepdims=True)
            masked = jnp.where(mine, dout_wide, 0.0).astype(BF16)
            bands = [jnp.zeros((LANES, LANES), F32) for _ in range(3)]
            before = jnp.zeros((1, LANES), F32)
            after = jnp.zeros((1, LANES), F32)
            for part_of in range(length // rows):
                first = part_of * rows
                block = pl.ds(first, rows)
                dprob = lax.dot_general(
                    masked[first : first + rows], values, NT, preferred_element_type=F32
                )
                scores = kept_ref[head, block, :].astype(F32) * (
                    dprob - inner_sum[first : first + rows]
                )
                rounded = scores.astype(BF16)
                dscores[block, :] = rounded
                both = jnp.dot(rounded, widened, preferred_element_type=F32)
                dqueries[head].append(both[:, :LANES])
                for part in range(inner):
                    tile = part_of * inner + part
                    here = slice(part * LANES, (part + 1) * LANES)
                    for at in range(3):
                        there = tile - 1 + at
                        if 0 <= there < tiles:
                            bands[at] = bands[at] + scores[here, there * LANES : (there + 1) * LANES]
                    sums = jnp.sum(both[here, LANES:], axis=0, keepdims=True)
                    before = before + jnp.where(lane <= tile - 2, sums, 0.0)
                    after = after + jnp.where((lane >= tile + 2) & (lane < tiles), sums, 0.0)
            band = jnp.concatenate([*bands, jnp.zeros((LANES, LANES), F32)], axis=1)
            band = jnp.dot(
                mirror, band, preferred_element_type=F32, precision=lax.Precision.HIGHEST
            )
            band = pltpu.roll(band, 3 * LANES + 1, 1, stride=1, stride_axis=0)
            near = jnp.sum(band, axis=0, keepdims=True)
            lines[pl.ds(2 * pair + head, 1), :] = jnp.concatenate([near, before, after], axis=1)
            half = slice(HEAD * head, HEAD * head + HEAD)
            dkeys.append(
                jnp.dot(queries_turned[half], dscores[...], preferred_element_type=F32)
            )
            dvalues.append(jnp.dot(dout_turned[half], kept_ref[head], preferred_element_type=F32))
        scale = HEAD**-0.5
        dq = jnp.concatenate(
            [
                (jnp.where(lane < HEAD, left, right) * scale).astype(BF16)
                for left, right in zip(*dqueries, strict=True)
            ],
            axis=0,
        )
        dk = (jnp.concatenate(dkeys, axis=0) * scale).T.astype(BF16)
        dv = jnp.concatenate(dvalues, axis=0).T.astype(BF16)
        joined = jnp.concatenate([dq, dk, dv], axis=1)
        weights = jnp.concatenate([wq_ref[...], wk_ref[...], wv_ref[...]], axis=1)
        dnormed[...] += lax.dot_general(joined, weights, NT, preferred_element_type=F32)
        dense = jnp.dot(normed[...], joined, preferred_element_type=F32)
        dwq, dwk, dwv = dense[:, :LANES], dense[:, LANES : 2 * LANES], dense[:, 2 * LANES :]
        own_first, away_first = jnp.where(core == 0, dwq, dwv), jnp.where(core == 0, dwv, dwq)
        for now in range(2 * groups):

            @pl.when(step == now + 1)
            def _(now=now):
                unit, part = now // 2 + 1, now % 2
                at = slice(part * LANES, (part + 1) * LANES)
                own[unit % 2, :, at] = own_first
                core_out[unit - 1, :, at] = away_first.astype(BF16)

                @pl.when(core == part)
                def _():
                    own[unit % 2, :, 2 * LANES :] = dwk

                @pl.when(core != part)
                def _():
                    core_out[unit - 1, :, 2 * LANES :] = dwk.astype(BF16)

                if part == 1:
                    core_copy(unit).start()

    last = 2 * groups + 1
    plan = {}
    for unit in range(groups + 1):
        plan.setdefault(min(2 * unit + 1, last), []).append((sum_cores, unit))
        plan.setdefault(min(2 * unit + 4, last), []).append((sum_planes, unit))
        plan.setdefault(last, []).append((sum_layers, unit))
    order = [sum_layers, sum_planes, sum_cores]
    for now in range(1, last):

        @pl.when(step == now)
        def _(now=now):
            for action, unit in sorted(plan.get(now, []), key=lambda p: order.index(p[0])):
                action(unit)

    @pl.when(step == last)
    def _():
        todo = plan.get(last, [])
        for action, unit in todo:
            if action is sum_cores:
                action(unit)
        for action, unit in todo:
            if action is sum_planes and unit < groups:
                action(unit)
        load(tokens_hbm, narrow, 5).wait()
        gain = gain_ref[0:1, :]
        inputs = narrow[...].astype(F32)
        spread = lax.rsqrt(jnp.mean(inputs * inputs, axis=1, keepdims=True) + EPSILON)
        back = dnormed[...]
        scaled = inputs * spread
        dgain = jnp.sum(back * scaled, axis=0, keepdims=True)
        moved = back * gain
        tokens_grad_ref[...] = tokens_grad_ref[...] + spread * (
            moved - scaled * jnp.mean(moved * scaled, axis=1, keepdims=True)
        )
        table = jnp.dot(
            lines[...], bucket_ref[...], preferred_element_type=F32, precision=lax.Precision.HIGHEST
        )
        small_out[0, 0 : lines.shape[0], :] = table
        base = lines.shape[0]
        wide = features // LANES
        for part in range(wide):
            small_out[0, base + part : base + part + 1, :] = dgain[
                :, part * LANES : (part + 1) * LANES
            ]
        if small_out.shape[1] > base + 2 * wide:
            small_out[0, base + 2 * wide :, :] = jnp.zeros(
                (small_out.shape[1] - base - 2 * wide, LANES), F32
            )

        small_start(0, 0, 1)
        load(residual_hbm, dnormed, 6).start()
        for action, unit in todo:
            if action is sum_planes and unit == groups:
                action(unit)
        small_out[1] = small_add(0, 0, 1)
        small_start(1, 1, plane)
        own_made().wait()
        each(1, ranks, lambda number: made_copy(number).wait_recv())
        each(0, ranks, lambda number: came_load(number).start())
        each(0, ranks, lambda number: came_load(number).wait())
        load(residual_hbm, dnormed, 6).wait()

        def finish(number, carry):
            block = pl.ds(pl.multiple_of(number * rows, rows), rows)
            datt[block, :] = (dnormed[block, :] + gate_ref[block, :] * taken(block)).astype(BF16)
            return carry

        lax.fori_loop(0, length // rows, finish, 0)
        load(datt, output_hbm, 10).start()
        small_out[2] = small_add(1, 1, plane)
        small_start(2, plane, plane + layers - 1)
        for action, unit in todo:
            if action is sum_layers:
                action(unit)
        small_ref[...] = small_add(2, plane, plane + layers - 1)
        for number in range(plane + layers - 1):
            small_copy(number).wait_send()
        each(1, ranks, lambda number: made_copy(number).wait_send())
        load(datt, output_hbm, 10).wait()
        for unit in range(groups + 1):
            core_copy(unit).wait_send()
            for k in range(1, plane):
                plane_copy(unit, k).wait_send()
            for k in range(1, layers):
                layer_copy(unit, k).wait_send()


def run_tail(
    projected, attended, kept, qkv_weight, out_weight, normed_turned, tokens, cotangent, residual, gains,
    drouter, target, gate, moved, made, rows,
):
    length, features = tokens.shape
    heads = kept.shape[0]
    ranks = made.shape[0]
    pairs = heads // 2
    groups = pairs // 2
    plane = 4
    layers = ranks // plane
    slab = features // ranks
    early = features // 2 + LANES
    late = 3 * LANES
    tile_of = (
        jnp.arange(length)[:, None] // LANES == jnp.arange(LANES)[None, :]
    ).astype(BF16)
    at = jnp.arange(4 * LANES, dtype=jnp.int32)
    relative = jnp.where(at < 3 * LANES, at - LANES, at - 5 * LANES)
    ends = bucket_index(jnp.array([-length, length], jnp.int32))
    bucket = jnp.concatenate([bucket_index(relative), jnp.repeat(ends, LANES)])
    bucket_of = (bucket[:, None] == jnp.arange(LANES)[None, :]).astype(F32)
    line_rows = heads + -heads % 4
    small_rows = line_rows + 2 * (features // LANES)
    small_rows += -small_rows % 8

    def pair_of(i):
        i = jnp.clip(i - 1, 0, pairs - 1)
        return i % 2 * groups + i // 2

    def column(shape, offset):
        return pl.BlockSpec(shape, lambda i: (0, offset + pair_of(i)))

    def whole(shape):
        return pl.BlockSpec(shape, lambda i: (0, 0), pipeline_mode=pl.Buffered(1))

    dma = pltpu.SemaphoreType.DMA
    any_ref = pl.BlockSpec(memory_space=pl.ANY)
    units = groups + 1
    return pl.pallas_call(
        functools.partial(tail_kernel, rows=rows, ranks=ranks, plane=plane),
        grid=(pairs + 2,),
        in_specs=[
            column((length, LANES), 0),
            column((length, LANES), pairs),
            column((length, LANES), 2 * pairs),
            pl.BlockSpec((2, length, length), lambda i: (pair_of(i), 0, 0)),
            column((features, LANES), 0),
            column((features, LANES), pairs),
            column((features, LANES), 2 * pairs),
            whole((length, LANES)),
            whole(gains.shape),
            whole(bucket_of.shape),
            whole((features, LANES)),
            whole((length, 1)),
            whole((length, 1)),
            *[any_ref] * 8,
        ],
        out_specs=[
            whole((length, features)),
            whole((slab, groups * late)),
            whole((slab, features // 2)),
            whole((slab, LANES)),
            whole((small_rows, LANES)),
            any_ref,
            any_ref,
        ],
        out_shape=[
            jax.ShapeDtypeStruct((length, features), F32),
            jax.ShapeDtypeStruct((slab, groups * late), F32),
            jax.ShapeDtypeStruct((slab, features // 2), F32),
            jax.ShapeDtypeStruct((slab, LANES), F32),
            jax.ShapeDtypeStruct((small_rows, LANES), F32),
            jax.ShapeDtypeStruct((length, features), BF16),
            jax.ShapeDtypeStruct(made.shape, BF16),
        ],
        scratch_shapes=[
            pltpu.VMEM((features, length), BF16),
            pltpu.VMEM((length, features), BF16),
            pltpu.VMEM((length, features), BF16),
            pltpu.VMEM((features, features), BF16),
            pltpu.VMEM((ranks * made.shape[1], features), BF16),
            pltpu.VMEM((length, features), BF16),
            pltpu.VMEM((length, length), BF16),
            pltpu.VMEM((length, features), F32),
            pltpu.VMEM((line_rows, 6 * LANES), F32),
            pltpu.VMEM((2, features, late), F32),
            pltpu.VMEM((groups, features, late), BF16),
            pltpu.VMEM((groups, features, late), BF16),
            pltpu.VMEM((groups, layers, plane, slab, late), BF16),
            pltpu.VMEM((groups, plane - 1, layers, slab, late), BF16),
            pltpu.VMEM((groups, layers, slab, late), BF16),
            pltpu.VMEM((groups, layers - 1, slab, late), BF16),
            pltpu.VMEM((features, early), BF16),
            pltpu.VMEM((features, early), BF16),
            pltpu.VMEM((features, early), BF16),
            pltpu.VMEM((layers, plane, slab, early), BF16),
            pltpu.VMEM((plane - 1, layers, slab, early), BF16),
            pltpu.VMEM((layers, slab, early), BF16),
            pltpu.VMEM((layers - 1, slab, early), BF16),
            pltpu.VMEM((3, small_rows, LANES), F32),
            pltpu.VMEM((plane + layers - 1, small_rows, LANES), F32),
            dma((11,)),
            dma((ranks,)),
            dma((ranks,)),
            dma((units,)),
            dma((units,)),
            dma((units, plane)),
            dma((units, plane)),
            dma((units, layers)),
            dma((units, layers)),
            dma((plane + layers - 1,)),
            dma((plane + layers - 1,)),
        ],
        compiler_params=pltpu.CompilerParams(
            collective_id=2, has_side_effects=True, vmem_limit_bytes=62 * MIB
        ),
        cost_estimate=pl.CostEstimate(
            flops=36 * heads * length * length * HEAD,
            bytes_accessed=2 * heads * length * length + 30 * length * features,
            transcendentals=0,
        ),
    )(
        projected, projected, projected, kept, qkv_weight, qkv_weight, qkv_weight, tile_of, gains,
        bucket_of, drouter, target, gate, normed_turned, tokens, cotangent, residual, attended,
        out_weight, moved, made,
    )


def core_sum(values, dim):
    half = values.shape[dim] // 2
    core = lax.axis_index("group")
    own = lax.dynamic_slice_in_dim(values, core * half, half, dim)
    other = lax.dynamic_slice_in_dim(values, (1 - core) * half, half, dim).astype(BF16)
    return own + lax.ppermute(other, "group", [(0, 1), (1, 0)]).astype(F32)


def exchange(values):
    return lax.all_to_all(values, "expert", split_axis=0, concat_axis=0, tiled=True)


def per_device(
    tokens, gains, qkv_weight, out_weight, rel_bias, router_weight, w_in, w_out, routes, factors,
    cotangent,
):
    length, features = tokens.shape
    bucket_count = rel_bias.shape[0]
    expert_count = router_weight.shape[1]
    slot_count = 2 * length // expert_count
    rows = min(256, length)
    gain_rows = gains.astype(F32)
    w_in, w_out = w_in[0], w_out[0]
    me = lax.axis_index("expert")
    core = lax.axis_index("group")

    routed = routes[:, 0]
    row_index = jnp.arange(length, dtype=jnp.int32)
    chosen = routed[:, None] == jnp.arange(expert_count, dtype=jnp.int32)[None, :]
    earlier = (row_index[:, None] > row_index[None, :]).astype(BF16)
    before = jnp.dot(earlier, chosen.astype(BF16), preferred_element_type=F32)
    place = jnp.sum(before * chosen.astype(F32), axis=-1).astype(jnp.int32)
    capacity = factors[0] * (length // expert_count)
    target = jnp.where(place < capacity, routed * slot_count + place, -1)
    slots = jnp.arange(expert_count * slot_count, dtype=jnp.int32)
    picks = (slots[:, None] == target[None, :]).astype(BF16)

    def pack(values):
        packed = jnp.dot(picks, values, preferred_element_type=F32).astype(BF16)
        return packed.reshape(expert_count, slot_count, features)

    def unpack(values):
        return lax.dot_general(
            picks, values.reshape(-1, features), TN, preferred_element_type=F32
        )

    upstream_there = exchange(pack(cotangent))

    inputs = tokens.astype(F32)
    normed_in = norm_rows(inputs, gain_rows[0]).astype(BF16)
    projected = jnp.dot(normed_in, qkv_weight, preferred_element_type=F32).astype(BF16)
    attended, kept = attend(projected, bias_lines(rel_bias, length), rows)
    residual_one = inputs + jnp.dot(attended, out_weight, preferred_element_type=F32)
    hidden = norm_rows(residual_one, gain_rows[1]).astype(BF16)

    logits = jnp.dot(hidden, router_weight, preferred_element_type=F32)
    raised = jnp.exp(logits - jnp.max(logits, axis=-1, keepdims=True))
    router = raised / jnp.sum(raised, axis=-1, keepdims=True)
    gate_value = jnp.sum(router * chosen.astype(F32), axis=-1)

    padded = -expert_count % LANES
    router_padded = jnp.pad(router_weight, ((0, 0), (0, padded)))
    packed, normed_turned = lax.optimization_barrier((pack(hidden), normed_in.T))
    made, dmoved_back, grad_first, grad_second, drouter = run_expert(
        packed, upstream_there, w_in, w_out, router_padded, expert_count
    )
    experts = lax.axis_size("expert")
    cores = lax.axis_size("group")
    slab = features // experts
    gain_at = (core, me * slab)
    router_at = (core * (expert_count // cores),)
    if experts == 16 and cores == 2 and features % (16 * experts) == 0:
        grad_tokens, grad_qkv, grad_out, router_sums, small, output, _ = run_tail(
            projected, attended, kept, qkv_weight, out_weight, normed_turned, tokens, cotangent,
            residual_one, gain_rows, drouter, target[:, None], gate_value[:, None], dmoved_back, made,
            rows,
        )
        heads = rel_bias.shape[1]
        gain_sums = small[heads + -heads % 4 :][: 2 * features // LANES].reshape(2, features)
        return (
            output,
            grad_tokens,
            lax.dynamic_slice(gain_sums, gain_at, (2 // cores, slab)),
            grad_qkv,
            grad_out,
            small[:heads, :bucket_count].T,
            lax.dynamic_slice(router_sums, (0, *router_at), (slab, expert_count // cores)),
            grad_first[None],
            grad_second[None],
        )

    made_back = exchange(made)
    grad_router = drouter[:, :expert_count]

    dhidden = unpack(dmoved_back)
    upstream = cotangent.astype(F32)
    _, back_two = jax.vjp(norm_rows, residual_one, gain_rows[1])
    dres_norm, dgain_two = back_two(dhidden)
    dres = upstream + dres_norm
    dbranch = dres.astype(BF16)
    datt = lax.dot_general(dbranch, out_weight, NT, preferred_element_type=F32).astype(BF16)
    grad_out = lax.dot_general(attended, dbranch, TN, preferred_element_type=F32)
    dqkv, band, far = attend_back(projected, attended, datt, kept, rows)
    grad_proj = jnp.einsum("td,cte->dce", normed_in, dqkv, preferred_element_type=F32)
    grad_proj = grad_proj.reshape(features, 3 * features)
    dnormed = jnp.einsum(
        "cte,dce->td",
        dqkv,
        qkv_weight.reshape(features, 3, features),
        preferred_element_type=F32,
    )
    _, back_one = jax.vjp(norm_rows, inputs, gain_rows[0])
    dinput_norm, dgain_one = back_one(dnormed)
    grad_tokens = dres + dinput_norm

    brought = unpack(made_back)
    output = (residual_one + gate_value[:, None] * brought).astype(BF16)

    def scattered(values):
        return lax.psum_scatter(
            core_sum(values, 1).astype(BF16), "expert", scatter_dimension=0, tiled=True
        ).astype(F32)

    small = [
        jnp.stack([dgain_one, dgain_two], axis=0),
        grad_router,
        table_gradient(band, far, bucket_count),
    ]
    flat = lax.psum(jnp.concatenate([s.reshape(-1) for s in small]), ("group", "expert"))
    summed = []
    at = 0
    for s in small:
        summed.append(flat[at : at + s.size].reshape(s.shape))
        at += s.size
    grad_gains = lax.dynamic_slice(summed[0], gain_at, (2 // cores, slab))
    grad_router = lax.dynamic_slice(
        summed[1], (me * slab, *router_at), (slab, expert_count // cores)
    )
    return (
        output,
        grad_tokens,
        grad_gains,
        scattered(grad_proj),
        scattered(grad_out),
        summed[2],
        grad_router,
        grad_first[None],
        grad_second[None],
    )


def solution(mesh):
    return jax.shard_map(
        per_device,
        mesh=mesh,
        in_specs=(
            P(("group", "expert"), None),
            P(),
            P(),
            P(),
            P(),
            P(),
            P("expert", None, None),
            P("expert", None, None),
            P(("group", "expert"), None),
            P(("group", "expert")),
            P(("group", "expert"), None),
        ),
        out_specs=(
            P(("group", "expert"), None),
            P(("group", "expert"), None),
            P("group", "expert"),
            P("expert", "group"),
            P("expert", "group"),
            P(),
            P("expert", "group"),
            P("expert", None, "group"),
            P("expert", "group", None),
        ),
        check_vma=False,
    )
```

```python
import functools

import jax
import jax.numpy as jnp
from jax import lax
from jax.experimental import pallas as pl
from jax.experimental.pallas import tpu as pltpu
from jax.sharding import PartitionSpec as P

EPSILON = 1e-06
BOUNDARIES = (12, 16, 23, 32, 46, 64, 91)
F32 = jnp.float32
BF16 = jnp.bfloat16
LANES = 128
HEAD = 64
NT = (((1,), (1,)), ((), ()))
TN = (((0,), (0,)), ((), ()))
MIB = 2**20


def bucket_index(relative):
    distance = jnp.abs(relative)
    farther = jnp.full(relative.shape, 8, jnp.int32)
    for boundary in BOUNDARIES:
        farther = farther + (distance >= boundary).astype(jnp.int32)
    nearest = jnp.where(distance < 8, distance, farther)
    return nearest + 16 * (relative > 0).astype(jnp.int32)


def norm_rows(values, gain_row):
    return (
        values * lax.rsqrt(jnp.mean(values * values, axis=-1, keepdims=True) + EPSILON) * gain_row
    )


def attend_kernel(q_ref, k_ref, v_ref, line_ref, out_ref, kept_ref, slab_ref, *, rows):
    length = q_ref.shape[0]
    lane = lax.broadcasted_iota(jnp.int32, (1, LANES), 1)
    keys, values = k_ref[...], v_ref[...]
    for head in range(2):
        line = jnp.broadcast_to(line_ref[head], (rows, 2 * length))
        slab_ref[head] = pltpu.roll(line, 0, 1, stride=1, stride_axis=0)
    for step in range(length // rows):
        block = pl.ds(step * rows, rows)
        queries = q_ref[block, :].astype(F32) * HEAD**-0.5
        joined = []
        for head in range(2):
            mine = (lane < HEAD) if head == 0 else (lane >= HEAD)
            own = jnp.where(mine, queries, 0.0).astype(BF16)
            scores = lax.dot_general(own, keys, NT, preferred_element_type=F32)
            scores = scores + slab_ref[head, :, pl.ds(length - rows * step, length)]
            top = jnp.max(scores, axis=1, keepdims=True)
            raised = jnp.exp(scores - top)
            total = jnp.sum(raised, axis=1, keepdims=True)
            weights = (raised * (1.0 / total)).astype(BF16)
            kept_ref[head, block, :] = weights
            joined.append(jnp.dot(weights, values, preferred_element_type=F32))
        out_ref[block, :] = jnp.where(lane < HEAD, joined[0], joined[1]).astype(BF16)


def attend(projected, lines, rows):
    length, features = projected.shape[0], projected.shape[1] // 3
    heads = lines.shape[0]
    pairs = heads // 2
    return pl.pallas_call(
        functools.partial(attend_kernel, rows=rows),
        grid=(pairs,),
        in_specs=[
            pl.BlockSpec((length, LANES), lambda i: (0, i)),
            pl.BlockSpec((length, LANES), lambda i: (0, pairs + i)),
            pl.BlockSpec((length, LANES), lambda i: (0, 2 * pairs + i)),
            pl.BlockSpec((2, 1, 2 * length), lambda i: (i, 0, 0)),
        ],
        out_specs=[
            pl.BlockSpec((length, LANES), lambda i: (0, i)),
            pl.BlockSpec((2, length, length), lambda i: (i, 0, 0)),
        ],
        out_shape=[
            jax.ShapeDtypeStruct((length, features), BF16),
            jax.ShapeDtypeStruct((heads, length, length), BF16),
        ],
        scratch_shapes=[pltpu.VMEM((2, rows, 2 * length), F32)],
        compiler_params=pltpu.CompilerParams(vmem_limit_bytes=50 * MIB),
        cost_estimate=pl.CostEstimate(
            flops=16 * heads * length * length * HEAD,
            bytes_accessed=2 * heads * length * length + 8 * length * features,
            transcendentals=heads * length * length,
        ),
    )(projected, projected, projected, lines)


def attend_back_kernel(
    q_ref, k_ref, v_ref, out_ref, dout_ref, kept_ref, tile_ref,
    grad_ref, band_ref, far_ref, dscores_ref, *, rows,
):
    length = q_ref.shape[0]
    tiles = length // LANES
    inner = rows // LANES
    lane = lax.broadcasted_iota(jnp.int32, (1, LANES), 1)
    queries, values, dout = q_ref[...], v_ref[...], dout_ref[...]
    widened = jnp.concatenate([k_ref[...], tile_ref[...]], axis=1)
    dout_wide = dout.astype(F32)
    product = dout_wide * out_ref[...].astype(F32)
    dout_turned, queries_turned = dout.T, queries.T
    dqueries = [[], []]
    dkeys, dvalues = [], []
    for head in range(2):
        mine = (lane < HEAD) if head == 0 else (lane >= HEAD)
        inner_sum = jnp.sum(jnp.where(mine, product, 0.0), axis=1, keepdims=True)
        own = jnp.where(mine, dout_wide, 0.0).astype(BF16)
        band_ref[head] = jnp.zeros_like(band_ref[head])
        for step in range(length // rows):
            first = step * rows
            block = pl.ds(first, rows)
            dprob = lax.dot_general(
                own[first : first + rows], values, NT, preferred_element_type=F32
            )
            dscores = kept_ref[head, block, :].astype(F32) * (
                dprob - inner_sum[first : first + rows]
            )
            rounded = dscores.astype(BF16)
            dscores_ref[block, :] = rounded
            for part in range(inner):
                tile = step * inner + part
                low, high = max(tile - 1, 0), min(tile + 2, tiles)
                at = low - (tile - 1)
                band_ref[head, :, at * LANES : (at + high - low) * LANES] += dscores[
                    part * LANES : (part + 1) * LANES, low * LANES : high * LANES
                ]
            both = jnp.dot(rounded, widened, preferred_element_type=F32)
            dqueries[head].append(both[:, :LANES])
            for part in range(inner):
                far_ref[head, step * inner + part] = jnp.sum(
                    both[part * LANES : (part + 1) * LANES, LANES:], axis=0
                )
        half = slice(HEAD * head, HEAD * head + HEAD)
        dkeys.append(jnp.dot(queries_turned[half], dscores_ref[...], preferred_element_type=F32))
        dvalues.append(jnp.dot(dout_turned[half], kept_ref[head], preferred_element_type=F32))
    scale = HEAD**-0.5
    for step in range(length // rows):
        grad_ref[0, pl.ds(step * rows, rows), :] = (
            jnp.where(lane < HEAD, dqueries[0][step], dqueries[1][step]) * scale
        ).astype(BF16)
    grad_ref[1] = (jnp.concatenate(dkeys, axis=0) * scale).T.astype(BF16)
    grad_ref[2] = jnp.concatenate(dvalues, axis=0).T.astype(BF16)


def attend_back(projected, attended, datt, kept, rows):
    length, features = projected.shape[0], projected.shape[1] // 3
    heads = kept.shape[0]
    pairs = heads // 2
    tiles = length // LANES
    tile_of = (
        jnp.arange(length)[:, None] // LANES == jnp.arange(LANES)[None, :]
    ).astype(BF16)
    return pl.pallas_call(
        functools.partial(attend_back_kernel, rows=rows),
        grid=(pairs,),
        in_specs=[
            pl.BlockSpec((length, LANES), lambda i: (0, i)),
            pl.BlockSpec((length, LANES), lambda i: (0, pairs + i)),
            pl.BlockSpec((length, LANES), lambda i: (0, 2 * pairs + i)),
            pl.BlockSpec((length, LANES), lambda i: (0, i)),
            pl.BlockSpec((length, LANES), lambda i: (0, i)),
            pl.BlockSpec((2, length, length), lambda i: (i, 0, 0)),
            pl.BlockSpec((length, LANES), lambda i: (0, 0)),
        ],
        out_specs=[
            pl.BlockSpec((3, length, LANES), lambda i: (0, 0, i)),
            pl.BlockSpec((2, LANES, 3 * LANES), lambda i: (i, 0, 0)),
            pl.BlockSpec((2, tiles, LANES), lambda i: (i, 0, 0)),
        ],
        out_shape=[
            jax.ShapeDtypeStruct((3, length, features), BF16),
            jax.ShapeDtypeStruct((heads, LANES, 3 * LANES), F32),
            jax.ShapeDtypeStruct((heads, tiles, LANES), F32),
        ],
        scratch_shapes=[pltpu.VMEM((length, length), BF16)],
        compiler_params=pltpu.CompilerParams(vmem_limit_bytes=56 * MIB),
        cost_estimate=pl.CostEstimate(
            flops=32 * heads * length * length * HEAD,
            bytes_accessed=2 * heads * length * length + 18 * length * features,
            transcendentals=0,
        ),
    )(projected, projected, projected, attended, datt, kept, tile_of)


def bias_lines(rel_bias, length):
    relative = jnp.arange(2 * length, dtype=jnp.int32) - length
    onehot = (
        bucket_index(relative)[None, :]
        == jnp.arange(rel_bias.shape[0], dtype=jnp.int32)[:, None]
    ).astype(F32)
    return jnp.einsum(
        "ch,cr->hr", rel_bias.astype(F32), onehot, precision=lax.Precision.HIGHEST
    )[:, None, :]


def table_gradient(band, far, bucket_count):
    heads, tiles = far.shape[0], far.shape[1]
    relative = jnp.arange(3 * LANES)[None, :] - LANES - jnp.arange(LANES)[:, None]
    onehot = (bucket_index(relative)[:, :, None] == jnp.arange(bucket_count)).astype(F32)
    near = jnp.dot(
        band.reshape(heads, -1),
        onehot.reshape(-1, bucket_count),
        precision=lax.Precision.HIGHEST,
    )
    here = jnp.arange(tiles)[:, None]
    there = jnp.arange(LANES)[None, :]
    before = jnp.sum(jnp.where(there <= here - 2, far, 0.0), axis=(1, 2))
    after = jnp.sum(jnp.where(there >= here + 2, far, 0.0), axis=(1, 2))
    buckets = jnp.arange(bucket_count)
    last = bucket_index(jnp.array([-length_far(), length_far()], jnp.int32))
    return (
        near
        + before[:, None] * (buckets == last[0])
        + after[:, None] * (buckets == last[1])
    ).T


def length_far():
    return LANES


def turned(me, k, ranks, plane, sign):
    if plane == 1:
        return (me + ranks + sign * k) % ranks
    layer, side = me // plane, me % plane
    far, near = k // plane, k % plane
    if ranks // plane % 4:
        layers = ranks // plane
        to_layer = (layer + layers + sign * far) % layers
    else:
        sets = ranks // plane // 4
        low = (layer % 4 // 2 + far % 4 // 2) % 2 * 2 + (layer + far) % 2
        to_layer = (layer // 4 + sets + sign * (far // 4)) % sets * 4 + low
    to_side = (side // 2 + near // 2) % 2 * 2 + (side + near) % 2
    return to_layer * plane + to_side


def expert_kernel(
    hidden_ref, cot_ref, w_in_ref, w_out_ref, router_ref,
    made_ref, back_ref, first_ref, second_ref, drouter_ref,
    w_in, w_out, x, c, x_turned, dexp_turned, moved, act, dpre, stage_first, stage_second, load_sem, cot_sem, out_sem, sent, came, moved_sent, moved_came, core_sent,
    core_came, stage_sem, core_ready, *, ranks, expert_count, rows, width, columns,
):
    features = x.shape[1]
    slots = x.shape[0] // ranks
    hidden_width = w_in.shape[1]
    half = hidden_width // 2
    per_step = rows // slots
    core, me = lax.axis_index("group"), lax.axis_index("expert")
    plane = 4 if ranks % 4 == 0 else 1

    def partner(k, sign):
        return turned(me, k, ranks, plane, sign)

    def span(k):
        return pl.ds(pl.multiple_of(k * slots, slots), slots)

    barrier = pltpu.get_barrier_semaphore()

    def greet(k, carry):
        pl.semaphore_signal(
            barrier, inc=1, device_id=(core, partner(k, 1)), device_id_type=pl.DeviceIdType.MESH
        )
        return carry

    lax.fori_loop(1, ranks, greet, 0)
    pl.semaphore_signal(
        barrier, inc=1, device_id=(1 - core, me), device_id_type=pl.DeviceIdType.MESH
    )

    loads = [
        pltpu.make_async_copy(w_in_ref, w_in, load_sem.at[0]),
        pltpu.make_async_copy(w_out_ref, w_out, load_sem.at[1]),
        pltpu.make_async_copy(hidden_ref.at[me], x.at[pl.ds(0, slots)], load_sem.at[2]),
    ]
    for load in loads:
        load.start()

    def cot_copy(k):
        return pltpu.make_async_copy(cot_ref.at[partner(k, -1)], c.at[span(k)], cot_sem.at[k])

    def load_cot(k, carry):
        cot_copy(k).start()
        return carry

    lax.fori_loop(0, ranks, load_cot, 0)
    pl.semaphore_wait(barrier, ranks)

    def hidden_copy(k):
        return pltpu.make_async_remote_copy(
            src_ref=hidden_ref.at[partner(k, 1)],
            dst_ref=x.at[span(k)],
            send_sem=sent.at[k],
            recv_sem=came.at[k],
            device_id=(core, partner(k, 1)),
            device_id_type=pl.DeviceIdType.MESH,
        )

    def moved_copy(k):
        return pltpu.make_async_remote_copy(
            src_ref=moved.at[span(k)],
            dst_ref=back_ref.at[me],
            send_sem=moved_sent.at[k],
            recv_sem=moved_came.at[k],
            device_id=(core, partner(k, -1)),
            device_id_type=pl.DeviceIdType.MESH,
        )

    def own_moved_copy():
        return pltpu.make_async_copy(moved.at[pl.ds(0, slots)], back_ref.at[me], load_sem.at[3])

    def made_copy(k):
        return pltpu.make_async_copy(c.at[span(k)], made_ref.at[partner(k, -1)], out_sem.at[k])

    def start_hidden(k, carry):
        hidden_copy(k).start()
        return carry

    lax.fori_loop(1, ranks, start_hidden, 0)
    for load in loads:
        load.wait()
    drouter_ref[...] = jnp.zeros_like(drouter_ref)
    root = (2.0 / jnp.pi) ** 0.5

    def run(first_rank):
        block = pl.ds(pl.multiple_of(first_rank * slots, rows), rows)
        xs = x[block, :]
        upstream = c[block, :].astype(F32)
        router_weight = router_ref[...]
        lane = lax.broadcasted_iota(jnp.int32, (1, router_weight.shape[1]), 1)
        logits = jnp.dot(xs, router_weight, preferred_element_type=F32)
        logits = jnp.where(lane < expert_count, logits, -jnp.inf)
        raised = jnp.exp(logits - jnp.max(logits, axis=-1, keepdims=True))
        router = raised / jnp.sum(raised, axis=-1, keepdims=True)
        chosen = (lane == me).astype(F32)
        gate = jnp.sum(router * chosen, axis=-1, keepdims=True)
        dexp = (gate * upstream).astype(BF16)
        made = jnp.zeros((rows, features), F32)
        dmoved = jnp.zeros((rows, features), F32)
        for at in range(0, hidden_width, width):
            part = slice(at, at + width)
            pre = jnp.dot(xs, w_in[:, part], preferred_element_type=F32)
            square = pre * pre
            turned = jnp.tanh(pre * (root + (root * 0.044715) * square))
            upper = 0.5 + 0.5 * turned
            active = (pre * upper).astype(BF16)
            slope = upper + pre * (upper * (1.0 - turned)) * (
                root + (3 * root * 0.044715) * square
            )
            act[block, part] = active
            made = made + jnp.dot(active, w_out[part, :], preferred_element_type=F32)
            dact = lax.dot_general(dexp, w_out[part, :], NT, preferred_element_type=F32)
            dpart = (dact * slope).astype(BF16)
            dpre[block, part] = dpart
            dmoved = dmoved + lax.dot_general(
                dpart, w_in[:, part], NT, preferred_element_type=F32
            )
        made = made.astype(BF16)
        c[block, :] = made
        dgate = jnp.sum(upstream * made.astype(F32), axis=-1, keepdims=True)
        dlogits = (dgate * gate * (chosen - router)).astype(BF16)
        dmoved = dmoved + lax.dot_general(dlogits, router_weight, NT, preferred_element_type=F32)
        moved[block, :] = dmoved.astype(BF16)
        xt = xs.T
        x_turned[:, block] = xt
        dexp_turned[:, block] = dexp.T
        drouter_ref[...] += jnp.dot(xt, dlogits, preferred_element_type=F32)

    last = ranks // per_step - 1

    def step(number, carry):
        first_rank = number * per_step
        for inner in range(per_step):
            k = first_rank + inner
            cot_copy(k).wait()

            @pl.when(k > 0)
            def _(k=k):
                hidden_copy(k).wait_recv()

        @pl.when(number == last)
        def _():
            def start_moved(k, carry):
                moved_copy(k).start()
                return carry

            lax.fori_loop(plane, first_rank, start_moved, 0)

        run(first_rank)
        for inner in range(per_step):
            k = first_rank + inner
            made_copy(k).start()

            @pl.when((k > 0) & ((k < plane) | (number == last)))
            def _(k=k):
                moved_copy(k).start()

        @pl.when(number == 0)
        def _():
            own_moved_copy().start()

        return carry

    lax.fori_loop(0, ranks // per_step, step, 0)

    other = 1 - core
    across = features // columns

    def landed_first(n):
        return pl.ds(n // across * features, features), pl.ds(n % across * columns, columns)

    def first_copy(n):
        part = pl.ds(n * columns, columns)
        return pltpu.make_async_remote_copy(
            src_ref=w_in.at[:, part],
            dst_ref=c.at[landed_first(n)],
            send_sem=core_sent.at[0, n],
            recv_sem=core_came.at[0, n],
            device_id=(other, me),
            device_id_type=pl.DeviceIdType.MESH,
        )

    def second_copy(n):
        part = pl.ds(n * columns, columns)
        return pltpu.make_async_remote_copy(
            src_ref=w_out.at[part],
            dst_ref=x.at[part],
            send_sem=core_sent.at[1, n],
            recv_sem=core_came.at[1, n],
            device_id=(other, me),
            device_id_type=pl.DeviceIdType.MESH,
        )

    def product(turned, wide, part):
        return jnp.dot(turned[...], wide[:, part], preferred_element_type=F32)

    def made_out(k, carry):
        made_copy(k).wait()
        return carry

    lax.fori_loop(0, ranks, made_out, 0)
    pl.semaphore_signal(
        core_ready, inc=1, device_id=(other, me), device_id_type=pl.DeviceIdType.MESH
    )
    tiles = half // columns
    for n in range(tiles):
        part = pl.ds(pl.multiple_of(other * half + n * columns, columns), columns)
        w_in[:, n * columns : (n + 1) * columns] = product(x_turned, dpre, part).astype(BF16)
        if n == 0:
            pl.semaphore_wait(core_ready, 1)
        first_copy(n).start()
        w_out[n * columns : (n + 1) * columns, :] = product(dexp_turned, act, part).T.astype(BF16)
        second_copy(n).start()
    stores = []
    for n in range(tiles):
        part = pl.ds(pl.multiple_of(core * half + n * columns, columns), columns)
        here = slice(n * columns, (n + 1) * columns)
        own = product(x_turned, dpre, part)
        first_copy(n).wait_recv()
        if n:
            stores[2 * n - 2].wait()
        stage_first[...] = own + c[landed_first(n)].astype(F32)
        stores.append(
            pltpu.make_async_copy(
                stage_first, first_ref.at[:, pl.ds(n * columns, columns)],
                stage_sem.at[0, n],
            )
        )
        stores[-1].start()
        own = product(dexp_turned, act, part).T
        second_copy(n).wait_recv()
        if n:
            stores[2 * n - 1].wait()
        stage_second[...] = own + x[here, :].astype(F32)
        stores.append(
            pltpu.make_async_copy(
                stage_second, second_ref.at[pl.ds(n * columns, columns)],
                stage_sem.at[1, n],
            )
        )
        stores[-1].start()
    for store in stores[-2:]:
        store.wait()
    for n in range(tiles):
        first_copy(n).wait_send()
        second_copy(n).wait_send()

    def finish(k, carry):
        @pl.when(k > 0)
        def _():
            hidden_copy(k).wait_send()
            moved_copy(k).wait_send()
            moved_copy(k).wait_recv()

        return carry

    lax.fori_loop(0, ranks, finish, 0)
    own_moved_copy().wait()


def run_expert(hidden, cot, w_in, w_out, router_padded, expert_count):
    ranks, slots, features = hidden.shape
    hidden_width = w_in.shape[1]
    rows = max(min(256, ranks * slots), slots)
    total = ranks * slots
    padded = router_padded.shape[1]
    half = hidden_width // 2
    columns = min(256, half)
    tiles = half // columns
    any_ref = pl.BlockSpec(memory_space=pl.ANY)
    vmem = pl.BlockSpec(memory_space=pltpu.VMEM)
    dma = pltpu.SemaphoreType.DMA
    return pl.pallas_call(
        functools.partial(
            expert_kernel,
            ranks=ranks,
            expert_count=expert_count,
            rows=rows,
            width=min(512, hidden_width),
            columns=columns,
        ),
        in_specs=[any_ref, any_ref, any_ref, any_ref, vmem],
        out_specs=[any_ref, any_ref, any_ref, any_ref, vmem],
        out_shape=[
            jax.ShapeDtypeStruct((ranks, slots, features), BF16),
            jax.ShapeDtypeStruct((ranks, slots, features), BF16),
            jax.ShapeDtypeStruct((features, half), F32),
            jax.ShapeDtypeStruct((half, features), F32),
            jax.ShapeDtypeStruct((features, padded), F32),
        ],
        scratch_shapes=[
            pltpu.VMEM((features, hidden_width), BF16),
            pltpu.VMEM((hidden_width, features), BF16),
            pltpu.VMEM((total, features), BF16),
            pltpu.VMEM((total, features), BF16),
            pltpu.VMEM((features, total), BF16),
            pltpu.VMEM((features, total), BF16),
            pltpu.VMEM((total, features), BF16),
            pltpu.VMEM((total, hidden_width), BF16),
            pltpu.VMEM((total, hidden_width), BF16),
            pltpu.VMEM((features, columns), F32),
            pltpu.VMEM((columns, features), F32),
            dma((4,)),
            dma((ranks,)),
            dma((ranks,)),
            dma((ranks,)),
            dma((ranks,)),
            dma((ranks,)),
            dma((ranks,)),
            dma((2, tiles)),
            dma((2, tiles)),
            dma((2, tiles)),
            pltpu.SemaphoreType.REGULAR,
        ],
        compiler_params=pltpu.CompilerParams(
            collective_id=1, has_side_effects=True, vmem_limit_bytes=63 * MIB
        ),
        cost_estimate=pl.CostEstimate(
            flops=12 * total * features * hidden_width,
            bytes_accessed=8 * features * hidden_width + 8 * total * features,
            transcendentals=total * hidden_width,
        ),
    )(hidden, cot, w_in, w_out, router_padded)


def tail_kernel(
    q_ref, k_ref, v_ref, kept_ref, wq_ref, wk_ref, wv_ref, tile_ref, gain_ref, bucket_ref,
    drouter_ref, target_ref, gate_ref, normed_hbm, tokens_hbm, cot_hbm, residual_hbm, attended_hbm,
    out_weight_hbm, moved_hbm, made_hbm,
    tokens_grad_ref, dense_ref, early_ref, router_ref, small_ref, output_hbm, came_hbm,
    normed, narrow, attended, out_weight, slots, datt,
    dscores, dnormed, lines, own, core_out, core_in, plane_out, plane_in, layer_out, layer_in,
    early_out, early_core, early_own, early_plane_out, early_plane_in, early_layer_out,
    early_layer_in, small_out, small_in, load_sem, made_sent, made_came, core_sent, core_came,
    plane_sent, plane_came, layer_sent, layer_came, small_sent, small_came, *, rows, ranks, plane,
):
    length, features = narrow.shape
    tiles = length // LANES
    inner = rows // LANES
    layers = ranks // plane
    groups = (pl.num_programs(0) - 2) // 2
    per_slot = slots.shape[0] // ranks
    step = pl.program_id(0)
    core, me = lax.axis_index("group"), lax.axis_index("expert")
    other = 1 - core
    layer, spot = me // plane, me % plane
    mesh = pl.DeviceIdType.MESH

    def in_plane(k, sign):
        return (spot + plane + sign * k) % plane

    def in_line(k, sign):
        return (layer + layers + sign * k) % layers

    def rank_of(a_layer, a_spot):
        return a_layer * plane + a_spot

    def core_copy(unit):
        early = unit == 0
        return pltpu.make_async_remote_copy(
            src_ref=early_out if early else core_out.at[unit - 1],
            dst_ref=early_core if early else core_in.at[unit - 1],
            send_sem=core_sent.at[unit],
            recv_sem=core_came.at[unit],
            device_id=(other, me),
            device_id_type=mesh,
        )

    def plane_copy(unit, k):
        early = unit == 0
        source = early_plane_out if early else plane_out.at[unit - 1]
        return pltpu.make_async_remote_copy(
            src_ref=source.at[:, in_plane(k, 1)],
            dst_ref=early_plane_in.at[k - 1] if early else plane_in.at[unit - 1, k - 1],
            send_sem=plane_sent.at[unit, k],
            recv_sem=plane_came.at[unit, k],
            device_id=(core, rank_of(layer, in_plane(k, 1))),
            device_id_type=mesh,
        )

    def layer_copy(unit, k):
        early = unit == 0
        source = early_layer_out if early else layer_out.at[unit - 1]
        return pltpu.make_async_remote_copy(
            src_ref=source.at[in_line(k, 1)],
            dst_ref=early_layer_in.at[k - 1] if early else layer_in.at[unit - 1, k - 1],
            send_sem=layer_sent.at[unit, k],
            recv_sem=layer_came.at[unit, k],
            device_id=(core, rank_of(in_line(k, 1), spot)),
            device_id_type=mesh,
        )

    def small_copy(number):
        if number == 0:
            there = (other, me)
        elif number < plane:
            there = (core, rank_of(layer, in_plane(number, 1)))
        else:
            there = (core, rank_of(in_line(number - plane + 1, 1), spot))
        return pltpu.make_async_remote_copy(
            src_ref=small_out.at[min(number, 1) + number // plane],
            dst_ref=small_in.at[number],
            send_sem=small_sent.at[number],
            recv_sem=small_came.at[number],
            device_id=there,
            device_id_type=mesh,
        )

    def small_start(stage, first, end):
        for number in range(first, end):
            small_copy(number).start()

    def small_add(stage, first, end):
        total = small_out[stage]
        for number in range(first, end):
            small_copy(number).wait_recv()
            total = total + small_in[number]
        return total

    def partner(number):
        return turned(me, number, ranks, plane, 1)

    def made_copy(number):
        return pltpu.make_async_remote_copy(
            src_ref=made_hbm.at[partner(number)],
            dst_ref=came_hbm.at[me],
            send_sem=made_sent.at[number],
            recv_sem=made_came.at[number],
            device_id=(core, partner(number)),
            device_id_type=mesh,
        )

    def load(source, target, number):
        return pltpu.make_async_copy(source, target, load_sem.at[number])

    def moved_load(number):
        part = pl.ds(pl.multiple_of(number * per_slot, per_slot), per_slot)
        return pltpu.make_async_copy(moved_hbm.at[number], slots.at[part], load_sem.at[8])

    def came_load(number):
        part = pl.ds(pl.multiple_of(number * per_slot, per_slot), per_slot)
        return pltpu.make_async_copy(came_hbm.at[number], slots.at[part], load_sem.at[9])

    def own_made():
        return load(made_hbm.at[me], came_hbm.at[me], 7)

    def each(first, last, action):
        def run(number, carry):
            action(number)
            return carry

        lax.fori_loop(first, last, run, 0)

    def taken(block):
        total = jnp.zeros((rows, features), F32)
        width = 4 * LANES
        for first in range(0, slots.shape[0], width):
            at = first + lax.broadcasted_iota(jnp.int32, (1, width), 1)
            picks = (target_ref[block, :] == at).astype(F32).astype(BF16)
            total = total + jnp.dot(
                picks, slots[first : first + width, :], preferred_element_type=F32
            )
        return total

    def sum_cores(unit):
        core_copy(unit).wait_recv()
        if unit == 0:
            summed = early_own[...].astype(F32) + early_core[...].astype(F32)
            early_plane_out[...] = summed.astype(BF16).reshape(early_plane_out.shape)
        else:
            summed = own[unit % 2] + core_in[unit - 1].astype(F32)
            plane_out[unit - 1] = summed.astype(BF16).reshape(plane_out.shape[1:])
        for k in range(1, plane):
            plane_copy(unit, k).start()

    def sum_planes(unit):
        summed = (early_plane_out[:, spot] if unit == 0 else plane_out[unit - 1, :, spot]).astype(F32)
        for k in range(1, plane):
            plane_copy(unit, k).wait_recv()
            came = early_plane_in[k - 1] if unit == 0 else plane_in[unit - 1, k - 1]
            summed = summed + came.astype(F32)
        if unit == 0:
            early_layer_out[...] = summed.astype(BF16)
        else:
            layer_out[unit - 1] = summed.astype(BF16)
        for k in range(1, layers):
            layer_copy(unit, k).start()

    def sum_layers(unit):
        summed = (early_layer_out[layer] if unit == 0 else layer_out[unit - 1, layer]).astype(F32)
        for k in range(1, layers):
            layer_copy(unit, k).wait_recv()
            came = early_layer_in[k - 1] if unit == 0 else layer_in[unit - 1, k - 1]
            summed = summed + came.astype(F32)
        if unit == 0:
            early_ref[...] = summed[:, : early_ref.shape[1]]
            router_ref[...] = summed[:, early_ref.shape[1] :]
        else:
            group = unit - 1
            base = core * (groups * LANES)
            keys_at = other * (2 * groups * LANES) + group * LANES
            for part, at in enumerate(
                (base + group * LANES, base + (groups + group) * LANES, keys_at)
            ):
                dense_ref[:, pl.ds(pl.multiple_of(at, LANES), LANES)] = summed[
                    :, part * LANES : (part + 1) * LANES
                ]

    @pl.when(step == 0)
    def _():
        each(0, ranks, lambda number: moved_load(number).start())
        load(residual_hbm, dnormed, 0).start()
        load(cot_hbm, narrow, 1).start()
        load(out_weight_hbm, out_weight, 2).start()
        load(attended_hbm, attended, 3).start()
        load(normed_hbm, normed, 4).start()
        own_made().start()
        barrier = pltpu.get_barrier_semaphore()
        each(
            1,
            ranks,
            lambda number: pl.semaphore_signal(
                barrier, inc=1, device_id=(core, partner(number)), device_id_type=mesh
            ),
        )
        pl.semaphore_signal(barrier, inc=1, device_id=(other, me), device_id_type=mesh)
        pl.semaphore_wait(barrier, ranks)

    middle = min(3 * plane, ranks)
    for now, (first, end) in enumerate(((plane, middle), (middle, ranks), (1, plane))):

        @pl.when(step == now)
        def _(first=first, end=end):
            each(first, end, lambda number: made_copy(number).start())

    @pl.when(step == 0)
    def _():
        each(0, ranks, lambda number: moved_load(number).wait())
        load(residual_hbm, dnormed, 0).wait()
        load(cot_hbm, narrow, 1).wait()
        load(out_weight_hbm, out_weight, 2).wait()

        def branch(number, dgain):
            block = pl.ds(pl.multiple_of(number * rows, rows), rows)
            back = taken(block)
            residual = dnormed[block, :]
            spread = lax.rsqrt(jnp.mean(residual * residual, axis=1, keepdims=True) + EPSILON)
            scaled = residual * spread
            moved = back * gain_ref[1:2, :]
            dres = narrow[block, :].astype(F32) + spread * (
                moved - scaled * jnp.mean(moved * scaled, axis=1, keepdims=True)
            )
            tokens_grad_ref[block, :] = dres
            dbranch = dres.astype(BF16)
            dscores[block, :features] = dbranch
            datt[block, :] = lax.dot_general(
                dbranch, out_weight[...], NT, preferred_element_type=F32
            ).astype(BF16)
            return dgain + jnp.sum(back * scaled, axis=0, keepdims=True)

        dgain = lax.fori_loop(0, length // rows, branch, jnp.zeros((1, features), F32))
        for part in range(features // LANES):
            at = lines.shape[0] + features // LANES + part
            small_out[0, at : at + 1, :] = dgain[:, part * LANES : (part + 1) * LANES]
        load(attended_hbm, attended, 3).wait()
        load(normed_hbm, normed, 4).wait()
        load(tokens_hbm, narrow, 5).start()
        dense = lax.dot_general(
            attended[...], dscores[:, :features], TN, preferred_element_type=F32
        )
        half = features // 2
        early_own[:, :half] = jnp.where(core == 0, dense[:, :half], dense[:, half:]).astype(BF16)
        early_out[:, :half] = jnp.where(core == 0, dense[:, half:], dense[:, :half]).astype(BF16)
        drouter = drouter_ref[...].astype(BF16)
        early_own[:, half:] = drouter
        early_out[:, half:] = drouter
        core_copy(0).start()
        dnormed[...] = jnp.zeros_like(dnormed)

    @pl.when((step > 0) & (step <= 2 * groups))
    def _():
        lane = lax.broadcasted_iota(jnp.int32, (1, LANES), 1)
        pair = (step - 1) % 2 * groups + (step - 1) // 2
        columns = pl.ds(pl.multiple_of(pair * LANES, LANES), LANES)
        queries, values, dout = q_ref[...], v_ref[...], datt[:, columns]
        widened = jnp.concatenate([k_ref[...], tile_ref[...]], axis=1)
        dout_wide = dout.astype(F32)
        product = dout_wide * attended[:, columns].astype(F32)
        dout_turned, queries_turned = dout.T, queries.T
        mirror = (
            lax.broadcasted_iota(jnp.int32, (LANES, LANES), 0)
            + lax.broadcasted_iota(jnp.int32, (LANES, LANES), 1)
            == LANES - 1
        ).astype(F32)
        dqueries = [[], []]
        dkeys, dvalues = [], []
        for head in range(2):
            mine = (lane < HEAD) if head == 0 else (lane >= HEAD)
            inner_sum = jnp.sum(jnp.where(mine, product, 0.0), axis=1, keepdims=True)
            masked = jnp.where(mine, dout_wide, 0.0).astype(BF16)
            bands = [jnp.zeros((LANES, LANES), F32) for _ in range(3)]
            before = jnp.zeros((1, LANES), F32)
            after = jnp.zeros((1, LANES), F32)
            for part_of in range(length // rows):
                first = part_of * rows
                block = pl.ds(first, rows)
                dprob = lax.dot_general(
                    masked[first : first + rows], values, NT, preferred_element_type=F32
                )
                scores = kept_ref[head, block, :].astype(F32) * (
                    dprob - inner_sum[first : first + rows]
                )
                rounded = scores.astype(BF16)
                dscores[block, :] = rounded
                both = jnp.dot(rounded, widened, preferred_element_type=F32)
                dqueries[head].append(both[:, :LANES])
                for part in range(inner):
                    tile = part_of * inner + part
                    here = slice(part * LANES, (part + 1) * LANES)
                    for at in range(3):
                        there = tile - 1 + at
                        if 0 <= there < tiles:
                            bands[at] = bands[at] + scores[here, there * LANES : (there + 1) * LANES]
                    sums = jnp.sum(both[here, LANES:], axis=0, keepdims=True)
                    before = before + jnp.where(lane <= tile - 2, sums, 0.0)
                    after = after + jnp.where((lane >= tile + 2) & (lane < tiles), sums, 0.0)
            band = jnp.concatenate([*bands, jnp.zeros((LANES, LANES), F32)], axis=1)
            band = jnp.dot(
                mirror, band, preferred_element_type=F32, precision=lax.Precision.HIGHEST
            )
            band = pltpu.roll(band, 3 * LANES + 1, 1, stride=1, stride_axis=0)
            near = jnp.sum(band, axis=0, keepdims=True)
            lines[pl.ds(2 * pair + head, 1), :] = jnp.concatenate([near, before, after], axis=1)
            half = slice(HEAD * head, HEAD * head + HEAD)
            dkeys.append(
                jnp.dot(queries_turned[half], dscores[...], preferred_element_type=F32)
            )
            dvalues.append(jnp.dot(dout_turned[half], kept_ref[head], preferred_element_type=F32))
        scale = HEAD**-0.5
        dq = jnp.concatenate(
            [
                (jnp.where(lane < HEAD, left, right) * scale).astype(BF16)
                for left, right in zip(*dqueries, strict=True)
            ],
            axis=0,
        )
        dk = (jnp.concatenate(dkeys, axis=0) * scale).T.astype(BF16)
        dv = jnp.concatenate(dvalues, axis=0).T.astype(BF16)
        joined = jnp.concatenate([dq, dk, dv], axis=1)
        weights = jnp.concatenate([wq_ref[...], wk_ref[...], wv_ref[...]], axis=1)
        dnormed[...] += lax.dot_general(joined, weights, NT, preferred_element_type=F32)
        dense = jnp.dot(normed[...], joined, preferred_element_type=F32)
        dwq, dwk, dwv = dense[:, :LANES], dense[:, LANES : 2 * LANES], dense[:, 2 * LANES :]
        own_first, away_first = jnp.where(core == 0, dwq, dwv), jnp.where(core == 0, dwv, dwq)
        for now in range(2 * groups):

            @pl.when(step == now + 1)
            def _(now=now):
                unit, part = now // 2 + 1, now % 2
                at = slice(part * LANES, (part + 1) * LANES)
                own[unit % 2, :, at] = own_first
                core_out[unit - 1, :, at] = away_first.astype(BF16)

                @pl.when(core == part)
                def _():
                    own[unit % 2, :, 2 * LANES :] = dwk

                @pl.when(core != part)
                def _():
                    core_out[unit - 1, :, 2 * LANES :] = dwk.astype(BF16)

                if part == 1:
                    core_copy(unit).start()

    last = 2 * groups + 1
    plan = {}
    for unit in range(groups + 1):
        plan.setdefault(min(2 * unit + 1, last), []).append((sum_cores, unit))
        plan.setdefault(min(2 * unit + 4, last), []).append((sum_planes, unit))
        plan.setdefault(last, []).append((sum_layers, unit))
    order = [sum_layers, sum_planes, sum_cores]
    for now in range(1, last):

        @pl.when(step == now)
        def _(now=now):
            for action, unit in sorted(plan.get(now, []), key=lambda p: order.index(p[0])):
                action(unit)

    @pl.when(step == last)
    def _():
        todo = plan.get(last, [])
        for action, unit in todo:
            if action is sum_cores:
                action(unit)
        for action, unit in todo:
            if action is sum_planes and unit < groups:
                action(unit)
        load(tokens_hbm, narrow, 5).wait()
        gain = gain_ref[0:1, :]
        inputs = narrow[...].astype(F32)
        spread = lax.rsqrt(jnp.mean(inputs * inputs, axis=1, keepdims=True) + EPSILON)
        back = dnormed[...]
        scaled = inputs * spread
        dgain = jnp.sum(back * scaled, axis=0, keepdims=True)
        moved = back * gain
        tokens_grad_ref[...] = tokens_grad_ref[...] + spread * (
            moved - scaled * jnp.mean(moved * scaled, axis=1, keepdims=True)
        )
        table = jnp.dot(
            lines[...], bucket_ref[...], preferred_element_type=F32, precision=lax.Precision.HIGHEST
        )
        small_out[0, 0 : lines.shape[0], :] = table
        base = lines.shape[0]
        wide = features // LANES
        for part in range(wide):
            small_out[0, base + part : base + part + 1, :] = dgain[
                :, part * LANES : (part + 1) * LANES
            ]
        if small_out.shape[1] > base + 2 * wide:
            small_out[0, base + 2 * wide :, :] = jnp.zeros(
                (small_out.shape[1] - base - 2 * wide, LANES), F32
            )

        small_start(0, 0, 1)
        load(residual_hbm, dnormed, 6).start()
        for action, unit in todo:
            if action is sum_planes and unit == groups:
                action(unit)
        small_out[1] = small_add(0, 0, 1)
        small_start(1, 1, plane)
        own_made().wait()
        each(1, ranks, lambda number: made_copy(number).wait_recv())
        each(0, ranks, lambda number: came_load(number).start())
        each(0, ranks, lambda number: came_load(number).wait())
        load(residual_hbm, dnormed, 6).wait()

        def finish(number, carry):
            block = pl.ds(pl.multiple_of(number * rows, rows), rows)
            datt[block, :] = (dnormed[block, :] + gate_ref[block, :] * taken(block)).astype(BF16)
            return carry

        lax.fori_loop(0, length // rows, finish, 0)
        load(datt, output_hbm, 10).start()
        small_out[2] = small_add(1, 1, plane)
        small_start(2, plane, plane + layers - 1)
        for action, unit in todo:
            if action is sum_layers:
                action(unit)
        small_ref[...] = small_add(2, plane, plane + layers - 1)
        for number in range(plane + layers - 1):
            small_copy(number).wait_send()
        each(1, ranks, lambda number: made_copy(number).wait_send())
        load(datt, output_hbm, 10).wait()
        for unit in range(groups + 1):
            core_copy(unit).wait_send()
            for k in range(1, plane):
                plane_copy(unit, k).wait_send()
            for k in range(1, layers):
                layer_copy(unit, k).wait_send()


def run_tail(
    projected, attended, kept, qkv_weight, out_weight, normed_turned, tokens, cotangent, residual, gains,
    drouter, target, gate, moved, made, rows,
):
    length, features = tokens.shape
    heads = kept.shape[0]
    ranks = made.shape[0]
    pairs = heads // 2
    groups = pairs // 2
    plane = 4
    layers = ranks // plane
    slab = features // ranks
    early = features // 2 + LANES
    late = 3 * LANES
    tile_of = (
        jnp.arange(length)[:, None] // LANES == jnp.arange(LANES)[None, :]
    ).astype(BF16)
    at = jnp.arange(4 * LANES, dtype=jnp.int32)
    relative = jnp.where(at < 3 * LANES, at - LANES, at - 5 * LANES)
    ends = bucket_index(jnp.array([-length, length], jnp.int32))
    bucket = jnp.concatenate([bucket_index(relative), jnp.repeat(ends, LANES)])
    bucket_of = (bucket[:, None] == jnp.arange(LANES)[None, :]).astype(F32)
    line_rows = heads + -heads % 4
    small_rows = line_rows + 2 * (features // LANES)
    small_rows += -small_rows % 8

    def pair_of(i):
        i = jnp.clip(i - 1, 0, pairs - 1)
        return i % 2 * groups + i // 2

    def column(shape, offset):
        return pl.BlockSpec(shape, lambda i: (0, offset + pair_of(i)))

    def whole(shape):
        return pl.BlockSpec(shape, lambda i: (0, 0), pipeline_mode=pl.Buffered(1))

    dma = pltpu.SemaphoreType.DMA
    any_ref = pl.BlockSpec(memory_space=pl.ANY)
    units = groups + 1
    return pl.pallas_call(
        functools.partial(tail_kernel, rows=rows, ranks=ranks, plane=plane),
        grid=(pairs + 2,),
        in_specs=[
            column((length, LANES), 0),
            column((length, LANES), pairs),
            column((length, LANES), 2 * pairs),
            pl.BlockSpec((2, length, length), lambda i: (pair_of(i), 0, 0)),
            column((features, LANES), 0),
            column((features, LANES), pairs),
            column((features, LANES), 2 * pairs),
            whole((length, LANES)),
            whole(gains.shape),
            whole(bucket_of.shape),
            whole((features, LANES)),
            whole((length, 1)),
            whole((length, 1)),
            *[any_ref] * 8,
        ],
        out_specs=[
            whole((length, features)),
            whole((slab, groups * late)),
            whole((slab, features // 2)),
            whole((slab, LANES)),
            whole((small_rows, LANES)),
            any_ref,
            any_ref,
        ],
        out_shape=[
            jax.ShapeDtypeStruct((length, features), F32),
            jax.ShapeDtypeStruct((slab, groups * late), F32),
            jax.ShapeDtypeStruct((slab, features // 2), F32),
            jax.ShapeDtypeStruct((slab, LANES), F32),
            jax.ShapeDtypeStruct((small_rows, LANES), F32),
            jax.ShapeDtypeStruct((length, features), BF16),
            jax.ShapeDtypeStruct(made.shape, BF16),
        ],
        scratch_shapes=[
            pltpu.VMEM((features, length), BF16),
            pltpu.VMEM((length, features), BF16),
            pltpu.VMEM((length, features), BF16),
            pltpu.VMEM((features, features), BF16),
            pltpu.VMEM((ranks * made.shape[1], features), BF16),
            pltpu.VMEM((length, features), BF16),
            pltpu.VMEM((length, length), BF16),
            pltpu.VMEM((length, features), F32),
            pltpu.VMEM((line_rows, 6 * LANES), F32),
            pltpu.VMEM((2, features, late), F32),
            pltpu.VMEM((groups, features, late), BF16),
            pltpu.VMEM((groups, features, late), BF16),
            pltpu.VMEM((groups, layers, plane, slab, late), BF16),
            pltpu.VMEM((groups, plane - 1, layers, slab, late), BF16),
            pltpu.VMEM((groups, layers, slab, late), BF16),
            pltpu.VMEM((groups, layers - 1, slab, late), BF16),
            pltpu.VMEM((features, early), BF16),
            pltpu.VMEM((features, early), BF16),
            pltpu.VMEM((features, early), BF16),
            pltpu.VMEM((layers, plane, slab, early), BF16),
            pltpu.VMEM((plane - 1, layers, slab, early), BF16),
            pltpu.VMEM((layers, slab, early), BF16),
            pltpu.VMEM((layers - 1, slab, early), BF16),
            pltpu.VMEM((3, small_rows, LANES), F32),
            pltpu.VMEM((plane + layers - 1, small_rows, LANES), F32),
            dma((11,)),
            dma((ranks,)),
            dma((ranks,)),
            dma((units,)),
            dma((units,)),
            dma((units, plane)),
            dma((units, plane)),
            dma((units, layers)),
            dma((units, layers)),
            dma((plane + layers - 1,)),
            dma((plane + layers - 1,)),
        ],
        compiler_params=pltpu.CompilerParams(
            collective_id=2, has_side_effects=True, vmem_limit_bytes=62 * MIB
        ),
        cost_estimate=pl.CostEstimate(
            flops=36 * heads * length * length * HEAD,
            bytes_accessed=2 * heads * length * length + 30 * length * features,
            transcendentals=0,
        ),
    )(
        projected, projected, projected, kept, qkv_weight, qkv_weight, qkv_weight, tile_of, gains,
        bucket_of, drouter, target, gate, normed_turned, tokens, cotangent, residual, attended,
        out_weight, moved, made,
    )


def core_sum(values, dim):
    half = values.shape[dim] // 2
    core = lax.axis_index("group")
    own = lax.dynamic_slice_in_dim(values, core * half, half, dim)
    other = lax.dynamic_slice_in_dim(values, (1 - core) * half, half, dim).astype(BF16)
    return own + lax.ppermute(other, "group", [(0, 1), (1, 0)]).astype(F32)


def exchange(values):
    return lax.all_to_all(values, "expert", split_axis=0, concat_axis=0, tiled=True)


def per_device(
    tokens, gains, qkv_weight, out_weight, rel_bias, router_weight, w_in, w_out, routes, factors,
    cotangent,
):
    length, features = tokens.shape
    bucket_count = rel_bias.shape[0]
    expert_count = router_weight.shape[1]
    slot_count = 2 * length // expert_count
    rows = min(256, length)
    gain_rows = gains.astype(F32)
    w_in, w_out = w_in[0], w_out[0]
    me = lax.axis_index("expert")
    core = lax.axis_index("group")

    routed = routes[:, 0]
    row_index = jnp.arange(length, dtype=jnp.int32)
    chosen = routed[:, None] == jnp.arange(expert_count, dtype=jnp.int32)[None, :]
    earlier = (row_index[:, None] > row_index[None, :]).astype(BF16)
    before = jnp.dot(earlier, chosen.astype(BF16), preferred_element_type=F32)
    place = jnp.sum(before * chosen.astype(F32), axis=-1).astype(jnp.int32)
    capacity = factors[0] * (length // expert_count)
    target = jnp.where(place < capacity, routed * slot_count + place, -1)
    slots = jnp.arange(expert_count * slot_count, dtype=jnp.int32)
    picks = (slots[:, None] == target[None, :]).astype(BF16)

    def pack(values):
        packed = jnp.dot(picks, values, preferred_element_type=F32).astype(BF16)
        return packed.reshape(expert_count, slot_count, features)

    def unpack(values):
        return lax.dot_general(
            picks, values.reshape(-1, features), TN, preferred_element_type=F32
        )

    upstream_there = exchange(pack(cotangent))

    inputs = tokens.astype(F32)
    normed_in = norm_rows(inputs, gain_rows[0]).astype(BF16)
    projected = jnp.dot(normed_in, qkv_weight, preferred_element_type=F32).astype(BF16)
    attended, kept = attend(projected, bias_lines(rel_bias, length), rows)
    residual_one = inputs + jnp.dot(attended, out_weight, preferred_element_type=F32)
    hidden = norm_rows(residual_one, gain_rows[1]).astype(BF16)

    logits = jnp.dot(hidden, router_weight, preferred_element_type=F32)
    raised = jnp.exp(logits - jnp.max(logits, axis=-1, keepdims=True))
    router = raised / jnp.sum(raised, axis=-1, keepdims=True)
    gate_value = jnp.sum(router * chosen.astype(F32), axis=-1)

    padded = -expert_count % LANES
    router_padded = jnp.pad(router_weight, ((0, 0), (0, padded)))
    packed, normed_turned = lax.optimization_barrier((pack(hidden), normed_in.T))
    made, dmoved_back, grad_first, grad_second, drouter = run_expert(
        packed, upstream_there, w_in, w_out, router_padded, expert_count
    )
    experts = lax.axis_size("expert")
    cores = lax.axis_size("group")
    slab = features // experts
    gain_at = (core, me * slab)
    router_at = (core * (expert_count // cores),)
    if experts == 16 and cores == 2 and features % (16 * experts) == 0:
        grad_tokens, grad_qkv, grad_out, router_sums, small, output, _ = run_tail(
            projected, attended, kept, qkv_weight, out_weight, normed_turned, tokens, cotangent,
            residual_one, gain_rows, drouter, target[:, None], gate_value[:, None], dmoved_back, made,
            rows,
        )
        heads = rel_bias.shape[1]
        gain_sums = small[heads + -heads % 4 :][: 2 * features // LANES].reshape(2, features)
        return (
            output,
            grad_tokens,
            lax.dynamic_slice(gain_sums, gain_at, (2 // cores, slab)),
            grad_qkv,
            grad_out,
            small[:heads, :bucket_count].T,
            lax.dynamic_slice(router_sums, (0, *router_at), (slab, expert_count // cores)),
            grad_first[None],
            grad_second[None],
        )

    made_back = exchange(made)
    grad_router = drouter[:, :expert_count]

    dhidden = unpack(dmoved_back)
    upstream = cotangent.astype(F32)
    _, back_two = jax.vjp(norm_rows, residual_one, gain_rows[1])
    dres_norm, dgain_two = back_two(dhidden)
    dres = upstream + dres_norm
    dbranch = dres.astype(BF16)
    datt = lax.dot_general(dbranch, out_weight, NT, preferred_element_type=F32).astype(BF16)
    grad_out = lax.dot_general(attended, dbranch, TN, preferred_element_type=F32)
    dqkv, band, far = attend_back(projected, attended, datt, kept, rows)
    grad_proj = jnp.einsum("td,cte->dce", normed_in, dqkv, preferred_element_type=F32)
    grad_proj = grad_proj.reshape(features, 3 * features)
    dnormed = jnp.einsum(
        "cte,dce->td",
        dqkv,
        qkv_weight.reshape(features, 3, features),
        preferred_element_type=F32,
    )
    _, back_one = jax.vjp(norm_rows, inputs, gain_rows[0])
    dinput_norm, dgain_one = back_one(dnormed)
    grad_tokens = dres + dinput_norm

    brought = unpack(made_back)
    output = (residual_one + gate_value[:, None] * brought).astype(BF16)

    def scattered(values):
        return lax.psum_scatter(
            core_sum(values, 1).astype(BF16), "expert", scatter_dimension=0, tiled=True
        ).astype(F32)

    small = [
        jnp.stack([dgain_one, dgain_two], axis=0),
        grad_router,
        table_gradient(band, far, bucket_count),
    ]
    flat = lax.psum(jnp.concatenate([s.reshape(-1) for s in small]), ("group", "expert"))
    summed = []
    at = 0
    for s in small:
        summed.append(flat[at : at + s.size].reshape(s.shape))
        at += s.size
    grad_gains = lax.dynamic_slice(summed[0], gain_at, (2 // cores, slab))
    grad_router = lax.dynamic_slice(
        summed[1], (me * slab, *router_at), (slab, expert_count // cores)
    )
    return (
        output,
        grad_tokens,
        grad_gains,
        scattered(grad_proj),
        scattered(grad_out),
        summed[2],
        grad_router,
        grad_first[None],
        grad_second[None],
    )


def solution(mesh):
    return jax.shard_map(
        per_device,
        mesh=mesh,
        in_specs=(
            P(("group", "expert"), None),
            P(),
            P(),
            P(),
            P(),
            P(),
            P("expert", None, None),
            P("expert", None, None),
            P(("group", "expert"), None),
            P(("group", "expert")),
            P(("group", "expert"), None),
        ),
        out_specs=(
            P(("group", "expert"), None),
            P(("group", "expert"), None),
            P("group", "expert"),
            P("expert", "group"),
            P("expert", "group"),
            P(),
            P("expert", "group"),
            P("expert", None, "group"),
            P("expert", "group", None),
        ),
        check_vma=False,
    )
```

```python
import functools

import jax
import jax.numpy as jnp
from jax import lax
from jax.experimental import pallas as pl
from jax.experimental.pallas import tpu as pltpu
from jax.sharding import PartitionSpec as P

EPSILON = 1e-06
BOUNDARIES = (12, 16, 23, 32, 46, 64, 91)
F32 = jnp.float32
BF16 = jnp.bfloat16
LANES = 128
HEAD = 64
NT = (((1,), (1,)), ((), ()))
TN = (((0,), (0,)), ((), ()))
MIB = 2**20


def bucket_index(relative):
    distance = jnp.abs(relative)
    farther = jnp.full(relative.shape, 8, jnp.int32)
    for boundary in BOUNDARIES:
        farther = farther + (distance >= boundary).astype(jnp.int32)
    nearest = jnp.where(distance < 8, distance, farther)
    return nearest + 16 * (relative > 0).astype(jnp.int32)


def norm_rows(values, gain_row):
    return (
        values * lax.rsqrt(jnp.mean(values * values, axis=-1, keepdims=True) + EPSILON) * gain_row
    )


def pack_kernel(target_ref, values_ref, packed_ref):
    rows = packed_ref.shape[0]
    slot = pl.program_id(0) * rows + lax.broadcasted_iota(jnp.int32, (rows, 1), 0)
    picks = (slot == target_ref[...]).astype(F32).astype(BF16)
    packed_ref[...] = jnp.dot(picks, values_ref[...], preferred_element_type=F32).astype(BF16)


def pack_rows(target, values, slots):
    length, features = values.shape
    rows = min(512, slots)
    return pl.pallas_call(
        pack_kernel,
        grid=(slots // rows,),
        in_specs=[
            pl.BlockSpec((1, length), lambda i: (0, 0)),
            pl.BlockSpec((length, features), lambda i: (0, 0)),
        ],
        out_specs=pl.BlockSpec((rows, features), lambda i: (i, 0)),
        out_shape=jax.ShapeDtypeStruct((slots, features), BF16),
        compiler_params=pltpu.CompilerParams(vmem_limit_bytes=32 * MIB),
        cost_estimate=pl.CostEstimate(
            flops=2 * slots * length * features,
            bytes_accessed=2 * (length + slots) * features,
            transcendentals=0,
        ),
    )(target[None, :], values)


def attend_kernel(q_ref, k_ref, v_ref, line_ref, out_ref, kept_ref, slab_ref, *, rows):
    length = q_ref.shape[0]
    lane = lax.broadcasted_iota(jnp.int32, (1, LANES), 1)
    keys, values = k_ref[...], v_ref[...]
    for head in range(2):
        line = jnp.broadcast_to(line_ref[head], (rows, 2 * length))
        slab_ref[head] = pltpu.roll(line, 0, 1, stride=1, stride_axis=0)
    for step in range(length // rows):
        block = pl.ds(step * rows, rows)
        queries = q_ref[block, :].astype(F32) * HEAD**-0.5
        joined = []
        for head in range(2):
            mine = (lane < HEAD) if head == 0 else (lane >= HEAD)
            own = jnp.where(mine, queries, 0.0).astype(BF16)
            scores = lax.dot_general(own, keys, NT, preferred_element_type=F32)
            scores = scores + slab_ref[head, :, pl.ds(length - rows * step, length)]
            top = jnp.max(scores, axis=1, keepdims=True)
            raised = jnp.exp(scores - top)
            total = jnp.sum(raised, axis=1, keepdims=True)
            weights = (raised * (1.0 / total)).astype(BF16)
            kept_ref[head, block, :] = weights
            joined.append(jnp.dot(weights, values, preferred_element_type=F32))
        out_ref[block, :] = jnp.where(lane < HEAD, joined[0], joined[1]).astype(BF16)


def attend(projected, lines, rows):
    length, features = projected.shape[0], projected.shape[1] // 3
    heads = lines.shape[0]
    pairs = heads // 2
    return pl.pallas_call(
        functools.partial(attend_kernel, rows=rows),
        grid=(pairs,),
        in_specs=[
            pl.BlockSpec((length, LANES), lambda i: (0, i)),
            pl.BlockSpec((length, LANES), lambda i: (0, pairs + i)),
            pl.BlockSpec((length, LANES), lambda i: (0, 2 * pairs + i)),
            pl.BlockSpec((2, 1, 2 * length), lambda i: (i, 0, 0)),
        ],
        out_specs=[
            pl.BlockSpec((length, LANES), lambda i: (0, i)),
            pl.BlockSpec((2, length, length), lambda i: (i, 0, 0)),
        ],
        out_shape=[
            jax.ShapeDtypeStruct((length, features), BF16),
            jax.ShapeDtypeStruct((heads, length, length), BF16),
        ],
        scratch_shapes=[pltpu.VMEM((2, rows, 2 * length), F32)],
        compiler_params=pltpu.CompilerParams(vmem_limit_bytes=50 * MIB),
        cost_estimate=pl.CostEstimate(
            flops=16 * heads * length * length * HEAD,
            bytes_accessed=2 * heads * length * length + 8 * length * features,
            transcendentals=heads * length * length,
        ),
    )(projected, projected, projected, lines)


def attend_back_kernel(
    q_ref, k_ref, v_ref, out_ref, dout_ref, kept_ref, tile_ref,
    grad_ref, band_ref, far_ref, dscores_ref, *, rows,
):
    length = q_ref.shape[0]
    tiles = length // LANES
    inner = rows // LANES
    lane = lax.broadcasted_iota(jnp.int32, (1, LANES), 1)
    queries, values, dout = q_ref[...], v_ref[...], dout_ref[...]
    widened = jnp.concatenate([k_ref[...], tile_ref[...]], axis=1)
    dout_wide = dout.astype(F32)
    product = dout_wide * out_ref[...].astype(F32)
    dout_turned, queries_turned = dout.T, queries.T
    dqueries = [[], []]
    dkeys, dvalues = [], []
    for head in range(2):
        mine = (lane < HEAD) if head == 0 else (lane >= HEAD)
        inner_sum = jnp.sum(jnp.where(mine, product, 0.0), axis=1, keepdims=True)
        own = jnp.where(mine, dout_wide, 0.0).astype(BF16)
        band_ref[head] = jnp.zeros_like(band_ref[head])
        for step in range(length // rows):
            first = step * rows
            block = pl.ds(first, rows)
            dprob = lax.dot_general(
                own[first : first + rows], values, NT, preferred_element_type=F32
            )
            dscores = kept_ref[head, block, :].astype(F32) * (
                dprob - inner_sum[first : first + rows]
            )
            rounded = dscores.astype(BF16)
            dscores_ref[block, :] = rounded
            for part in range(inner):
                tile = step * inner + part
                low, high = max(tile - 1, 0), min(tile + 2, tiles)
                at = low - (tile - 1)
                band_ref[head, :, at * LANES : (at + high - low) * LANES] += dscores[
                    part * LANES : (part + 1) * LANES, low * LANES : high * LANES
                ]
            both = jnp.dot(rounded, widened, preferred_element_type=F32)
            dqueries[head].append(both[:, :LANES])
            for part in range(inner):
                far_ref[head, step * inner + part] = jnp.sum(
                    both[part * LANES : (part + 1) * LANES, LANES:], axis=0
                )
        half = slice(HEAD * head, HEAD * head + HEAD)
        dkeys.append(jnp.dot(queries_turned[half], dscores_ref[...], preferred_element_type=F32))
        dvalues.append(jnp.dot(dout_turned[half], kept_ref[head], preferred_element_type=F32))
    scale = HEAD**-0.5
    for step in range(length // rows):
        grad_ref[0, pl.ds(step * rows, rows), :] = (
            jnp.where(lane < HEAD, dqueries[0][step], dqueries[1][step]) * scale
        ).astype(BF16)
    grad_ref[1] = (jnp.concatenate(dkeys, axis=0) * scale).T.astype(BF16)
    grad_ref[2] = jnp.concatenate(dvalues, axis=0).T.astype(BF16)


def attend_back(projected, attended, datt, kept, rows):
    length, features = projected.shape[0], projected.shape[1] // 3
    heads = kept.shape[0]
    pairs = heads // 2
    tiles = length // LANES
    tile_of = (
        jnp.arange(length)[:, None] // LANES == jnp.arange(LANES)[None, :]
    ).astype(BF16)
    return pl.pallas_call(
        functools.partial(attend_back_kernel, rows=rows),
        grid=(pairs,),
        in_specs=[
            pl.BlockSpec((length, LANES), lambda i: (0, i)),
            pl.BlockSpec((length, LANES), lambda i: (0, pairs + i)),
            pl.BlockSpec((length, LANES), lambda i: (0, 2 * pairs + i)),
            pl.BlockSpec((length, LANES), lambda i: (0, i)),
            pl.BlockSpec((length, LANES), lambda i: (0, i)),
            pl.BlockSpec((2, length, length), lambda i: (i, 0, 0)),
            pl.BlockSpec((length, LANES), lambda i: (0, 0)),
        ],
        out_specs=[
            pl.BlockSpec((3, length, LANES), lambda i: (0, 0, i)),
            pl.BlockSpec((2, LANES, 3 * LANES), lambda i: (i, 0, 0)),
            pl.BlockSpec((2, tiles, LANES), lambda i: (i, 0, 0)),
        ],
        out_shape=[
            jax.ShapeDtypeStruct((3, length, features), BF16),
            jax.ShapeDtypeStruct((heads, LANES, 3 * LANES), F32),
            jax.ShapeDtypeStruct((heads, tiles, LANES), F32),
        ],
        scratch_shapes=[pltpu.VMEM((length, length), BF16)],
        compiler_params=pltpu.CompilerParams(vmem_limit_bytes=56 * MIB),
        cost_estimate=pl.CostEstimate(
            flops=32 * heads * length * length * HEAD,
            bytes_accessed=2 * heads * length * length + 18 * length * features,
            transcendentals=0,
        ),
    )(projected, projected, projected, attended, datt, kept, tile_of)


def bias_lines(rel_bias, length):
    relative = jnp.arange(2 * length, dtype=jnp.int32) - length
    onehot = (
        bucket_index(relative)[None, :]
        == jnp.arange(rel_bias.shape[0], dtype=jnp.int32)[:, None]
    ).astype(F32)
    return jnp.einsum(
        "ch,cr->hr", rel_bias.astype(F32), onehot, precision=lax.Precision.HIGHEST
    )[:, None, :]


def table_gradient(band, far, bucket_count):
    heads, tiles = far.shape[0], far.shape[1]
    relative = jnp.arange(3 * LANES)[None, :] - LANES - jnp.arange(LANES)[:, None]
    onehot = (bucket_index(relative)[:, :, None] == jnp.arange(bucket_count)).astype(F32)
    near = jnp.dot(
        band.reshape(heads, -1),
        onehot.reshape(-1, bucket_count),
        precision=lax.Precision.HIGHEST,
    )
    here = jnp.arange(tiles)[:, None]
    there = jnp.arange(LANES)[None, :]
    before = jnp.sum(jnp.where(there <= here - 2, far, 0.0), axis=(1, 2))
    after = jnp.sum(jnp.where(there >= here + 2, far, 0.0), axis=(1, 2))
    buckets = jnp.arange(bucket_count)
    last = bucket_index(jnp.array([-LANES, LANES], jnp.int32))
    return (
        near
        + before[:, None] * (buckets == last[0])
        + after[:, None] * (buckets == last[1])
    ).T


def turned(me, k, ranks, plane, sign):
    if plane == 1:
        return (me + ranks + sign * k) % ranks
    layer, side = me // plane, me % plane
    far, near = k // plane, k % plane
    if ranks // plane % 4:
        layers = ranks // plane
        to_layer = (layer + layers + sign * far) % layers
    else:
        sets = ranks // plane // 4
        low = (layer % 4 // 2 + far % 4 // 2) % 2 * 2 + (layer + far) % 2
        to_layer = (layer // 4 + sets + sign * (far // 4)) % sets * 4 + low
    to_side = (side // 2 + near // 2) % 2 * 2 + (side + near) % 2
    return to_layer * plane + to_side


def expert_kernel(
    hidden_ref, cot_ref, w_in_ref, w_out_ref, router_ref,
    made_ref, back_ref, first_ref, second_ref, drouter_ref,
    w_in, w_out, x, c, x_turned, dexp_turned, moved, act, dpre, stage_first, stage_second, load_sem, cot_sem, out_sem, sent, came, moved_sent, moved_came, core_sent,
    core_came, stage_sem, core_ready, *, ranks, expert_count, rows, width, columns,
):
    features = x.shape[1]
    slots = x.shape[0] // ranks
    hidden_width = w_in.shape[1]
    half = hidden_width // 2
    per_step = rows // slots
    core, me = lax.axis_index("group"), lax.axis_index("expert")
    plane = 4 if ranks % 4 == 0 else 1

    def partner(k, sign):
        return turned(me, k, ranks, plane, sign)

    def span(k):
        return pl.ds(pl.multiple_of(k * slots, slots), slots)

    barrier = pltpu.get_barrier_semaphore()

    def greet(k, carry):
        pl.semaphore_signal(
            barrier, inc=1, device_id=(core, partner(k, 1)), device_id_type=pl.DeviceIdType.MESH
        )
        return carry

    lax.fori_loop(1, ranks, greet, 0)
    pl.semaphore_signal(
        barrier, inc=1, device_id=(1 - core, me), device_id_type=pl.DeviceIdType.MESH
    )

    loads = [
        pltpu.make_async_copy(w_in_ref, w_in, load_sem.at[0]),
        pltpu.make_async_copy(w_out_ref, w_out, load_sem.at[1]),
        pltpu.make_async_copy(hidden_ref.at[me], x.at[pl.ds(0, slots)], load_sem.at[2]),
    ]
    for load in loads:
        load.start()

    def cot_copy(k):
        return pltpu.make_async_copy(cot_ref.at[partner(k, -1)], c.at[span(k)], cot_sem.at[k])

    def load_cot(k, carry):
        cot_copy(k).start()
        return carry

    lax.fori_loop(0, ranks, load_cot, 0)
    pl.semaphore_wait(barrier, ranks)

    def hidden_copy(k):
        return pltpu.make_async_remote_copy(
            src_ref=hidden_ref.at[partner(k, 1)],
            dst_ref=x.at[span(k)],
            send_sem=sent.at[k],
            recv_sem=came.at[k],
            device_id=(core, partner(k, 1)),
            device_id_type=pl.DeviceIdType.MESH,
        )

    def moved_copy(k):
        return pltpu.make_async_remote_copy(
            src_ref=moved.at[span(k)],
            dst_ref=back_ref.at[me],
            send_sem=moved_sent.at[k],
            recv_sem=moved_came.at[k],
            device_id=(core, partner(k, -1)),
            device_id_type=pl.DeviceIdType.MESH,
        )

    def own_moved_copy():
        return pltpu.make_async_copy(moved.at[pl.ds(0, slots)], back_ref.at[me], load_sem.at[3])

    def made_copy(k):
        return pltpu.make_async_copy(c.at[span(k)], made_ref.at[partner(k, -1)], out_sem.at[k])

    def start_hidden(k, carry):
        hidden_copy(k).start()
        return carry

    lax.fori_loop(1, ranks, start_hidden, 0)
    for load in loads:
        load.wait()
    drouter_ref[...] = jnp.zeros_like(drouter_ref)
    root = (2.0 / jnp.pi) ** 0.5

    def run(first_rank):
        block = pl.ds(pl.multiple_of(first_rank * slots, rows), rows)
        xs = x[block, :]
        upstream = c[block, :].astype(F32)
        router_weight = router_ref[...]
        lane = lax.broadcasted_iota(jnp.int32, (1, router_weight.shape[1]), 1)
        logits = jnp.dot(xs, router_weight, preferred_element_type=F32)
        logits = jnp.where(lane < expert_count, logits, -jnp.inf)
        raised = jnp.exp(logits - jnp.max(logits, axis=-1, keepdims=True))
        router = raised / jnp.sum(raised, axis=-1, keepdims=True)
        chosen = (lane == me).astype(F32)
        gate = jnp.sum(router * chosen, axis=-1, keepdims=True)
        dexp = (gate * upstream).astype(BF16)
        made = jnp.zeros((rows, features), F32)
        dmoved = jnp.zeros((rows, features), F32)
        for at in range(0, hidden_width, width):
            part = slice(at, at + width)
            pre = jnp.dot(xs, w_in[:, part], preferred_element_type=F32)
            square = pre * pre
            turned = jnp.tanh(pre * (root + (root * 0.044715) * square))
            upper = 0.5 + 0.5 * turned
            active = (pre * upper).astype(BF16)
            slope = upper + pre * (upper * (1.0 - turned)) * (
                root + (3 * root * 0.044715) * square
            )
            act[block, part] = active
            made = made + jnp.dot(active, w_out[part, :], preferred_element_type=F32)
            dact = lax.dot_general(dexp, w_out[part, :], NT, preferred_element_type=F32)
            dpart = (dact * slope).astype(BF16)
            dpre[block, part] = dpart
            dmoved = dmoved + lax.dot_general(
                dpart, w_in[:, part], NT, preferred_element_type=F32
            )
        made = made.astype(BF16)
        c[block, :] = made
        dgate = jnp.sum(upstream * made.astype(F32), axis=-1, keepdims=True)
        dlogits = (dgate * gate * (chosen - router)).astype(BF16)
        dmoved = dmoved + lax.dot_general(dlogits, router_weight, NT, preferred_element_type=F32)
        moved[block, :] = dmoved.astype(BF16)
        xt = xs.T
        x_turned[:, block] = xt
        dexp_turned[:, block] = dexp.T
        drouter_ref[...] += jnp.dot(xt, dlogits, preferred_element_type=F32)

    last = ranks // per_step - 1

    def step(number, carry):
        first_rank = number * per_step
        for inner in range(per_step):
            k = first_rank + inner
            cot_copy(k).wait()

            @pl.when(k > 0)
            def _(k=k):
                hidden_copy(k).wait_recv()

        @pl.when(number == last)
        def _():
            def start_moved(k, carry):
                moved_copy(k).start()
                return carry

            lax.fori_loop(plane, first_rank, start_moved, 0)

        run(first_rank)
        for inner in range(per_step):
            k = first_rank + inner
            made_copy(k).start()

            @pl.when((k > 0) & ((k < plane) | (number == last)))
            def _(k=k):
                moved_copy(k).start()

        @pl.when(number == 0)
        def _():
            own_moved_copy().start()

        return carry

    lax.fori_loop(0, ranks // per_step, step, 0)

    other = 1 - core
    across = features // columns

    def landed_first(n):
        return pl.ds(n // across * features, features), pl.ds(n % across * columns, columns)

    def first_copy(n):
        part = pl.ds(n * columns, columns)
        return pltpu.make_async_remote_copy(
            src_ref=w_in.at[:, part],
            dst_ref=c.at[landed_first(n)],
            send_sem=core_sent.at[0, n],
            recv_sem=core_came.at[0, n],
            device_id=(other, me),
            device_id_type=pl.DeviceIdType.MESH,
        )

    def second_copy(n):
        part = pl.ds(n * columns, columns)
        return pltpu.make_async_remote_copy(
            src_ref=w_out.at[part],
            dst_ref=x.at[part],
            send_sem=core_sent.at[1, n],
            recv_sem=core_came.at[1, n],
            device_id=(other, me),
            device_id_type=pl.DeviceIdType.MESH,
        )

    def product(turned, wide, part):
        return jnp.dot(turned[...], wide[:, part], preferred_element_type=F32)

    def made_out(k, carry):
        made_copy(k).wait()
        return carry

    lax.fori_loop(0, ranks, made_out, 0)
    pl.semaphore_signal(
        core_ready, inc=1, device_id=(other, me), device_id_type=pl.DeviceIdType.MESH
    )
    tiles = half // columns
    for n in range(tiles):
        part = pl.ds(pl.multiple_of(other * half + n * columns, columns), columns)
        w_in[:, n * columns : (n + 1) * columns] = product(x_turned, dpre, part).astype(BF16)
        if n == 0:
            pl.semaphore_wait(core_ready, 1)
        first_copy(n).start()
        w_out[n * columns : (n + 1) * columns, :] = product(dexp_turned, act, part).T.astype(BF16)
        second_copy(n).start()
    stores = []
    for n in range(tiles):
        part = pl.ds(pl.multiple_of(core * half + n * columns, columns), columns)
        here = slice(n * columns, (n + 1) * columns)
        own = product(x_turned, dpre, part)
        first_copy(n).wait_recv()
        if n:
            stores[2 * n - 2].wait()
        stage_first[...] = own + c[landed_first(n)].astype(F32)
        stores.append(
            pltpu.make_async_copy(
                stage_first, first_ref.at[:, pl.ds(n * columns, columns)],
                stage_sem.at[0, n],
            )
        )
        stores[-1].start()
        own = product(dexp_turned, act, part).T
        second_copy(n).wait_recv()
        if n:
            stores[2 * n - 1].wait()
        stage_second[...] = own + x[here, :].astype(F32)
        stores.append(
            pltpu.make_async_copy(
                stage_second, second_ref.at[pl.ds(n * columns, columns)],
                stage_sem.at[1, n],
            )
        )
        stores[-1].start()
    for store in stores[-2:]:
        store.wait()
    for n in range(tiles):
        first_copy(n).wait_send()
        second_copy(n).wait_send()

    def finish(k, carry):
        @pl.when(k > 0)
        def _():
            hidden_copy(k).wait_send()
            moved_copy(k).wait_send()
            moved_copy(k).wait_recv()

        return carry

    lax.fori_loop(0, ranks, finish, 0)
    own_moved_copy().wait()


def run_expert(hidden, cot, w_in, w_out, router_padded, expert_count):
    ranks, slots, features = hidden.shape
    hidden_width = w_in.shape[1]
    rows = max(min(256, ranks * slots), slots)
    total = ranks * slots
    padded = router_padded.shape[1]
    half = hidden_width // 2
    columns = min(256, half)
    tiles = half // columns
    any_ref = pl.BlockSpec(memory_space=pl.ANY)
    vmem = pl.BlockSpec(memory_space=pltpu.VMEM)
    dma = pltpu.SemaphoreType.DMA
    return pl.pallas_call(
        functools.partial(
            expert_kernel,
            ranks=ranks,
            expert_count=expert_count,
            rows=rows,
            width=min(512, hidden_width),
            columns=columns,
        ),
        in_specs=[any_ref, any_ref, any_ref, any_ref, vmem],
        out_specs=[any_ref, any_ref, any_ref, any_ref, vmem],
        out_shape=[
            jax.ShapeDtypeStruct((ranks, slots, features), BF16),
            jax.ShapeDtypeStruct((ranks, slots, features), BF16),
            jax.ShapeDtypeStruct((features, half), F32),
            jax.ShapeDtypeStruct((half, features), F32),
            jax.ShapeDtypeStruct((features, padded), F32),
        ],
        scratch_shapes=[
            pltpu.VMEM((features, hidden_width), BF16),
            pltpu.VMEM((hidden_width, features), BF16),
            pltpu.VMEM((total, features), BF16),
            pltpu.VMEM((total, features), BF16),
            pltpu.VMEM((features, total), BF16),
            pltpu.VMEM((features, total), BF16),
            pltpu.VMEM((total, features), BF16),
            pltpu.VMEM((total, hidden_width), BF16),
            pltpu.VMEM((total, hidden_width), BF16),
            pltpu.VMEM((features, columns), F32),
            pltpu.VMEM((columns, features), F32),
            dma((4,)),
            dma((ranks,)),
            dma((ranks,)),
            dma((ranks,)),
            dma((ranks,)),
            dma((ranks,)),
            dma((ranks,)),
            dma((2, tiles)),
            dma((2, tiles)),
            dma((2, tiles)),
            pltpu.SemaphoreType.REGULAR,
        ],
        compiler_params=pltpu.CompilerParams(
            collective_id=1, has_side_effects=True, vmem_limit_bytes=63 * MIB
        ),
        cost_estimate=pl.CostEstimate(
            flops=12 * total * features * hidden_width,
            bytes_accessed=8 * features * hidden_width + 8 * total * features,
            transcendentals=total * hidden_width,
        ),
    )(hidden, cot, w_in, w_out, router_padded)


def tail_kernel(
    q_ref, k_ref, v_ref, kept_ref, wq_ref, wk_ref, wv_ref, tile_ref, gain_ref, bucket_ref,
    drouter_ref, target_ref, gate_ref, normed_hbm, tokens_hbm, cot_hbm, residual_hbm, attended_hbm,
    out_weight_hbm, moved_hbm, made_hbm,
    tokens_grad_ref, dense_ref, early_ref, router_ref, table_ref, gains_ref, output_hbm, came_hbm,
    normed, narrow, attended, out_weight, slots, datt,
    dscores, dnormed, lines, own, core_out, core_in, plane_out, plane_in, layer_out, layer_in,
    early_out, early_core, early_own, early_plane_out, early_plane_in, early_layer_out,
    early_layer_in, far_out, far_in, kept_sum, early_far_out, early_far_in, early_sum,
    small_out, small_in, load_sem, made_sent, made_came, core_sent, core_came,
    plane_sent, plane_came, layer_sent, layer_came, small_sent, small_came, *, rows, ranks, plane,
):
    length, features = narrow.shape
    tiles = length // LANES
    inner = rows // LANES
    layers = ranks // plane
    groups = (pl.num_programs(0) - 2) // 2
    per_slot = slots.shape[0] // ranks
    step = pl.program_id(0)
    core, me = lax.axis_index("group"), lax.axis_index("expert")
    other = 1 - core
    layer, spot = me // plane, me % plane
    mesh = pl.DeviceIdType.MESH

    def in_plane(k, sign):
        return (spot + plane + sign * k) % plane

    def in_line(k, sign):
        return (layer + layers + sign * k) % layers

    def rank_of(a_layer, a_spot):
        return a_layer * plane + a_spot

    def core_copy(unit):
        early = unit == 0
        return pltpu.make_async_remote_copy(
            src_ref=early_out if early else core_out.at[unit - 1],
            dst_ref=early_core if early else core_in.at[unit - 1],
            send_sem=core_sent.at[unit],
            recv_sem=core_came.at[unit],
            device_id=(other, me),
            device_id_type=mesh,
        )

    def plane_copy(unit, k):
        early = unit == 0
        source = early_plane_out if early else plane_out.at[unit - 1]
        return pltpu.make_async_remote_copy(
            src_ref=source.at[:, in_plane(k, 1)],
            dst_ref=early_plane_in.at[k - 1] if early else plane_in.at[unit - 1, k - 1],
            send_sem=plane_sent.at[unit, k],
            recv_sem=plane_came.at[unit, k],
            device_id=(core, rank_of(layer, in_plane(k, 1))),
            device_id_type=mesh,
        )

    def near_copy(unit):
        early = unit == 0
        source = early_layer_out if early else layer_out.at[unit - 1]
        return pltpu.make_async_remote_copy(
            src_ref=source.at[:, 1 - layer % 2],
            dst_ref=early_layer_in if early else layer_in.at[unit - 1],
            send_sem=layer_sent.at[unit, 0],
            recv_sem=layer_came.at[unit, 0],
            device_id=(core, rank_of(layer // 2 * 2 + 1 - layer % 2, spot)),
            device_id_type=mesh,
        )

    def far_copy(unit):
        early = unit == 0
        return pltpu.make_async_remote_copy(
            src_ref=early_far_out if early else far_out.at[unit - 1],
            dst_ref=early_far_in if early else far_in.at[unit - 1],
            send_sem=layer_sent.at[unit, 1],
            recv_sem=layer_came.at[unit, 1],
            device_id=(core, rank_of((layer + 2) % layers, spot)),
            device_id_type=mesh,
        )

    def small_copy(number):
        if number == 0:
            there = (other, me)
        elif number < plane:
            there = (core, rank_of(layer, in_plane(number, 1)))
        else:
            there = (core, rank_of(in_line(number - plane + 1, 1), spot))
        return pltpu.make_async_remote_copy(
            src_ref=small_out.at[min(number, 1) + number // plane],
            dst_ref=small_in.at[number],
            send_sem=small_sent.at[number],
            recv_sem=small_came.at[number],
            device_id=there,
            device_id_type=mesh,
        )

    def small_start(stage, first, end):
        for number in range(first, end):
            small_copy(number).start()

    def small_add(stage, first, end):
        total = small_out[stage]
        for number in range(first, end):
            small_copy(number).wait_recv()
            total = total + small_in[number]
        return total

    def partner(number):
        return turned(me, number, ranks, plane, 1)

    def made_copy(number):
        return pltpu.make_async_remote_copy(
            src_ref=made_hbm.at[partner(number)],
            dst_ref=came_hbm.at[me],
            send_sem=made_sent.at[number],
            recv_sem=made_came.at[number],
            device_id=(core, partner(number)),
            device_id_type=mesh,
        )

    def load(source, target, number):
        return pltpu.make_async_copy(source, target, load_sem.at[number])

    def moved_load(number):
        part = pl.ds(pl.multiple_of(number * per_slot, per_slot), per_slot)
        return pltpu.make_async_copy(moved_hbm.at[number], slots.at[part], load_sem.at[8])

    def came_load(number):
        part = pl.ds(pl.multiple_of(number * per_slot, per_slot), per_slot)
        return pltpu.make_async_copy(came_hbm.at[number], slots.at[part], load_sem.at[9])

    def own_made():
        return load(made_hbm.at[me], came_hbm.at[me], 7)

    def each(first, last, action):
        def run(number, carry):
            action(number)
            return carry

        lax.fori_loop(first, last, run, 0)

    def taken(block):
        total = jnp.zeros((rows, features), F32)
        width = 4 * LANES
        for first in range(0, slots.shape[0], width):
            at = first + lax.broadcasted_iota(jnp.int32, (1, width), 1)
            picks = (target_ref[block, :] == at).astype(F32).astype(BF16)
            total = total + jnp.dot(
                picks, slots[first : first + width, :], preferred_element_type=F32
            )
        return total

    def sum_cores(unit):
        core_copy(unit).wait_recv()
        if unit == 0:
            summed = early_own[...].astype(F32) + early_core[...].astype(F32)
            early_plane_out[...] = summed.astype(BF16).reshape(early_plane_out.shape)
        else:
            summed = own[unit % 2] + core_in[unit - 1].astype(F32)
            plane_out[unit - 1] = summed.astype(BF16).reshape(plane_out.shape[1:])
        for k in range(1, plane):
            plane_copy(unit, k).start()

    def sum_planes(unit):
        summed = (early_plane_out[:, spot] if unit == 0 else plane_out[unit - 1, :, spot]).astype(F32)
        for k in range(1, plane):
            plane_copy(unit, k).wait_recv()
            came = early_plane_in[k - 1] if unit == 0 else plane_in[unit - 1, k - 1]
            summed = summed + came.astype(F32)
        if unit == 0:
            early_layer_out[...] = summed.astype(BF16).reshape(early_layer_out.shape)
        else:
            layer_out[unit - 1] = summed.astype(BF16).reshape(layer_out.shape[1:])
        near_copy(unit).start()

    def sum_near(unit):
        near_copy(unit).wait_recv()
        here, there = layer // 2, 1 - layer // 2
        if unit == 0:
            early_sum[...] = early_layer_out[here, layer % 2].astype(F32) + early_layer_in[
                here
            ].astype(F32)
            passed = early_layer_out[there, layer % 2].astype(F32) + early_layer_in[there].astype(F32)
            early_far_out[...] = passed.astype(BF16)
        else:
            mine, came = layer_out.at[unit - 1], layer_in.at[unit - 1]
            kept_sum[unit - 1] = mine[here, layer % 2].astype(F32) + came[here].astype(F32)
            passed = mine[there, layer % 2].astype(F32) + came[there].astype(F32)
            far_out[unit - 1] = passed.astype(BF16)
        far_copy(unit).start()

    def sum_layers(unit):
        far_copy(unit).wait_recv()
        if unit == 0:
            summed = early_sum[...] + early_far_in[...].astype(F32)
        else:
            summed = kept_sum[unit - 1] + far_in[unit - 1].astype(F32)
        if unit == 0:
            early_ref[...] = summed[:, : early_ref.shape[1]]
            share = router_ref.shape[0]
            moved_up = pltpu.roll(summed[:, early_ref.shape[1] :], (LANES - core * share) % LANES, 1)
            router_ref[...] = moved_up.T[:share]
        else:
            group = unit - 1
            base = core * (groups * LANES)
            keys_at = other * (2 * groups * LANES) + group * LANES
            for part, at in enumerate(
                (base + group * LANES, base + (groups + group) * LANES, keys_at)
            ):
                dense_ref[:, pl.ds(pl.multiple_of(at, LANES), LANES)] = summed[
                    :, part * LANES : (part + 1) * LANES
                ]

    @pl.when(step == 0)
    def _():
        each(0, ranks, lambda number: moved_load(number).start())
        load(residual_hbm, dnormed, 0).start()
        load(cot_hbm, narrow, 1).start()
        load(out_weight_hbm, out_weight, 2).start()
        load(attended_hbm, attended, 3).start()
        load(normed_hbm, normed, 4).start()
        own_made().start()
        barrier = pltpu.get_barrier_semaphore()
        each(
            1,
            ranks,
            lambda number: pl.semaphore_signal(
                barrier, inc=1, device_id=(core, partner(number)), device_id_type=mesh
            ),
        )
        pl.semaphore_signal(barrier, inc=1, device_id=(other, me), device_id_type=mesh)
        pl.semaphore_wait(barrier, ranks)
        each(1, ranks, lambda number: made_copy(number).start())
        each(0, ranks, lambda number: moved_load(number).wait())
        load(residual_hbm, dnormed, 0).wait()
        load(cot_hbm, narrow, 1).wait()
        load(out_weight_hbm, out_weight, 2).wait()

        def branch(number, dgain):
            block = pl.ds(pl.multiple_of(number * rows, rows), rows)
            back = taken(block)
            residual = dnormed[block, :]
            spread = lax.rsqrt(jnp.mean(residual * residual, axis=1, keepdims=True) + EPSILON)
            scaled = residual * spread
            moved = back * gain_ref[1:2, :]
            dres = narrow[block, :].astype(F32) + spread * (
                moved - scaled * jnp.mean(moved * scaled, axis=1, keepdims=True)
            )
            tokens_grad_ref[block, :] = dres
            dbranch = dres.astype(BF16)
            dscores[block, :features] = dbranch
            datt[block, :] = lax.dot_general(
                dbranch, out_weight[...], NT, preferred_element_type=F32
            ).astype(BF16)
            return dgain + jnp.sum(back * scaled, axis=0, keepdims=True)

        dgain = lax.fori_loop(0, length // rows, branch, jnp.zeros((1, features), F32))
        for part in range(features // LANES):
            at = lines.shape[0] + features // LANES + part
            small_out[0, at : at + 1, :] = dgain[:, part * LANES : (part + 1) * LANES]
        load(attended_hbm, attended, 3).wait()
        load(normed_hbm, normed, 4).wait()
        load(tokens_hbm, narrow, 5).start()
        dense = lax.dot_general(
            attended[...], dscores[:, :features], TN, preferred_element_type=F32
        )
        half = features // 2
        early_own[:, :half] = jnp.where(core == 0, dense[:, :half], dense[:, half:]).astype(BF16)
        early_out[:, :half] = jnp.where(core == 0, dense[:, half:], dense[:, :half]).astype(BF16)
        drouter = drouter_ref[...].astype(BF16)
        early_own[:, half:] = drouter
        early_out[:, half:] = drouter
        core_copy(0).start()
        dnormed[...] = jnp.zeros_like(dnormed)

    @pl.when((step > 0) & (step <= 2 * groups))
    def _():
        lane = lax.broadcasted_iota(jnp.int32, (1, LANES), 1)
        pair = (step - 1) % 2 * groups + (step - 1) // 2
        columns = pl.ds(pl.multiple_of(pair * LANES, LANES), LANES)
        queries, values, dout = q_ref[...], v_ref[...], datt[:, columns]
        widened = jnp.concatenate([k_ref[...], tile_ref[...]], axis=1)
        dout_wide = dout.astype(F32)
        product = dout_wide * attended[:, columns].astype(F32)
        dout_turned, queries_turned = dout.T, queries.T
        mirror = (
            lax.broadcasted_iota(jnp.int32, (LANES, LANES), 0)
            + lax.broadcasted_iota(jnp.int32, (LANES, LANES), 1)
            == LANES - 1
        ).astype(F32)
        dqueries = [[], []]
        dkeys, dvalues = [], []
        for head in range(2):
            mine = (lane < HEAD) if head == 0 else (lane >= HEAD)
            inner_sum = jnp.sum(jnp.where(mine, product, 0.0), axis=1, keepdims=True)
            masked = jnp.where(mine, dout_wide, 0.0).astype(BF16)
            bands = [jnp.zeros((LANES, LANES), F32) for _ in range(3)]
            before = jnp.zeros((1, LANES), F32)
            after = jnp.zeros((1, LANES), F32)
            for part_of in range(length // rows):
                first = part_of * rows
                block = pl.ds(first, rows)
                dprob = lax.dot_general(
                    masked[first : first + rows], values, NT, preferred_element_type=F32
                )
                scores = kept_ref[head, block, :].astype(F32) * (
                    dprob - inner_sum[first : first + rows]
                )
                rounded = scores.astype(BF16)
                dscores[block, :] = rounded
                both = jnp.dot(rounded, widened, preferred_element_type=F32)
                dqueries[head].append(both[:, :LANES])
                for part in range(inner):
                    tile = part_of * inner + part
                    here = slice(part * LANES, (part + 1) * LANES)
                    for at in range(3):
                        there = tile - 1 + at
                        if 0 <= there < tiles:
                            bands[at] = bands[at] + scores[here, there * LANES : (there + 1) * LANES]
                    sums = jnp.sum(both[here, LANES:], axis=0, keepdims=True)
                    before = before + jnp.where(lane <= tile - 2, sums, 0.0)
                    after = after + jnp.where((lane >= tile + 2) & (lane < tiles), sums, 0.0)
            band = jnp.concatenate([*bands, jnp.zeros((LANES, LANES), F32)], axis=1)
            band = jnp.dot(
                mirror, band, preferred_element_type=F32, precision=lax.Precision.HIGHEST
            )
            band = pltpu.roll(band, 3 * LANES + 1, 1, stride=1, stride_axis=0)
            near = jnp.sum(band, axis=0, keepdims=True)
            lines[pl.ds(2 * pair + head, 1), :] = jnp.concatenate([near, before, after], axis=1)
            half = slice(HEAD * head, HEAD * head + HEAD)
            dkeys.append(
                jnp.dot(queries_turned[half], dscores[...], preferred_element_type=F32)
            )
            dvalues.append(jnp.dot(dout_turned[half], kept_ref[head], preferred_element_type=F32))
        scale = HEAD**-0.5
        dq = jnp.concatenate(
            [
                (jnp.where(lane < HEAD, left, right) * scale).astype(BF16)
                for left, right in zip(*dqueries, strict=True)
            ],
            axis=0,
        )
        dk = (jnp.concatenate(dkeys, axis=0) * scale).T.astype(BF16)
        dv = jnp.concatenate(dvalues, axis=0).T.astype(BF16)
        joined = jnp.concatenate([dq, dk, dv], axis=1)
        weights = jnp.concatenate([wq_ref[...], wk_ref[...], wv_ref[...]], axis=1)
        dnormed[...] += lax.dot_general(joined, weights, NT, preferred_element_type=F32)
        dense = jnp.dot(normed[...], joined, preferred_element_type=F32)
        dwq, dwk, dwv = dense[:, :LANES], dense[:, LANES : 2 * LANES], dense[:, 2 * LANES :]
        own_first, away_first = jnp.where(core == 0, dwq, dwv), jnp.where(core == 0, dwv, dwq)
        for now in range(2 * groups):

            @pl.when(step == now + 1)
            def _(now=now):
                unit, part = now // 2 + 1, now % 2
                at = slice(part * LANES, (part + 1) * LANES)
                own[unit % 2, :, at] = own_first
                core_out[unit - 1, :, at] = away_first.astype(BF16)

                @pl.when(core == part)
                def _():
                    own[unit % 2, :, 2 * LANES :] = dwk

                @pl.when(core != part)
                def _():
                    core_out[unit - 1, :, 2 * LANES :] = dwk.astype(BF16)

                if part == 1:
                    core_copy(unit).start()

    last = 2 * groups + 1
    plan = {}
    for unit in range(groups + 1):
        plan.setdefault(min(2 * unit + 1, last), []).append((sum_cores, unit))
        plan.setdefault(min(2 * unit + 4, last), []).append((sum_planes, unit))
        plan.setdefault(min(2 * unit + 6, last), []).append((sum_near, unit))
        plan.setdefault(last, []).append((sum_layers, unit))
    order = [sum_layers, sum_near, sum_planes, sum_cores]
    for now in range(1, last):

        @pl.when(step == now)
        def _(now=now):
            for action, unit in sorted(plan.get(now, []), key=lambda p: order.index(p[0])):
                action(unit)

    @pl.when(step == last)
    def _():
        todo = plan.get(last, [])
        for action, unit in todo:
            if action is sum_cores:
                action(unit)
        for action, unit in todo:
            if action is sum_planes and unit < groups:
                action(unit)
        for action, unit in todo:
            if action is sum_near and unit + 1 < groups:
                action(unit)
        load(tokens_hbm, narrow, 5).wait()
        gain = gain_ref[0:1, :]
        inputs = narrow[...].astype(F32)
        spread = lax.rsqrt(jnp.mean(inputs * inputs, axis=1, keepdims=True) + EPSILON)
        back = dnormed[...]
        scaled = inputs * spread
        dgain = jnp.sum(back * scaled, axis=0, keepdims=True)
        moved = back * gain
        tokens_grad_ref[...] = tokens_grad_ref[...] + spread * (
            moved - scaled * jnp.mean(moved * scaled, axis=1, keepdims=True)
        )
        table = jnp.dot(
            lines[...], bucket_ref[...], preferred_element_type=F32, precision=lax.Precision.HIGHEST
        )
        small_out[0, 0 : lines.shape[0], :] = table
        base = lines.shape[0]
        wide = features // LANES
        for part in range(wide):
            small_out[0, base + part : base + part + 1, :] = dgain[
                :, part * LANES : (part + 1) * LANES
            ]
        if small_out.shape[1] > base + 2 * wide:
            small_out[0, base + 2 * wide :, :] = jnp.zeros(
                (small_out.shape[1] - base - 2 * wide, LANES), F32
            )

        small_start(0, 0, 1)
        load(residual_hbm, dnormed, 6).start()
        for action, unit in todo:
            if action is sum_planes and unit == groups:
                action(unit)
        for action, unit in todo:
            if action is sum_near and unit + 1 == groups:
                action(unit)
        small_out[1] = small_add(0, 0, 1)
        small_start(1, 1, plane)
        own_made().wait()
        each(1, ranks, lambda number: made_copy(number).wait_recv())
        each(0, ranks, lambda number: came_load(number).start())
        each(0, ranks, lambda number: came_load(number).wait())
        load(residual_hbm, dnormed, 6).wait()
        for action, unit in todo:
            if action is sum_near and unit == groups:
                action(unit)

        def finish(number, carry):
            block = pl.ds(pl.multiple_of(number * rows, rows), rows)
            datt[block, :] = (dnormed[block, :] + gate_ref[block, :] * taken(block)).astype(BF16)
            return carry

        lax.fori_loop(0, length // rows, finish, 0)
        load(datt, output_hbm, 10).start()
        small_out[2] = small_add(1, 1, plane)
        small_start(2, plane, plane + layers - 1)
        for action, unit in todo:
            if action is sum_layers:
                action(unit)
        total = small_add(2, plane, plane + layers - 1)
        heads, buckets = table_ref.shape
        table_ref[...] = total[:heads, :buckets]
        row = [
            jnp.where(core == 0, total[at : at + 1], total[at + wide : at + wide + 1])
            for at in range(base, base + wide)
        ]
        row = pltpu.roll(jnp.concatenate(row, axis=1), features - me * gains_ref.shape[1], 1)
        gains_ref[...] = row[:, : gains_ref.shape[1]]
        for number in range(plane + layers - 1):
            small_copy(number).wait_send()
        each(1, ranks, lambda number: made_copy(number).wait_send())
        load(datt, output_hbm, 10).wait()
        for unit in range(groups + 1):
            core_copy(unit).wait_send()
            for k in range(1, plane):
                plane_copy(unit, k).wait_send()
            near_copy(unit).wait_send()
            far_copy(unit).wait_send()


def run_tail(
    projected, attended, kept, qkv_weight, out_weight, normed_turned, tokens, cotangent, residual, gains,
    drouter, target, gate, moved, made, rows, router_share, bucket_count,
):
    length, features = tokens.shape
    heads = kept.shape[0]
    ranks = made.shape[0]
    pairs = heads // 2
    groups = pairs // 2
    plane = 4
    layers = ranks // plane
    slab = features // ranks
    early = features // 2 + LANES
    late = 3 * LANES
    tile_of = (
        jnp.arange(length)[:, None] // LANES == jnp.arange(LANES)[None, :]
    ).astype(BF16)
    at = jnp.arange(4 * LANES, dtype=jnp.int32)
    relative = jnp.where(at < 3 * LANES, at - LANES, at - 5 * LANES)
    ends = bucket_index(jnp.array([-length, length], jnp.int32))
    bucket = jnp.concatenate([bucket_index(relative), jnp.repeat(ends, LANES)])
    bucket_of = (bucket[:, None] == jnp.arange(LANES)[None, :]).astype(F32)
    line_rows = heads + -heads % 4
    small_rows = line_rows + 2 * (features // LANES)
    small_rows += -small_rows % 8

    def pair_of(i):
        i = jnp.clip(i - 1, 0, pairs - 1)
        return i % 2 * groups + i // 2

    def column(shape, offset):
        return pl.BlockSpec(shape, lambda i: (0, offset + pair_of(i)))

    def whole(shape):
        return pl.BlockSpec(shape, lambda i: (0, 0), pipeline_mode=pl.Buffered(1))

    dma = pltpu.SemaphoreType.DMA
    any_ref = pl.BlockSpec(memory_space=pl.ANY)
    units = groups + 1
    return pl.pallas_call(
        functools.partial(tail_kernel, rows=rows, ranks=ranks, plane=plane),
        grid=(pairs + 2,),
        in_specs=[
            column((length, LANES), 0),
            column((length, LANES), pairs),
            column((length, LANES), 2 * pairs),
            pl.BlockSpec((2, length, length), lambda i: (pair_of(i), 0, 0)),
            column((features, LANES), 0),
            column((features, LANES), pairs),
            column((features, LANES), 2 * pairs),
            whole((length, LANES)),
            whole(gains.shape),
            whole(bucket_of.shape),
            whole((features, LANES)),
            whole((length, 1)),
            whole((length, 1)),
            *[any_ref] * 8,
        ],
        out_specs=[
            whole((length, features)),
            whole((slab, groups * late)),
            whole((slab, features // 2)),
            whole((router_share, slab)),
            whole((heads, bucket_count)),
            whole((1, slab)),
            any_ref,
            any_ref,
        ],
        out_shape=[
            jax.ShapeDtypeStruct((length, features), F32),
            jax.ShapeDtypeStruct((slab, groups * late), F32),
            jax.ShapeDtypeStruct((slab, features // 2), F32),
            jax.ShapeDtypeStruct((router_share, slab), F32),
            jax.ShapeDtypeStruct((heads, bucket_count), F32),
            jax.ShapeDtypeStruct((1, slab), F32),
            jax.ShapeDtypeStruct((length, features), BF16),
            jax.ShapeDtypeStruct(made.shape, BF16),
        ],
        scratch_shapes=[
            pltpu.VMEM((features, length), BF16),
            pltpu.VMEM((length, features), BF16),
            pltpu.VMEM((length, features), BF16),
            pltpu.VMEM((features, features), BF16),
            pltpu.VMEM((ranks * made.shape[1], features), BF16),
            pltpu.VMEM((length, features), BF16),
            pltpu.VMEM((length, length), BF16),
            pltpu.VMEM((length, features), F32),
            pltpu.VMEM((line_rows, 6 * LANES), F32),
            pltpu.VMEM((2, features, late), F32),
            pltpu.VMEM((groups, features, late), BF16),
            pltpu.VMEM((groups, features, late), BF16),
            pltpu.VMEM((groups, layers, plane, slab, late), BF16),
            pltpu.VMEM((groups, plane - 1, layers, slab, late), BF16),
            pltpu.VMEM((groups, 2, 2, slab, late), BF16),
            pltpu.VMEM((groups, 2, slab, late), BF16),
            pltpu.VMEM((features, early), BF16),
            pltpu.VMEM((features, early), BF16),
            pltpu.VMEM((features, early), BF16),
            pltpu.VMEM((layers, plane, slab, early), BF16),
            pltpu.VMEM((plane - 1, layers, slab, early), BF16),
            pltpu.VMEM((2, 2, slab, early), BF16),
            pltpu.VMEM((2, slab, early), BF16),
            pltpu.VMEM((groups, slab, late), BF16),
            pltpu.VMEM((groups, slab, late), BF16),
            pltpu.VMEM((groups, slab, late), F32),
            pltpu.VMEM((slab, early), BF16),
            pltpu.VMEM((slab, early), BF16),
            pltpu.VMEM((slab, early), F32),
            pltpu.VMEM((3, small_rows, LANES), F32),
            pltpu.VMEM((plane + layers - 1, small_rows, LANES), F32),
            dma((11,)),
            dma((ranks,)),
            dma((ranks,)),
            dma((units,)),
            dma((units,)),
            dma((units, plane)),
            dma((units, plane)),
            dma((units, 2)),
            dma((units, 2)),
            dma((plane + layers - 1,)),
            dma((plane + layers - 1,)),
        ],
        compiler_params=pltpu.CompilerParams(
            collective_id=2, has_side_effects=True, vmem_limit_bytes=62 * MIB
        ),
        cost_estimate=pl.CostEstimate(
            flops=36 * heads * length * length * HEAD,
            bytes_accessed=2 * heads * length * length + 30 * length * features,
            transcendentals=0,
        ),
    )(
        projected, projected, projected, kept, qkv_weight, qkv_weight, qkv_weight, tile_of, gains,
        bucket_of, drouter, target, gate, normed_turned, tokens, cotangent, residual, attended,
        out_weight, moved, made,
    )


def core_sum(values, dim):
    half = values.shape[dim] // 2
    core = lax.axis_index("group")
    own = lax.dynamic_slice_in_dim(values, core * half, half, dim)
    other = lax.dynamic_slice_in_dim(values, (1 - core) * half, half, dim).astype(BF16)
    return own + lax.ppermute(other, "group", [(0, 1), (1, 0)]).astype(F32)


def exchange(values):
    return lax.all_to_all(values, "expert", split_axis=0, concat_axis=0, tiled=True)


def per_device(
    tokens, gains, qkv_weight, out_weight, rel_bias, router_weight, w_in, w_out, routes, factors,
    cotangent,
):
    length, features = tokens.shape
    bucket_count = rel_bias.shape[0]
    expert_count = router_weight.shape[1]
    slot_count = 2 * length // expert_count
    rows = min(256, length)
    gain_rows = gains.astype(F32)
    w_in, w_out = w_in[0], w_out[0]
    me = lax.axis_index("expert")
    core = lax.axis_index("group")

    routed = routes[:, 0]
    row_index = jnp.arange(length, dtype=jnp.int32)
    chosen = routed[:, None] == jnp.arange(expert_count, dtype=jnp.int32)[None, :]
    earlier = (row_index[:, None] > row_index[None, :]).astype(BF16)
    before = jnp.dot(earlier, chosen.astype(BF16), preferred_element_type=F32)
    place = jnp.sum(before * chosen.astype(F32), axis=-1).astype(jnp.int32)
    capacity = factors[0] * (length // expert_count)
    target = jnp.where(place < capacity, routed * slot_count + place, -1)
    slots = jnp.arange(expert_count * slot_count, dtype=jnp.int32)
    picks = (slots[:, None] == target[None, :]).astype(BF16)

    def pack(values):
        packed = pack_rows(target, values, expert_count * slot_count)
        return packed.reshape(expert_count, slot_count, features)

    def unpack(values):
        return lax.dot_general(
            picks, values.reshape(-1, features), TN, preferred_element_type=F32
        )

    upstream_there = exchange(pack(cotangent))

    inputs = tokens.astype(F32)
    normed_in = norm_rows(inputs, gain_rows[0]).astype(BF16)
    projected = jnp.dot(normed_in, qkv_weight, preferred_element_type=F32).astype(BF16)
    attended, kept = attend(projected, bias_lines(rel_bias, length), rows)
    residual_one = inputs + jnp.dot(attended, out_weight, preferred_element_type=F32)
    hidden = norm_rows(residual_one, gain_rows[1]).astype(BF16)

    logits = jnp.dot(hidden, router_weight, preferred_element_type=F32)
    raised = jnp.exp(logits - jnp.max(logits, axis=-1, keepdims=True))
    router = raised / jnp.sum(raised, axis=-1, keepdims=True)
    gate_value = jnp.sum(router * chosen.astype(F32), axis=-1)

    padded = -expert_count % LANES
    router_padded = jnp.pad(router_weight, ((0, 0), (0, padded)))
    packed, normed_turned = lax.optimization_barrier((pack(hidden), normed_in.T))
    made, dmoved_back, grad_first, grad_second, drouter = run_expert(
        packed, upstream_there, w_in, w_out, router_padded, expert_count
    )
    experts = lax.axis_size("expert")
    cores = lax.axis_size("group")
    slab = features // experts
    gain_at = (core, me * slab)
    router_at = (core * (expert_count // cores),)
    if experts == 16 and cores == 2 and features % (16 * experts) == 0:
        grad_tokens, grad_qkv, grad_out, grad_router, grad_table, grad_gains, output, _ = run_tail(
            projected, attended, kept, qkv_weight, out_weight, normed_turned, tokens, cotangent,
            residual_one, gain_rows, drouter, target[:, None], gate_value[:, None], dmoved_back, made,
            rows, expert_count // cores, bucket_count,
        )
        return (
            output,
            grad_tokens,
            grad_gains,
            grad_qkv,
            grad_out,
            grad_table.T,
            grad_router.T,
            grad_first[None],
            grad_second[None],
        )

    made_back = exchange(made)
    grad_router = drouter[:, :expert_count]

    dhidden = unpack(dmoved_back)
    upstream = cotangent.astype(F32)
    _, back_two = jax.vjp(norm_rows, residual_one, gain_rows[1])
    dres_norm, dgain_two = back_two(dhidden)
    dres = upstream + dres_norm
    dbranch = dres.astype(BF16)
    datt = lax.dot_general(dbranch, out_weight, NT, preferred_element_type=F32).astype(BF16)
    grad_out = lax.dot_general(attended, dbranch, TN, preferred_element_type=F32)
    dqkv, band, far = attend_back(projected, attended, datt, kept, rows)
    grad_proj = jnp.einsum("td,cte->dce", normed_in, dqkv, preferred_element_type=F32)
    grad_proj = grad_proj.reshape(features, 3 * features)
    dnormed = jnp.einsum(
        "cte,dce->td",
        dqkv,
        qkv_weight.reshape(features, 3, features),
        preferred_element_type=F32,
    )
    _, back_one = jax.vjp(norm_rows, inputs, gain_rows[0])
    dinput_norm, dgain_one = back_one(dnormed)
    grad_tokens = dres + dinput_norm

    brought = unpack(made_back)
    output = (residual_one + gate_value[:, None] * brought).astype(BF16)

    def scattered(values):
        return lax.psum_scatter(
            core_sum(values, 1).astype(BF16), "expert", scatter_dimension=0, tiled=True
        ).astype(F32)

    small = [
        jnp.stack([dgain_one, dgain_two], axis=0),
        grad_router,
        table_gradient(band, far, bucket_count),
    ]
    flat = lax.psum(jnp.concatenate([s.reshape(-1) for s in small]), ("group", "expert"))
    summed = []
    at = 0
    for s in small:
        summed.append(flat[at : at + s.size].reshape(s.shape))
        at += s.size
    grad_gains = lax.dynamic_slice(summed[0], gain_at, (2 // cores, slab))
    grad_router = lax.dynamic_slice(
        summed[1], (me * slab, *router_at), (slab, expert_count // cores)
    )
    return (
        output,
        grad_tokens,
        grad_gains,
        scattered(grad_proj),
        scattered(grad_out),
        summed[2],
        grad_router,
        grad_first[None],
        grad_second[None],
    )


def solution(mesh):
    return jax.shard_map(
        per_device,
        mesh=mesh,
        in_specs=(
            P(("group", "expert"), None),
            P(),
            P(),
            P(),
            P(),
            P(),
            P("expert", None, None),
            P("expert", None, None),
            P(("group", "expert"), None),
            P(("group", "expert")),
            P(("group", "expert"), None),
        ),
        out_specs=(
            P(("group", "expert"), None),
            P(("group", "expert"), None),
            P("group", "expert"),
            P("expert", "group"),
            P("expert", "group"),
            P(),
            P("expert", "group"),
            P("expert", None, "group"),
            P("expert", "group", None),
        ),
        check_vma=False,
    )
```
